128 devices in a mesh: row: 16 (over z_lo, x, core), col: 8 (over y, z_hi).
Axes of the slice: x: 4, y: 4, z: 4 (z_hi: 2, z_lo: 2; z = z_hi * 2 + z_lo), core: 2. Of those that a mesh axis runs over, the one named last changes fastest.
Arguments:
- front: float32 [12288, 12288], P('row', 'col'), as said below
- children: float32 [16384, 8192], P('row', 'col'), as said below
- maps: int32 [2, 64], replicated, may hold values from 0 to 95, as said below
Outputs:
- factored: float32 [12288, 12288], P('row', 'col')
The draws below stay inside these ranges and needn't reach their ends.
Inputs may be any that keep to these rules, and one draw needn't show every extreme that they name: `maps`: each row increases, starts at 0 and ends at 95; each aligned run of 8 entries holds consecutive integers. Symmetric in matrix order; the assembled front is positive definite. `children`: each child's update is symmetric.
All inputs are finite; a program needn't handle non-finite values.
Results may differ from the reference program's by a relative error of at most 0.0003.
Values sent between devices are 32-bit elements; how exact they have to be, the bound alone decides.
A program may use at most 128 MiB of HBM per device.

```python
import jax
import jax.numpy as jnp
from jax import lax

ORDER = 12288
CHILD = 8192
BLOCK = 128
PANEL = 768
PANELS = 2
NBLK = 96
CBLK = 64
GROUP = 8
LROW = 6
LCOL = 12
N_ROW = 16
N_COL = 8


def grid_order(matrix):
    by_rows = matrix.reshape(LROW, N_ROW, BLOCK, ORDER).transpose(1, 0, 2, 3).reshape(ORDER, ORDER)
    return by_rows.reshape(ORDER, LCOL, N_COL, BLOCK).transpose(0, 2, 1, 3).reshape(ORDER, ORDER)


def gram_rows(key, rows, inner, spread):
    gauss_key = jax.random.fold_in(key, 0)
    scale_key = jax.random.fold_in(key, 3)
    gauss = jax.random.normal(gauss_key, (rows, inner), jnp.float32)
    scales = jnp.exp(jax.random.uniform(scale_key, (rows,), jnp.float32, -spread, spread))
    factor = gauss * scales[:, None]
    product = jnp.dot(factor, factor.T, precision=lax.Precision.HIGHEST) / inner
    return 0.5 * (product + product.T)


def draw_front(key, part):
    key = jax.random.fold_in(key, 11)
    matrix = gram_rows(key, ORDER, ORDER // 4, 0.5)
    matrix = matrix + 0.5 * jnp.eye(ORDER, dtype=jnp.float32)
    return grid_order(matrix)


def draw_children(key, part):
    key = jax.random.fold_in(key, 12)
    result = []
    for member in range(2):
        member_key = jax.random.fold_in(key, member)
        result.append(gram_rows(member_key, CHILD, CHILD // 4, 0.5))
    return jnp.concatenate(result, 0)


def draw_maps(key, part):
    key = jax.random.fold_in(key, 13)
    runs_count = CBLK // GROUP
    pool = NBLK - CBLK + runs_count
    result = []
    for member in range(2):
        member_key = jax.random.fold_in(key, member)
        shuffled = jax.random.permutation(member_key, pool - 2) + 1
        middle = jnp.sort(shuffled[:runs_count - 2])
        marks = jnp.concatenate([jnp.zeros((1,), jnp.int32), middle.astype(jnp.int32), jnp.full((1,), pool - 1, jnp.int32)])
        starts = marks + jnp.arange(runs_count, dtype=jnp.int32) * (GROUP - 1)
        result.append((starts[:, None] + jnp.arange(GROUP, dtype=jnp.int32)[None, :]).reshape(-1))
    return jnp.stack(result).astype(jnp.int32)


def setup_inputs(seed: int = 0) -> dict:
    keys = jax.random.split(jax.random.key(seed), 4)
    front = draw_front(jax.random.fold_in(keys[3], 71), 0)
    children = draw_children(jax.random.fold_in(keys[3], 71), 0)
    maps = draw_maps(jax.random.fold_in(keys[3], 71), 0)
    return dict(front=front, children=children, maps=maps)


def to_matrix(stored):
    by_rows = stored.reshape(N_ROW, LROW, BLOCK, ORDER).transpose(1, 0, 2, 3).reshape(ORDER, ORDER)
    return by_rows.reshape(ORDER, N_COL, LCOL, BLOCK).transpose(0, 2, 1, 3).reshape(ORDER, ORDER)

def to_stored(matrix):
    by_rows = matrix.reshape(LROW, N_ROW, BLOCK, ORDER).transpose(1, 0, 2, 3).reshape(ORDER, ORDER)
    return by_rows.reshape(ORDER, LCOL, N_COL, BLOCK).transpose(0, 2, 1, 3).reshape(ORDER, ORDER)

def reference(front, children, maps):
    assembled = to_matrix(front)
    offsets = jnp.arange(BLOCK, dtype=jnp.int32)
    for member in range(2):
        update = children[member * CHILD:(member + 1) * CHILD]
        indices = (maps[member][:, None] * BLOCK + offsets[None, :]).reshape(-1).astype(jnp.int32)
        assembled = assembled.at[indices[:, None], indices[None, :]].add(update)
    row_index = jnp.arange(ORDER)
    steps_in = jnp.arange(PANEL)
    factors = []
    for panel_index in range(PANELS):
        start_col = panel_index * PANEL
        panel_cols = assembled[:, start_col:start_col + PANEL]
        for earlier in factors:
            panel_cols = panel_cols - jnp.dot(earlier, earlier[start_col:start_col + PANEL].T, precision=lax.Precision.HIGHEST)
        factor = jnp.linalg.cholesky(panel_cols[start_col:start_col + PANEL])
        solved = jax.scipy.linalg.solve_triangular(factor, panel_cols.T, lower=True).T
        keep_mask = row_index[:, None] >= start_col + steps_in[None, :]
        assembled = assembled.at[:, start_col:start_col + PANEL].set(jnp.where(keep_mask, solved, 0.0))
        factors.append(jnp.where(row_index[:, None] >= start_col + PANEL, solved, 0.0))
    boundary = PANELS * PANEL
    remaining = ORDER - boundary
    stacked = jnp.concatenate(factors, 1)[boundary:]
    strips = []
    for offset in range(0, remaining, PANEL):
        product = jnp.dot(stacked[offset:offset + PANEL], stacked[:offset + PANEL].T, precision=lax.Precision.HIGHEST)
        strips.append(jnp.pad(product, ((0, 0), (0, remaining - offset - PANEL))))
    lower_half = jnp.concatenate(strips, 0)
    tiles = jnp.arange(remaining) // PANEL
    symmetric = jnp.where(tiles[:, None] >= tiles[None, :], lower_half, lower_half.T)
    complement = assembled[boundary:, boundary:] - symmetric
    assembled = assembled.at[boundary:, boundary:].set(complement)
    assembled = assembled.at[:boundary, boundary:].set(0.0)
    return to_stored(assembled)
```

```python
import jax
import jax.numpy as jnp
from jax import lax
from jax.experimental import pallas as pl
from jax.experimental.pallas import tpu as pltpu
from jax.sharding import PartitionSpec as P

HIGHEST = lax.Precision.HIGHEST
MESH = pl.DeviceIdType.MESH
F32 = jnp.float32
BF16 = jnp.bfloat16
NN = (((1,), (0,)), ((), ()))
NT = (((1,), (1,)), ((), ()))
VMEM = pl.BlockSpec(memory_space=pltpu.VMEM)
SMEM = pl.BlockSpec(memory_space=pltpu.SMEM)
VMEM_LIMIT = 60 * 2**20


def run_of(maps_ref, member, block):
    run = jnp.int32(0)
    found = jnp.int32(0)
    for j in range(8):
        start = maps_ref[member, 8 * j]
        hit = ((block >= start) & (block < start + 8)).astype(jnp.int32)
        run = jnp.maximum(run, hit * j)
        found = jnp.maximum(found, hit)
    return run, found


def extend_kernel(maps_ref, child_ref, front_ref, out_ref, blocks, packed, arrived, send_sem, recv_sem):
    row, col = lax.axis_index("row"), lax.axis_index("col")
    me = row * 8 + col

    def peer(o):
        return lax.rem(row + o // 8, 16), lax.rem(col + lax.rem(o, 8), 8)

    barrier = pltpu.get_barrier_semaphore()

    @pl.loop(1, 128)
    def _(o):
        pl.semaphore_signal(barrier, inc=1, device_id=peer(o), device_id_type=MESH)

    for g in range(8):
        for h in range(8):
            blocks[g * 8 + h] = child_ref[128 * g : 128 * g + 128, 128 * h : 128 * h + 128]
    member = row // 8
    row_start = maps_ref[member, 8 * lax.rem(row, 8)]
    col_start = maps_ref[member, 8 * col]

    @pl.loop(0, 64)
    def _(p):
        g = lax.rem(p // 8 - lax.rem(row_start, 8) + 8, 8)
        h = lax.rem(lax.rem(p, 8) - lax.rem(col_start, 8) + 8, 8)
        packed[p] = blocks[g * 8 + h]

    arrived[me] = packed[lax.rem(row, 8) * 8 + col]
    pl.semaphore_wait(barrier, 127)

    @pl.loop(1, 128)
    def _(o):
        to_row, to_col = peer(o)
        pltpu.make_async_remote_copy(
            src_ref=packed.at[lax.rem(to_row, 8) * 8 + to_col],
            dst_ref=arrived.at[me],
            send_sem=send_sem,
            recv_sem=recv_sem,
            device_id=(to_row, to_col),
            device_id_type=MESH,
        ).start()

    everything = pltpu.make_async_remote_copy(
        src_ref=arrived.at[pl.ds(0, 127)],
        dst_ref=arrived.at[pl.ds(0, 127)],
        send_sem=send_sem,
        recv_sem=recv_sem,
        device_id=peer(1),
        device_id_type=MESH,
    )
    everything.wait_recv()

    @pl.loop(0, 6)
    def _(l):
        runs = [run_of(maps_ref, k, l * 16 + row) for k in range(2)]
        rows = pl.ds(pl.multiple_of(l * 128, 128), 128)

        @pl.loop(0, 12)
        def _(m):
            cols = pl.ds(pl.multiple_of(m * 128, 128), 128)
            total = front_ref[rows, cols]
            for k in range(2):
                run, found = runs[k]
                other, also = run_of(maps_ref, k, m * 8 + col)
                update = arrived[(k * 8 + run) * 8 + other]
                total = total + update * (found * also).astype(F32)
            out_ref[rows, cols] = total

    everything.wait_send()


def extend(maps, children, front):
    return pl.pallas_call(
        extend_kernel,
        out_shape=jax.ShapeDtypeStruct(front.shape, F32),
        in_specs=[SMEM, VMEM, VMEM],
        out_specs=VMEM,
        scratch_shapes=[
            pltpu.VMEM((64, 128, 128), F32),
            pltpu.VMEM((64, 128, 128), F32),
            pltpu.VMEM((128, 128, 128), F32),
            pltpu.SemaphoreType.DMA,
            pltpu.SemaphoreType.DMA,
        ],
        compiler_params=pltpu.CompilerParams(
            collective_id=0, has_side_effects=True, vmem_limit_bytes=VMEM_LIMIT
        ),
        name="extend_add",
    )(maps, children, front)


class Mover:
    def __init__(self, send_sem):
        self.send_sem = send_sem
        self.sent = []

    def send(self, guard, src, dst, recv_sem, target):
        copy = pltpu.make_async_remote_copy(
            src_ref=src,
            dst_ref=dst,
            send_sem=self.send_sem.at[len(self.sent)],
            recv_sem=recv_sem,
            device_id=target,
            device_id_type=MESH,
        )
        self.sent.append((guard, copy))

        @pl.when(guard)
        def _():
            copy.start()

    def finish(self):
        for guard, copy in self.sent:

            @pl.when(guard)
            def _():
                copy.wait_send()


def await_copy(guard, dst, recv_sem, peer):
    @pl.when(guard)
    def _():
        pltpu.make_async_remote_copy(
            src_ref=dst,
            dst_ref=dst,
            send_sem=recv_sem,
            recv_sem=recv_sem,
            device_id=peer,
            device_id_type=MESH,
        ).wait_recv()


class RowGather:
    def __init__(self, mover, view, half, sem, needed, places):
        self.mover, self.view, self.half, self.sem, self.needed = mover, view, half, sem, needed
        (self.h, self.x, self.k), (self.z_peer, self.right, self.left, self.mate) = places

    def slot(self, h, x):
        return h * 8 + x * 2 + self.k

    def near(self, step):
        x = lax.rem(self.x + step + 4, 4)
        return [self.slot(self.h, x), self.slot(1 - self.h, x)]

    def whole(self, slot, target):
        v = self.view(slot)
        self.mover.send(self.needed(slot), v, v, self.sem.at[0, slot], target)

    def part(self, slot, i, target):
        v = self.half(slot, i)
        self.mover.send(self.needed(slot), v, v, self.sem.at[i, slot], target)

    def got(self, slot, peer):
        await_copy(self.needed(slot), self.view(slot), self.sem.at[0, slot], peer)

    def got_part(self, slot, i, peer):
        await_copy(self.needed(slot), self.half(slot, i), self.sem.at[i, slot], peer)

    def to_pair(self):
        own = self.slot(self.h, self.x)
        self.whole(own, self.z_peer)
        self.whole(own, self.right)
        self.whole(own, self.left)
        self.whole(own, self.mate)

    def to_ring(self):
        other = self.slot(1 - self.h, self.x)
        self.got(other, self.z_peer)
        self.whole(other, self.right)
        self.whole(other, self.left)
        self.whole(other, self.mate)

    def forward(self):
        for slot in self.near(-1):
            self.got(slot, self.left)
            self.part(slot, 0, self.right)
        for slot in self.near(1):
            self.got(slot, self.right)
            self.part(slot, 1, self.left)
        for slot in self.near(-1) + self.near(1):
            self.whole(slot, self.mate)

    def to_mate(self):
        for slot in self.near(2):
            self.got_part(slot, 0, self.left)
            self.got_part(slot, 1, self.right)
            self.whole(slot, self.mate)

    def finish(self):
        for h in range(2):
            for x in range(4):
                slot = h * 8 + x * 2 + 1 - self.k
                self.got(slot, self.mate)


class ColGather:
    def __init__(self, mover, view, half, sem, places):
        self.mover, self.view, self.half, self.sem = mover, view, half, sem
        (self.y, self.s), (self.z_peer, self.right, self.left) = places

    def slots(self, y, s):
        return [y * 2 + s, y * 2 + s + 8]

    def both(self, step):
        y = lax.rem(self.y + step + 4, 4)
        return self.slots(y, 0) + self.slots(y, 1)

    def whole(self, slot, target):
        v = self.view(slot)
        self.mover.send(slot < 12, v, v, self.sem.at[0, slot], target)

    def part(self, slot, i, target):
        v = self.half(slot, i)
        self.mover.send(slot < 12, v, v, self.sem.at[i, slot], target)

    def got(self, slot, peer):
        await_copy(slot < 12, self.view(slot), self.sem.at[0, slot], peer)

    def got_part(self, slot, i, peer):
        await_copy(slot < 12, self.half(slot, i), self.sem.at[i, slot], peer)

    def to_pair(self):
        for slot in self.slots(self.y, self.s):
            self.whole(slot, self.z_peer)
            self.whole(slot, self.right)
            self.whole(slot, self.left)

    def to_ring(self):
        for slot in self.slots(self.y, 1 - self.s):
            self.got(slot, self.z_peer)
            self.whole(slot, self.right)
            self.whole(slot, self.left)

    def forward(self):
        for slot in self.both(-1):
            self.got(slot, self.left)
            self.part(slot, 0, self.right)
        for slot in self.both(1):
            self.got(slot, self.right)
            self.part(slot, 1, self.left)

    def finish(self):
        for slot in self.both(2):
            self.got_part(slot, 0, self.left)
            self.got_part(slot, 1, self.right)


def gather_kernel(
    a_ref, g1, g2, pv, send_sem, g1_sem, g2_sem, pv_sem
):
    row, col = lax.axis_index("row"), lax.axis_index("col")
    h, x, k = row // 8, lax.rem(row, 8) // 2, lax.rem(row, 2)
    y, s = col // 2, lax.rem(col, 2)
    at_x = lambda p: h * 8 + lax.rem(p + 4, 4) * 2 + k
    at_y = lambda p: lax.rem(p + 4, 4) * 2 + s
    row_peers = [
        ((1 - h) * 8 + x * 2 + k, col),
        (at_x(x + 1), col),
        (at_x(x - 1), col),
        (h * 8 + x * 2 + 1 - k, col),
    ]
    col_peers = [(row, y * 2 + 1 - s), (row, at_y(y + 1)), (row, at_y(y - 1))]
    barrier = pltpu.get_barrier_semaphore()
    for p in row_peers + col_peers:
        pl.semaphore_signal(barrier, inc=1, device_id=p, device_id_type=MESH)

    g2[col] = a_ref[:, 0:128].T

    @pl.when(col < 4)
    def _():
        g2[col + 8] = a_ref[:, 128:256].T

    @pl.when(row < 12)
    def _():
        g1[row] = a_ref[0:128, :]

    pl.semaphore_wait(barrier, 7)

    mover = Mover(send_sem)
    row_places = ((h, x, k), row_peers)
    wide = pl.ds(128, 1408)
    rows1 = RowGather(
        mover,
        lambda q: g1.at[q, :, wide],
        lambda q, i: g1.at[q, pl.ds(64 * i, 64), wide],
        g1_sem,
        lambda q: q < 12,
        row_places,
    )
    cols2 = ColGather(
        mover,
        lambda e: g2.at[e],
        lambda e, i: g2.at[e, pl.ds(64 * i, 64), :],
        g2_sem,
        ((y, s), col_peers),
    )

    def block_col(q):
        return pl.ds(pl.multiple_of(q * 128, 128), 128)

    pivots = [
        RowGather(
            mover,
            lambda q, t=t: pv.at[pl.ds(512 * t, 512), block_col(q)],
            lambda q, i, t=t: pv.at[pl.ds(512 * t + 256 * i, 256), block_col(q)],
            pv_sem.at[t],
            lambda q, t=t: q < 4 * (t + 1),
            row_places,
        )
        for t in range(3)
    ]
    cols2.to_pair()
    cols2.to_ring()
    rows1.to_pair()
    cols2.forward()
    rows1.to_ring()
    cols2.finish()

    @pl.when(row < 12)
    def _():
        @pl.loop(0, 12)
        def _(e):
            pv[pl.ds(pl.multiple_of(e * 128, 128), 128), block_col(row)] = g2[e, :, 0:128]

    for p in pivots:
        p.to_pair()
    for p in pivots:
        p.to_ring()
    rows1.forward()
    for p in pivots:
        p.forward()
    rows1.to_mate()
    for p in pivots:
        p.to_mate()
    for p in pivots:
        p.finish()
    rows1.finish()
    mover.finish()


def gather(a):
    return pl.pallas_call(
        gather_kernel,
        out_shape=(
            jax.ShapeDtypeStruct((12, 128, 1536), F32),
            jax.ShapeDtypeStruct((12, 128, 768), F32),
            jax.ShapeDtypeStruct((1536, 1536), F32),
        ),
        in_specs=[VMEM],
        out_specs=[VMEM] * 3,
        scratch_shapes=[
            pltpu.SemaphoreType.DMA((128,)),
            pltpu.SemaphoreType.DMA((2, 16)),
            pltpu.SemaphoreType.DMA((2, 16)),
            pltpu.SemaphoreType.DMA((3, 2, 16)),
        ],
        compiler_params=pltpu.CompilerParams(
            collective_id=1, has_side_effects=True, vmem_limit_bytes=VMEM_LIMIT
        ),
        name="gather_panel",
    )(a)


def factor128(a):
    rows = lax.broadcasted_iota(jnp.int32, (8, 128), 0)
    lanes = lax.broadcasted_iota(jnp.int32, (8, 128), 1)
    strips = [a[8 * g : 8 * g + 8, :] for g in range(16)]
    units = [jnp.where(lanes == rows + 8 * g, 1.0, 0.0).astype(jnp.float32) for g in range(16)]
    uppers, inverses = [], []
    full = (8, 128)
    for g in range(16):
        s, t = strips[g], units[g]
        cols = [jnp.broadcast_to(s[:, 8 * g + m : 8 * g + m + 1], full) for m in range(8)]
        e = [[jnp.broadcast_to(cols[m][i : i + 1, :], full) if i >= m else None for m in range(8)] for i in range(8)]
        z = [jnp.broadcast_to(s[i : i + 1, :], full) for i in range(8)]
        y = [jnp.broadcast_to(t[i : i + 1, :], full) for i in range(8)]
        l = [[None] * 8 for _ in range(8)]
        r = []
        for k in range(8):
            d = e[k][k]
            r0 = pl.reciprocal(d, approx=True)
            rk = r0 * (2.0 - d * r0)
            r.append(rk)
            for i in range(k + 1, 8):
                l[i][k] = e[i][k] * rk
            for j in range(k + 1, 8):
                for i in range(j, 8):
                    e[i][j] = e[i][j] - l[i][k] * e[j][k]
            for i in range(k + 1, 8):
                z[i] = z[i] - l[i][k] * z[k]
                y[i] = y[i] - l[i][k] * y[k]
        u = jnp.zeros(full, jnp.float32)
        w = jnp.zeros(full, jnp.float32)
        for i in range(8):
            d = e[i][i]
            q = lax.rsqrt(d)
            q = q * (1.5 - 0.5 * d * q * q)
            u = jnp.where(rows == i, z[i] * q, u)
            w = jnp.where(rows == i, y[i] * q, w)
        uppers.append(jnp.where(lanes >= rows + 8 * g, u, 0.0))
        inverses.append(w)
        if g == 15:
            break
        v = [None] * 8
        x = [None] * 8
        for i in reversed(range(8)):
            vi, xi = z[i] * r[i], y[i] * r[i]
            for m in range(i + 1, 8):
                vi = vi - l[m][i] * v[m]
                xi = xi - l[m][i] * x[m]
            v[i], x[i] = vi, xi
        for h in range(g + 1, 16):
            sh = strips[h]
            acc = [sh[:, 8 * g + m : 8 * g + m + 1] for m in range(8)]
            acc = [jnp.broadcast_to(c, full) for c in acc]
            p = [acc[m] * v[m] for m in range(8)]
            o = [acc[m] * x[m] for m in range(8)]
            while len(p) > 1:
                p = [p[2 * i] + p[2 * i + 1] for i in range(len(p) // 2)]
                o = [o[2 * i] + o[2 * i + 1] for i in range(len(o) // 2)]
            strips[h] = sh - p[0]
            units[h] = units[h] - o[0]
    return jnp.concatenate(uppers, 0), jnp.concatenate(inverses, 0)


def dot(a, b, dims=NN):
    return lax.dot_general(a, b, dims, precision=HIGHEST, preferred_element_type=jnp.float32)


def chol_loop(pv, dinv, nsteps=6):
    @pl.loop(0, nsteps)
    def _(J):
        ca = pl.multiple_of(J * 256, 256)
        cb = pl.multiple_of(J * 256 + 128, 128)
        ua, ia = factor128(pv[pl.ds(ca, 128), pl.ds(ca, 128)])
        la = ua.T
        pv[pl.ds(ca, 128), pl.ds(ca, 128)] = la
        wb = dot(pv[pl.ds(cb, 128), pl.ds(ca, 128)], ia, NT)
        pv[pl.ds(cb, 128), pl.ds(ca, 128)] = wb
        ub, ib = factor128(pv[pl.ds(cb, 128), pl.ds(cb, 128)] - dot(wb, wb, NT))
        pv[pl.ds(cb, 128), pl.ds(cb, 128)] = ub.T
        off = -dot(ib, dot(wb, ia))
        dinv[J, 0:128, 0:128] = ia
        dinv[J, 0:128, 128:256] = jnp.zeros((128, 128), jnp.float32)
        dinv[J, 128:256, 0:128] = off
        dinv[J, 128:256, 128:256] = ib
        inv = dinv[J]
        @pl.loop(J + 1, nsteps)
        def _(R):
            ro = pl.multiple_of(R * 256, 256)
            pv[pl.ds(ro, 256), pl.ds(ca, 256)] = dot(pv[pl.ds(ro, 256), pl.ds(ca, 256)], inv, NT)
        @pl.loop(J + 1, nsteps)
        def _(I):
            io = pl.multiple_of(I * 256, 256)
            wi = pv[pl.ds(io, 256), pl.ds(ca, 256)]
            @pl.loop(I, nsteps)
            def _(R):
                ro = pl.multiple_of(R * 256, 256)
                pv[pl.ds(ro, 256), pl.ds(io, 256)] -= dot(pv[pl.ds(ro, 256), pl.ds(ca, 256)], wi, NT)


def factor_kernel(p_ref, l_ref, d_ref):
    l_ref[...] = p_ref[...]
    chol_loop(l_ref, d_ref)


def factor(pv):
    return pl.pallas_call(
        factor_kernel,
        out_shape=(
            jax.ShapeDtypeStruct((1536, 1536), F32),
            jax.ShapeDtypeStruct((6, 256, 256), F32),
        ),
        in_specs=[VMEM],
        out_specs=[VMEM] * 2,
        compiler_params=pltpu.CompilerParams(vmem_limit_bytes=VMEM_LIMIT),
        name="factor",
    )(pv)


def split(v):
    hi = v.astype(BF16)
    return hi, (v - hi.astype(F32)).astype(BF16)


def dot3(ah, al, bh, bl):
    a = jnp.concatenate([ah, ah, al], 1)
    b = jnp.concatenate([bh, bl, bh], 0)
    return lax.dot_general(a, b, NN, preferred_element_type=F32)


def finish_kernel(a_ref, g1, g2, l_ref, d_ref, out_ref, xh, xl, yh, yl):
    row, col = lax.axis_index("row"), lax.axis_index("col")
    for i in range(6):
        dh, dl = split(d_ref[i])
        lh, ll = split(l_ref[256 * i : 256 * i + 256, : 256 * i]) if i else (None, None)

        def solve(rhs, cols):
            if i:
                rhs = rhs - dot3(lh, ll, xh[: 256 * i, cols], xl[: 256 * i, cols])
            hi, lo = split(dot3(dh, dl, *split(rhs)))
            xh[256 * i : 256 * i + 256, cols] = hi
            xl[256 * i : 256 * i + 256, cols] = lo

        @pl.loop(0, 2)
        def _(n):
            cols = pl.ds(pl.multiple_of(n * 768, 256), 768)
            solve(g1[2 * i : 2 * i + 2, :, cols].reshape(256, 768), cols)

        solve(g2[2 * i : 2 * i + 2].reshape(256, 768), pl.ds(1536, 768))
    for l in range(6):
        lanes = slice(1536 + 128 * l, 1664 + 128 * l)
        yh[128 * l : 128 * l + 128, :] = xh[:, lanes].T
        yl[128 * l : 128 * l + 128, :] = xl[:, lanes].T

    @pl.loop(0, 6)
    def _(t):
        rows = pl.ds(pl.multiple_of(t // 2 * 256, 256), 256)
        cols = pl.ds(pl.multiple_of(lax.rem(t, 2) * 768, 256), 768)
        out_ref[rows, cols] = a_ref[rows, cols] - dot3(
            yh[rows, :], yl[rows, :], xh[:, cols], xl[:, cols]
        )

    @pl.when(row < 12)
    def _():
        out_ref[0:128, :] = jnp.zeros((128, 1536), F32)

    def panel(block, m):
        lanes = pl.ds(pl.multiple_of(block * 128, 128), 128)
        values = yh[:, lanes].astype(F32) + yl[:, lanes].astype(F32)
        i = lax.broadcasted_iota(jnp.int32, values.shape, 0)
        j = lax.broadcasted_iota(jnp.int32, values.shape, 1)
        matrix_row = (i // 128 * 16 + row) * 128 + lax.rem(i, 128)
        out_ref[:, 128 * m : 128 * m + 128] = jnp.where(
            matrix_row >= block * 128 + j, values, 0.0
        )

    panel(col, 0)

    @pl.when(col < 4)
    def _():
        panel(col + 8, 1)


def finish(a, g1, g2, lower, inverses):
    return pl.pallas_call(
        finish_kernel,
        out_shape=jax.ShapeDtypeStruct(a.shape, F32),
        in_specs=[VMEM] * 5,
        out_specs=VMEM,
        scratch_shapes=[
            pltpu.VMEM((1536, 2304), BF16),
            pltpu.VMEM((1536, 2304), BF16),
            pltpu.VMEM((768, 1536), BF16),
            pltpu.VMEM((768, 1536), BF16),
        ],
        compiler_params=pltpu.CompilerParams(vmem_limit_bytes=VMEM_LIMIT),
        name="finish",
    )(a, g1, g2, lower, inverses)


def shards(front, children, maps):
    matrix = extend(maps, children, front)
    g1, g2, pv = gather(matrix)
    lower, inverses = factor(pv)
    return finish(matrix, g1, g2, lower, inverses)


def solution(mesh):
    in_specs = (P("row", "col"), P("row", "col"), P())
    out_specs = P("row", "col")
    return jax.shard_map(shards, mesh=mesh, in_specs=in_specs, out_specs=out_specs, check_vma=False)
```

```python
import jax
import jax.numpy as jnp
from jax import lax
from jax.experimental import pallas as pl
from jax.experimental.pallas import tpu as pltpu
from jax.sharding import PartitionSpec as P

HIGHEST = lax.Precision.HIGHEST
MESH = pl.DeviceIdType.MESH
F32 = jnp.float32
BF16 = jnp.bfloat16
NN = (((1,), (0,)), ((), ()))
NT = (((1,), (1,)), ((), ()))
VMEM = pl.BlockSpec(memory_space=pltpu.VMEM)
SMEM = pl.BlockSpec(memory_space=pltpu.SMEM)
VMEM_LIMIT = 60 * 2**20


def run_of(maps_ref, member, block):
    run = jnp.int32(0)
    found = jnp.int32(0)
    for j in range(8):
        start = maps_ref[member, 8 * j]
        hit = ((block >= start) & (block < start + 8)).astype(jnp.int32)
        run = jnp.maximum(run, hit * j)
        found = jnp.maximum(found, hit)
    return run, found


def extend_kernel(maps_ref, child_ref, front_ref, out_ref, blocks, packed, arrived, send_sem, recv_sem):
    row, col = lax.axis_index("row"), lax.axis_index("col")
    me = row * 8 + col

    x, k, y = lax.rem(row, 8) // 2, lax.rem(row, 2), col // 2
    z = lax.rem(col, 2) * 2 + row // 8

    def peer(o):
        o = lax.rem(o * 29, 128)
        to_x = lax.rem(x + lax.rem(o, 4), 4)
        to_y = lax.rem(y + lax.rem(o // 4, 4), 4)
        to_z = lax.rem(z + lax.rem(o // 16, 4), 4)
        to_k = lax.rem(k + o // 64, 2)
        return lax.rem(to_z, 2) * 8 + to_x * 2 + to_k, to_y * 2 + to_z // 2

    barrier = pltpu.get_barrier_semaphore()

    @pl.loop(1, 128)
    def _(o):
        pl.semaphore_signal(barrier, inc=1, device_id=peer(o), device_id_type=MESH)

    for g in range(8):
        for h in range(8):
            blocks[g * 8 + h] = child_ref[128 * g : 128 * g + 128, 128 * h : 128 * h + 128]
    member = row // 8
    row_start = maps_ref[member, 8 * lax.rem(row, 8)]
    col_start = maps_ref[member, 8 * col]

    @pl.loop(0, 64)
    def _(p):
        g = lax.rem(p // 8 - lax.rem(row_start, 8) + 8, 8)
        h = lax.rem(lax.rem(p, 8) - lax.rem(col_start, 8) + 8, 8)
        packed[p] = blocks[g * 8 + h]

    arrived[me] = packed[lax.rem(row, 8) * 8 + col]
    pl.semaphore_wait(barrier, 127)

    @pl.loop(1, 128)
    def _(o):
        to_row, to_col = peer(o)
        pltpu.make_async_remote_copy(
            src_ref=packed.at[lax.rem(to_row, 8) * 8 + to_col],
            dst_ref=arrived.at[me],
            send_sem=send_sem,
            recv_sem=recv_sem,
            device_id=(to_row, to_col),
            device_id_type=MESH,
        ).start()

    everything = pltpu.make_async_remote_copy(
        src_ref=arrived.at[pl.ds(0, 127)],
        dst_ref=arrived.at[pl.ds(0, 127)],
        send_sem=send_sem,
        recv_sem=recv_sem,
        device_id=peer(1),
        device_id_type=MESH,
    )
    everything.wait_recv()

    @pl.loop(0, 6)
    def _(l):
        runs = [run_of(maps_ref, k, l * 16 + row) for k in range(2)]
        rows = pl.ds(pl.multiple_of(l * 128, 128), 128)

        @pl.loop(0, 12)
        def _(m):
            cols = pl.ds(pl.multiple_of(m * 128, 128), 128)
            total = front_ref[rows, cols]
            for k in range(2):
                run, found = runs[k]
                other, also = run_of(maps_ref, k, m * 8 + col)
                update = arrived[(k * 8 + run) * 8 + other]
                total = total + update * (found * also).astype(F32)
            out_ref[rows, cols] = total

    everything.wait_send()


def extend(maps, children, front):
    return pl.pallas_call(
        extend_kernel,
        out_shape=jax.ShapeDtypeStruct(front.shape, F32),
        in_specs=[SMEM, VMEM, VMEM],
        out_specs=VMEM,
        scratch_shapes=[
            pltpu.VMEM((64, 128, 128), F32),
            pltpu.VMEM((64, 128, 128), F32),
            pltpu.VMEM((128, 128, 128), F32),
            pltpu.SemaphoreType.DMA,
            pltpu.SemaphoreType.DMA,
        ],
        compiler_params=pltpu.CompilerParams(
            collective_id=0, has_side_effects=True, vmem_limit_bytes=VMEM_LIMIT
        ),
        name="extend_add",
    )(maps, children, front)


class Mover:
    def __init__(self, send_sem):
        self.send_sem = send_sem
        self.sent = []

    def send(self, guard, ref, recv_sem, target):
        number = len(self.sent)

        def copy():
            return pltpu.make_async_remote_copy(
                src_ref=ref(),
                dst_ref=ref(),
                send_sem=self.send_sem.at[number],
                recv_sem=recv_sem(),
                device_id=target,
                device_id_type=MESH,
            )

        self.sent.append((guard, copy))
        pl.when(guard())(lambda: copy().start())

    def finish(self):
        for guard, copy in self.sent:
            pl.when(guard())(lambda copy=copy: copy().wait_send())


def await_copy(guard, dst, recv_sem, peer):
    @pl.when(guard)
    def _():
        pltpu.make_async_remote_copy(
            src_ref=dst,
            dst_ref=dst,
            send_sem=recv_sem,
            recv_sem=recv_sem,
            device_id=peer,
            device_id_type=MESH,
        ).wait_recv()


class Gather:
    def __init__(self, mover, view, half, sem, needed):
        self.mover, self.view, self.half, self.sem, self.needed = mover, view, half, sem, needed

    def whole(self, slot, target):
        self.mover.send(
            lambda: self.needed(slot), lambda: self.view(slot), lambda: self.sem.at[0, slot], target
        )

    def part(self, slot, i, target):
        self.mover.send(
            lambda: self.needed(slot),
            lambda: self.half(slot, i),
            lambda: self.sem.at[i, slot],
            target,
        )

    def got(self, slot, peer):
        await_copy(self.needed(slot), self.view(slot), self.sem.at[0, slot], peer)

    def got_part(self, slot, i, peer):
        await_copy(self.needed(slot), self.half(slot, i), self.sem.at[i, slot], peer)

    def forward(self):
        for slot in self.near[-1]:
            self.got(slot, self.left)
            self.part(slot, 0, self.right)
        for slot in self.near[1]:
            self.got(slot, self.right)
            self.part(slot, 1, self.left)


class RowGather(Gather):
    def __init__(self, mover, view, half, sem, needed, places):
        super().__init__(mover, view, half, sem, needed)
        (h, x, k), (self.z_peer, self.right, self.left, self.mate) = places
        at = lambda h, x, k: h * 8 + lax.rem(x + 4, 4) * 2 + k
        self.own, self.other = at(h, x, k), at(1 - h, x, k)
        self.near = {d: [at(h, x + d, k), at(1 - h, x + d, k)] for d in (-1, 1, 2)}
        self.theirs = [at(g, jnp.int32(p), 1 - k) for g in range(2) for p in range(4)]

    def to_pair(self):
        for target in (self.z_peer, self.right, self.left, self.mate):
            self.whole(self.own, target)

    def to_ring(self):
        self.got(self.other, self.z_peer)
        for target in (self.right, self.left, self.mate):
            self.whole(self.other, target)

    def forward(self):
        super().forward()
        for slot in self.near[-1] + self.near[1]:
            self.whole(slot, self.mate)

    def to_mate(self):
        for slot in self.near[2]:
            self.got_part(slot, 0, self.left)
            self.got_part(slot, 1, self.right)
            self.whole(slot, self.mate)

    def finish(self):
        for slot in self.theirs:
            self.got(slot, self.mate)


class ColGather(Gather):
    def __init__(self, mover, view, half, sem, places):
        super().__init__(mover, view, half, sem, lambda e: e < 12)
        (y, s), (self.z_peer, self.right, self.left) = places
        at = lambda y, s: lax.rem(y + 4, 4) * 2 + s
        self.own = [at(y, s), at(y, s) + 8]
        self.other = [at(y, 1 - s), at(y, 1 - s) + 8]
        self.near = {
            d: [at(y + d, t) + e for t in range(2) for e in (0, 8)] for d in (-1, 1, 2)
        }

    def to_pair(self):
        for slot in self.own:
            for target in (self.z_peer, self.right, self.left):
                self.whole(slot, target)

    def to_ring(self):
        for slot in self.other:
            self.got(slot, self.z_peer)
            for target in (self.right, self.left):
                self.whole(slot, target)

    def finish(self):
        for slot in self.near[2]:
            self.got_part(slot, 0, self.left)
            self.got_part(slot, 1, self.right)


def factor128(a):
    rows = lax.broadcasted_iota(jnp.int32, (8, 128), 0)
    lanes = lax.broadcasted_iota(jnp.int32, (8, 128), 1)
    strips = [a[8 * g : 8 * g + 8, :] for g in range(16)]
    units = [jnp.where(lanes == rows + 8 * g, 1.0, 0.0).astype(jnp.float32) for g in range(16)]
    uppers, inverses = [], []
    full = (8, 128)
    for g in range(16):
        s, t = strips[g], units[g]
        cols = [jnp.broadcast_to(s[:, 8 * g + m : 8 * g + m + 1], full) for m in range(8)]
        e = [[jnp.broadcast_to(cols[m][i : i + 1, :], full) if i >= m else None for m in range(8)] for i in range(8)]
        z = [jnp.broadcast_to(s[i : i + 1, :], full) for i in range(8)]
        y = [jnp.broadcast_to(t[i : i + 1, :], full) for i in range(8)]
        l = [[None] * 8 for _ in range(8)]
        r = []
        for k in range(8):
            d = e[k][k]
            r0 = pl.reciprocal(d, approx=True)
            rk = r0 * (2.0 - d * r0)
            r.append(rk)
            for i in range(k + 1, 8):
                l[i][k] = e[i][k] * rk
            for j in range(k + 1, 8):
                for i in range(j, 8):
                    e[i][j] = e[i][j] - l[i][k] * e[j][k]
            for i in range(k + 1, 8):
                z[i] = z[i] - l[i][k] * z[k]
                y[i] = y[i] - l[i][k] * y[k]
        u = jnp.zeros(full, jnp.float32)
        w = jnp.zeros(full, jnp.float32)
        for i in range(8):
            d = e[i][i]
            q = lax.rsqrt(d)
            q = q * (1.5 - 0.5 * d * q * q)
            u = jnp.where(rows == i, z[i] * q, u)
            w = jnp.where(rows == i, y[i] * q, w)
        uppers.append(jnp.where(lanes >= rows + 8 * g, u, 0.0))
        inverses.append(w)
        if g == 15:
            break
        v = [None] * 8
        x = [None] * 8
        for i in reversed(range(8)):
            vi, xi = z[i] * r[i], y[i] * r[i]
            for m in range(i + 1, 8):
                vi = vi - l[m][i] * v[m]
                xi = xi - l[m][i] * x[m]
            v[i], x[i] = vi, xi
        for h in range(g + 1, 16):
            sh = strips[h]
            acc = [sh[:, 8 * g + m : 8 * g + m + 1] for m in range(8)]
            acc = [jnp.broadcast_to(c, full) for c in acc]
            p = [acc[m] * v[m] for m in range(8)]
            o = [acc[m] * x[m] for m in range(8)]
            while len(p) > 1:
                p = [p[2 * i] + p[2 * i + 1] for i in range(len(p) // 2)]
                o = [o[2 * i] + o[2 * i + 1] for i in range(len(o) // 2)]
            strips[h] = sh - p[0]
            units[h] = units[h] - o[0]
    return jnp.concatenate(uppers, 0), jnp.concatenate(inverses, 0)


def dot(a, b, dims=NN):
    return lax.dot_general(a, b, dims, precision=HIGHEST, preferred_element_type=jnp.float32)


def chol_loop(pv, dinv, between, nsteps=6):
    @pl.loop(0, nsteps)
    def _(J):
        ca = pl.multiple_of(J * 256, 256)
        cb = pl.multiple_of(J * 256 + 128, 128)
        for step, action in enumerate(between):
            pl.when(J == step)(action)
        ua, ia = factor128(pv[pl.ds(ca, 128), pl.ds(ca, 128)])
        la = ua.T
        pv[pl.ds(ca, 128), pl.ds(ca, 128)] = la
        wb = dot(pv[pl.ds(cb, 128), pl.ds(ca, 128)], ia, NT)
        pv[pl.ds(cb, 128), pl.ds(ca, 128)] = wb
        ub, ib = factor128(pv[pl.ds(cb, 128), pl.ds(cb, 128)] - dot(wb, wb, NT))
        pv[pl.ds(cb, 128), pl.ds(cb, 128)] = ub.T
        off = -dot(ib, dot(wb, ia))
        dinv[J, 0:128, 0:128] = ia
        dinv[J, 0:128, 128:256] = jnp.zeros((128, 128), jnp.float32)
        dinv[J, 128:256, 0:128] = off
        dinv[J, 128:256, 128:256] = ib
        inv = dinv[J]
        @pl.loop(J + 1, nsteps)
        def _(R):
            ro = pl.multiple_of(R * 256, 256)
            pv[pl.ds(ro, 256), pl.ds(ca, 256)] = dot(pv[pl.ds(ro, 256), pl.ds(ca, 256)], inv, NT)
        @pl.loop(J + 1, nsteps)
        def _(I):
            io = pl.multiple_of(I * 256, 256)
            wi = pv[pl.ds(io, 256), pl.ds(ca, 256)]
            @pl.loop(I, nsteps)
            def _(R):
                ro = pl.multiple_of(R * 256, 256)
                pv[pl.ds(ro, 256), pl.ds(io, 256)] -= dot(pv[pl.ds(ro, 256), pl.ds(ca, 256)], wi, NT)


def split(v):
    hi = v.astype(BF16)
    return hi, (v - hi.astype(F32)).astype(BF16)


def dot3(ah, al, bh, bl):
    a = jnp.concatenate([ah, ah, al], 1)
    b = jnp.concatenate([bh, bl, bh], 0)
    return lax.dot_general(a, b, NN, preferred_element_type=F32)


def finish_steps(row, col, a_ref, g1, g2, l_ref, d_ref, out_ref, xh, xl, yh, yl):
    for i in range(6):
        dh, dl = split(d_ref[i])
        lh, ll = split(l_ref[256 * i : 256 * i + 256, : 256 * i]) if i else (None, None)

        def solve(rhs, cols):
            if i:
                rhs = rhs - dot3(lh, ll, xh[: 256 * i, cols], xl[: 256 * i, cols])
            hi, lo = split(dot3(dh, dl, *split(rhs)))
            xh[256 * i : 256 * i + 256, cols] = hi
            xl[256 * i : 256 * i + 256, cols] = lo

        @pl.loop(0, 2)
        def _(n):
            cols = pl.ds(pl.multiple_of(n * 768, 256), 768)
            solve(g1[2 * i : 2 * i + 2, :, cols].reshape(256, 768), cols)

        solve(g2[2 * i : 2 * i + 2].reshape(256, 768), pl.ds(1536, 768))
    for l in range(6):
        lanes = slice(1536 + 128 * l, 1664 + 128 * l)
        yh[128 * l : 128 * l + 128, :] = xh[:, lanes].T
        yl[128 * l : 128 * l + 128, :] = xl[:, lanes].T

    @pl.loop(0, 6)
    def _(t):
        rows = pl.ds(pl.multiple_of(t // 2 * 256, 256), 256)
        cols = pl.ds(pl.multiple_of(lax.rem(t, 2) * 768, 256), 768)
        out_ref[rows, cols] = a_ref[rows, cols] - dot3(
            yh[rows, :], yl[rows, :], xh[:, cols], xl[:, cols]
        )

    @pl.when(row < 12)
    def _():
        out_ref[0:128, :] = jnp.zeros((128, 1536), F32)

    def place(block, m):
        lanes = pl.ds(pl.multiple_of(block * 128, 128), 128)
        values = yh[:, lanes].astype(F32) + yl[:, lanes].astype(F32)
        i = lax.broadcasted_iota(jnp.int32, values.shape, 0)
        j = lax.broadcasted_iota(jnp.int32, values.shape, 1)
        matrix_row = (i // 128 * 16 + row) * 128 + lax.rem(i, 128)
        out_ref[:, 128 * m : 128 * m + 128] = jnp.where(
            matrix_row >= block * 128 + j, values, 0.0
        )

    place(col, 0)

    @pl.when(col < 4)
    def _():
        place(col + 8, 1)


def panel_kernel(
    a_ref, out_ref, g1, g2, pv, dinv, xh, xl, yh, yl, early_sem, send_sem, head_sem, g1_sem, g2_sem, pv_sem
):
    row, col = lax.axis_index("row"), lax.axis_index("col")
    h, x, k = row // 8, lax.rem(row, 8) // 2, lax.rem(row, 2)
    y, s = col // 2, lax.rem(col, 2)
    at_x = lambda p: h * 8 + lax.rem(p + 4, 4) * 2 + k
    at_y = lambda p: lax.rem(p + 4, 4) * 2 + s
    row_peers = [
        ((1 - h) * 8 + x * 2 + k, col),
        (at_x(x + 1), col),
        (at_x(x - 1), col),
        (h * 8 + x * 2 + 1 - k, col),
    ]
    col_peers = [(row, y * 2 + 1 - s), (row, at_y(y + 1)), (row, at_y(y - 1))]
    all_cols = [(row, lax.rem(col + o, 8)) for o in range(1, 8)]
    barrier = pltpu.get_barrier_semaphore()
    for p in row_peers + all_cols:
        pl.semaphore_signal(barrier, inc=1, device_id=p, device_id_type=MESH)

    g2[col] = a_ref[:, 0:128].T

    @pl.when(col < 4)
    def _():
        g2[col + 8] = a_ref[:, 128:256].T

    pl.semaphore_wait(barrier, 11)

    early, mover = Mover(early_sem), Mover(send_sem)
    row_places = ((h, x, k), row_peers)

    def head(e):
        return g2.at[e, :, pl.ds(0, 128)]

    for p in all_cols:
        early.send(lambda: col >= 0, lambda: head(col), lambda: head_sem.at[col], p)
        early.send(lambda: col < 4, lambda: head(col + 8), lambda: head_sem.at[col + 8], p)

    @pl.when(row < 12)
    def _():
        g1[row] = a_ref[0:128, :]

    wide = pl.ds(128, 1408)
    rows1 = RowGather(
        mover,
        lambda q: g1.at[q, :, wide],
        lambda q, i: g1.at[q, pl.ds(64 * i, 64), wide],
        g1_sem,
        lambda q: q < 12,
        row_places,
    )
    rest = pl.ds(128, 640)
    cols2 = ColGather(
        mover,
        lambda e: g2.at[e, :, rest],
        lambda e, i: g2.at[e, pl.ds(64 * i, 64), rest],
        g2_sem,
        ((y, s), col_peers),
    )

    def block_col(q):
        return pl.ds(pl.multiple_of(q * 128, 128), 128)

    pivots = [
        RowGather(
            early,
            lambda q, t=t: pv.at[pl.ds(512 * t, 512), block_col(q)],
            lambda q, i, t=t: pv.at[pl.ds(512 * t + 256 * i, 256), block_col(q)],
            pv_sem.at[t],
            lambda q, t=t: q < 4 * (t + 1),
            row_places,
        )
        for t in range(3)
    ]
    for e in range(12):
        await_copy(col != e % 8, head(e), head_sem.at[e], (row, e % 8))

    @pl.when(row < 12)
    def _():
        @pl.loop(0, 12)
        def _(e):
            pv[pl.ds(pl.multiple_of(e * 128, 128), 128), block_col(row)] = g2[e, :, 0:128]

    for p in pivots:
        p.to_pair()
    cols2.to_pair()
    for p in pivots:
        p.to_ring()
    for p in pivots:
        p.forward()
    rows1.to_pair()
    cols2.to_ring()
    for p in pivots:
        p.to_mate()
    for p in pivots:
        p.finish()
    rows1.to_ring()
    early.finish()
    chol_loop(pv, dinv, [lambda: None, cols2.forward, rows1.forward, lambda: None, rows1.to_mate])
    cols2.finish()
    rows1.finish()
    mover.finish()
    finish_steps(row, col, a_ref, g1, g2, pv, dinv, out_ref, xh, xl, yh, yl)


def panel(a):
    return pl.pallas_call(
        panel_kernel,
        out_shape=jax.ShapeDtypeStruct(a.shape, F32),
        in_specs=[VMEM],
        out_specs=VMEM,
        scratch_shapes=[
            pltpu.VMEM((12, 128, 1536), F32),
            pltpu.VMEM((12, 128, 768), F32),
            pltpu.VMEM((1536, 1536), F32),
            pltpu.VMEM((6, 256, 256), F32),
            pltpu.VMEM((1536, 2304), BF16),
            pltpu.VMEM((1536, 2304), BF16),
            pltpu.VMEM((768, 1536), BF16),
            pltpu.VMEM((768, 1536), BF16),
            pltpu.SemaphoreType.DMA((96,)),
            pltpu.SemaphoreType.DMA((64,)),
            pltpu.SemaphoreType.DMA((16,)),
            pltpu.SemaphoreType.DMA((2, 16)),
            pltpu.SemaphoreType.DMA((2, 16)),
            pltpu.SemaphoreType.DMA((3, 2, 16)),
        ],
        compiler_params=pltpu.CompilerParams(
            collective_id=1, has_side_effects=True, vmem_limit_bytes=62 * 2**20
        ),
        name="panel",
    )(a)


def shards(front, children, maps):
    return panel(extend(maps, children, front))


def solution(mesh):
    in_specs = (P("row", "col"), P("row", "col"), P())
    out_specs = P("row", "col")
    return jax.shard_map(shards, mesh=mesh, in_specs=in_specs, out_specs=out_specs, check_vma=False)
```

```python
import jax
import jax.numpy as jnp
from jax import lax
from jax.experimental import pallas as pl
from jax.experimental.pallas import tpu as pltpu
from jax.sharding import PartitionSpec as P

HIGHEST = lax.Precision.HIGHEST
MESH = pl.DeviceIdType.MESH
F32 = jnp.float32
BF16 = jnp.bfloat16
NN = (((1,), (0,)), ((), ()))
NT = (((1,), (1,)), ((), ()))
VMEM = pl.BlockSpec(memory_space=pltpu.VMEM)
SMEM = pl.BlockSpec(memory_space=pltpu.SMEM)
VMEM_LIMIT = 60 * 2**20


def run_of(maps_ref, member, block):
    run = jnp.int32(0)
    found = jnp.int32(0)
    for j in range(8):
        start = maps_ref[member, 8 * j]
        hit = ((block >= start) & (block < start + 8)).astype(jnp.int32)
        run = jnp.maximum(run, hit * j)
        found = jnp.maximum(found, hit)
    return run, found


class Mover:
    def __init__(self, send_sem):
        self.send_sem = send_sem
        self.sent = []

    def send(self, guard, ref, recv_sem, target, to=None):
        number = len(self.sent)

        def copy():
            return pltpu.make_async_remote_copy(
                src_ref=ref(),
                dst_ref=(to or ref)(),
                send_sem=self.send_sem.at[number],
                recv_sem=recv_sem(),
                device_id=target,
                device_id_type=MESH,
            )

        self.sent.append((guard, copy))
        pl.when(guard())(lambda: copy().start())

    def finish(self):
        for guard, copy in self.sent:
            pl.when(guard())(lambda copy=copy: copy().wait_send())


def await_copy(guard, dst, recv_sem, peer):
    @pl.when(guard)
    def _():
        pltpu.make_async_remote_copy(
            src_ref=dst,
            dst_ref=dst,
            send_sem=recv_sem,
            recv_sem=recv_sem,
            device_id=peer,
            device_id_type=MESH,
        ).wait_recv()


class Gather:
    def __init__(self, mover, view, half, sem, needed):
        self.mover, self.view, self.half, self.sem, self.needed = mover, view, half, sem, needed

    def whole(self, slot, target):
        self.mover.send(
            lambda: self.needed(slot), lambda: self.view(slot), lambda: self.sem.at[0, slot], target
        )

    def part(self, slot, i, target):
        self.mover.send(
            lambda: self.needed(slot),
            lambda: self.half(slot, i),
            lambda: self.sem.at[i, slot],
            target,
        )

    def got(self, slot, peer):
        await_copy(self.needed(slot), self.view(slot), self.sem.at[0, slot], peer)

    def got_part(self, slot, i, peer):
        await_copy(self.needed(slot), self.half(slot, i), self.sem.at[i, slot], peer)

    def forward(self):
        for slot in self.near[-1]:
            self.got(slot, self.left)
            self.part(slot, 0, self.right)
        for slot in self.near[1]:
            self.got(slot, self.right)
            self.part(slot, 1, self.left)


class RowGather(Gather):
    def __init__(self, mover, view, half, sem, needed, places):
        super().__init__(mover, view, half, sem, needed)
        (h, x, k), (self.z_peer, self.right, self.left, self.mate) = places
        at = lambda h, x, k: h * 8 + lax.rem(x + 4, 4) * 2 + k
        self.own, self.other = at(h, x, k), at(1 - h, x, k)
        self.near = {d: [at(h, x + d, k), at(1 - h, x + d, k)] for d in (-1, 1, 2)}
        self.theirs = [at(g, jnp.int32(p), 1 - k) for g in range(2) for p in range(4)]

    def to_pair(self):
        for target in (self.z_peer, self.right, self.left, self.mate):
            self.whole(self.own, target)

    def to_ring(self):
        self.got(self.other, self.z_peer)
        for target in (self.right, self.left, self.mate):
            self.whole(self.other, target)

    def forward(self):
        super().forward()
        for slot in self.near[-1] + self.near[1]:
            self.whole(slot, self.mate)

    def to_mate(self):
        for slot in self.near[2]:
            self.got_part(slot, 0, self.left)
            self.got_part(slot, 1, self.right)
            self.whole(slot, self.mate)

    def finish(self):
        for slot in self.theirs:
            self.got(slot, self.mate)


class ColGather(Gather):
    def __init__(self, mover, view, half, sem, places):
        super().__init__(mover, view, half, sem, lambda e: e < 12)
        (y, s), (self.z_peer, self.right, self.left) = places
        at = lambda y, s: lax.rem(y + 4, 4) * 2 + s
        self.own = [at(y, s), at(y, s) + 8]
        self.other = [at(y, 1 - s), at(y, 1 - s) + 8]
        self.near = {
            d: [at(y + d, t) + e for t in range(2) for e in (0, 8)] for d in (-1, 1, 2)
        }

    def to_pair(self):
        for slot in self.own:
            for target in (self.z_peer, self.right, self.left):
                self.whole(slot, target)

    def to_ring(self):
        for slot in self.other:
            self.got(slot, self.z_peer)
            for target in (self.right, self.left):
                self.whole(slot, target)

    def finish(self):
        for slot in self.near[2]:
            self.got_part(slot, 0, self.left)
            self.got_part(slot, 1, self.right)


def factor128(a):
    full = (8, 128)
    rows = lax.broadcasted_iota(jnp.int32, full, 0)
    lanes = lax.broadcasted_iota(jnp.int32, full, 1)
    strips = [a[8 * g : 8 * g + 8, :] for g in range(16)]
    units = [jnp.where(lanes == rows + 8 * g, 1.0, 0.0).astype(F32) for g in range(16)]
    uppers, inverses = [], []
    for g in range(16):
        s, t = strips[g], units[g]
        cols = [jnp.broadcast_to(s[:, 8 * g + m : 8 * g + m + 1], full) for m in range(8)]
        e = [[jnp.broadcast_to(cols[m][i : i + 1, :], full) for m in range(i + 1)] for i in range(8)]
        z = [jnp.broadcast_to(s[i : i + 1, :], full) for i in range(8)]
        y = [jnp.broadcast_to(t[i : i + 1, :], full) for i in range(8)]
        l = [[None] * 8 for _ in range(8)]
        r = []
        for k in range(8):
            r.append(pl.reciprocal(e[k][k], approx=True))
            for i in range(k + 1, 8):
                l[i][k] = e[i][k] * r[k]
            for j in range(k + 1, 8):
                for i in range(j, 8):
                    e[i][j] = e[i][j] - l[i][k] * e[j][k]
            for i in range(k + 1, 8):
                z[i] = z[i] - l[i][k] * z[k]
                y[i] = y[i] - l[i][k] * y[k]
        u = jnp.zeros(full, F32)
        w = jnp.zeros(full, F32)
        for i in range(8):
            q = lax.rsqrt(e[i][i])
            u = jnp.where(rows == i, z[i] * q, u)
            w = jnp.where(rows == i, y[i] * q, w)
        uppers.append(jnp.where(lanes >= rows + 8 * g, u, 0.0))
        inverses.append(w)
        top = g // 4 * 4 + 4
        if g + 1 < top:
            v, x = [None] * 8, [None] * 8
            for i in reversed(range(8)):
                v[i], x[i] = z[i] * r[i], y[i] * r[i]
                for m in range(i + 1, 8):
                    v[i] = v[i] - l[m][i] * v[m]
                    x[i] = x[i] - l[m][i] * x[m]
            for h in range(g + 1, top):
                c = [
                    jnp.broadcast_to(strips[h][:, 8 * g + m : 8 * g + m + 1], full)
                    for m in range(8)
                ]
                p = [c[m] * v[m] for m in range(8)]
                o = [c[m] * x[m] for m in range(8)]
                while len(p) > 1:
                    p = [p[2 * i] + p[2 * i + 1] for i in range(len(p) // 2)]
                    o = [o[2 * i] + o[2 * i + 1] for i in range(len(o) // 2)]
                strips[h] = strips[h] - p[0]
                units[h] = units[h] - o[0]
        elif top < 16:
            u = jnp.concatenate(uppers[top - 4 : top], 0)
            w = jnp.concatenate(inverses[top - 4 : top], 0)
            product = lax.dot_general(
                u,
                jnp.concatenate([u, w], 1),
                (((0,), (0,)), ((), ())),
                precision=HIGHEST,
                preferred_element_type=F32,
            )
            for h in range(top, 16):
                strips[h] = strips[h] - product[8 * h : 8 * h + 8, :128]
                units[h] = units[h] - product[8 * h : 8 * h + 8, 128:]
    return jnp.concatenate(uppers, 0), jnp.concatenate(inverses, 0)


def dot(a, b, dims=NN):
    return lax.dot_general(a, b, dims, precision=HIGHEST, preferred_element_type=jnp.float32)


def inverse_at(dinv, J):
    a, b, c, d = (dinv[J * 4 + i] for i in range(4))
    return jnp.concatenate([jnp.concatenate([a, b], 1), jnp.concatenate([c, d], 1)], 0)


def chol_loop(pv, dinv, between, nsteps=6):
    @pl.loop(0, nsteps)
    def _(J):
        ca = pl.multiple_of(J * 256, 256)
        cb = pl.multiple_of(J * 256 + 128, 128)
        for step, action in enumerate(between):
            pl.when(J == step)(action)
        ua, ia = factor128(pv[pl.ds(ca, 128), pl.ds(ca, 128)])
        la = ua.T
        pv[pl.ds(ca, 128), pl.ds(ca, 128)] = la
        wb = dot(pv[pl.ds(cb, 128), pl.ds(ca, 128)], ia, NT)
        pv[pl.ds(cb, 128), pl.ds(ca, 128)] = wb
        ub, ib = factor128(pv[pl.ds(cb, 128), pl.ds(cb, 128)] - dot(wb, wb, NT))
        pv[pl.ds(cb, 128), pl.ds(cb, 128)] = ub.T
        off = -dot(ib, dot(wb, ia))
        dinv[J * 4] = ia
        dinv[J * 4 + 1] = jnp.zeros((128, 128), F32)
        dinv[J * 4 + 2] = off
        dinv[J * 4 + 3] = ib
        inv = inverse_at(dinv, J)
        @pl.loop(J + 1, nsteps)
        def _(R):
            ro = pl.multiple_of(R * 256, 256)
            pv[pl.ds(ro, 256), pl.ds(ca, 256)] = dot(pv[pl.ds(ro, 256), pl.ds(ca, 256)], inv, NT)
        @pl.loop(J + 1, nsteps)
        def _(I):
            io = pl.multiple_of(I * 256, 256)
            wi = pv[pl.ds(io, 256), pl.ds(ca, 256)]
            @pl.loop(I, nsteps)
            def _(R):
                ro = pl.multiple_of(R * 256, 256)
                pv[pl.ds(ro, 256), pl.ds(io, 256)] -= dot(pv[pl.ds(ro, 256), pl.ds(ca, 256)], wi, NT)


def split(v):
    hi = v.astype(BF16)
    return hi, (v - hi.astype(F32)).astype(BF16)


def dot3(ah, al, bh, bl):
    a = jnp.concatenate([ah, ah, al], 1)
    b = jnp.concatenate([bh, bl, bh], 0)
    return lax.dot_general(a, b, NN, preferred_element_type=F32)


def solve_steps(g1, g2, l_ref, d_ref, xh, xl, yh, yl):
    for i in range(6):
        dh, dl = split(inverse_at(d_ref, i))
        lh, ll = split(l_ref[256 * i : 256 * i + 256, : 256 * i]) if i else (None, None)
        span = slice(256 * i, 256 * i + 256)
        blocks = slice(2 * i, 2 * i + 2)

        @pl.loop(0, 2)
        def _(n):
            cols = pl.ds(pl.multiple_of(n * 768, 256), 768)
            rhs = g1[blocks, :, cols].reshape(256, 768)
            if i:
                rhs = rhs - dot3(lh, ll, xh[: 256 * i, cols], xl[: 256 * i, cols])
            hi, lo = split(dot3(dh, dl, *split(rhs)))
            xh[span, cols] = hi
            xl[span, cols] = lo

        rhs = g2[blocks].reshape(256, 768)
        if i:
            rhs = rhs - dot3(lh, ll, *split(g2[: 2 * i].reshape(256 * i, 768)))
        g2[blocks] = dot3(dh, dl, *split(rhs)).reshape(2, 128, 768)
    for l in range(6):
        rows = slice(128 * l, 128 * l + 128)
        hi, lo = split(g2[:, :, rows].reshape(1536, 128).T)
        yh[rows, :] = hi
        yl[rows, :] = lo

    @pl.loop(0, 6)
    def _(t):
        rows = pl.ds(pl.multiple_of(t // 2 * 256, 256), 256)
        cols = pl.ds(pl.multiple_of(lax.rem(t, 2) * 768, 256), 768)
        l_ref[rows, cols] = dot3(yh[rows, :], yl[rows, :], xh[:, cols], xl[:, cols])


def place_steps(row, col, out_ref, yh, yl):
    @pl.when(row < 12)
    def _():
        out_ref[0:128, :] = jnp.zeros((128, 1536), F32)

    def place(block, m):
        lanes = pl.ds(pl.multiple_of(block * 128, 128), 128)
        values = yh[:, lanes].astype(F32) + yl[:, lanes].astype(F32)
        i = lax.broadcasted_iota(jnp.int32, values.shape, 0)
        j = lax.broadcasted_iota(jnp.int32, values.shape, 1)
        matrix_row = (i // 128 * 16 + row) * 128 + lax.rem(i, 128)
        out_ref[:, 128 * m : 128 * m + 128] = jnp.where(
            matrix_row >= block * 128 + j, values, 0.0
        )

    place(col, 0)

    @pl.when(col < 4)
    def _():
        place(col + 8, 1)


def panel_kernel(
    maps_ref,
    front_ref,
    child_ref,
    out_ref,
    arrived,
    g1,
    g2,
    pv,
    dinv,
    xh,
    xl,
    yh,
    yl,
    load_sem,
    block_send,
    first_sem,
    block_sem,
    early_sem,
    send_sem,
    head_sem,
    turn_sem,
    g1_sem,
    g2_sem,
    pv_sem,
):
    first = dinv.at[pl.ds(0, 16)]
    row, col = lax.axis_index("row"), lax.axis_index("col")
    h, x, k = row // 8, lax.rem(row, 8) // 2, lax.rem(row, 2)
    y, s = col // 2, lax.rem(col, 2)
    z = s * 2 + h
    me = row * 8 + col
    at_x = lambda p: h * 8 + lax.rem(p + 4, 4) * 2 + k
    at_y = lambda p: lax.rem(p + 4, 4) * 2 + s
    row_peers = [
        ((1 - h) * 8 + x * 2 + k, col),
        (at_x(x + 1), col),
        (at_x(x - 1), col),
        (h * 8 + x * 2 + 1 - k, col),
    ]
    col_peers = [(row, y * 2 + 1 - s), (row, at_y(y + 1)), (row, at_y(y - 1))]

    def block_at(i):
        return pl.ds(pl.multiple_of(i * 128, 128), 128)

    for i in range(8):
        for j in range(8):
            pltpu.make_async_copy(
                child_ref.at[pl.ds(128 * i, 128), pl.ds(128 * j, 128)],
                arrived.at[i * 8 + j],
                load_sem,
            ).start()
    pltpu.make_async_copy(arrived.at[pl.ds(0, 64)], arrived.at[pl.ds(64, 64)], load_sem).wait()
    run = lax.rem(row, 8)
    row_start = lax.rem(maps_ref[h, 8 * run], 8)
    col_start = lax.rem(maps_ref[h, 8 * col], 8)

    @pl.loop(0, 8)
    def _(r):
        i = lax.rem(r - row_start + 8, 8)

        @pl.loop(0, 8)
        def _(c):
            j = lax.rem(c - col_start + 8, 8)
            p = r * 8 + c
            out_ref[block_at(p // 12), block_at(lax.rem(p, 12))] = arrived[i * 8 + j]

    def packed(r, c):
        p = r * 8 + c
        return out_ref.at[block_at(p // 12), block_at(lax.rem(p, 12))]

    arrived[me] = packed(run, col)[...]

    def peer(o):
        o = lax.rem(o * 37, 128)
        to_x = lax.rem(x + lax.rem(o, 4), 4)
        to_y = lax.rem(y + lax.rem(o // 4, 4), 4)
        to_z = lax.rem(z + lax.rem(o // 16, 4), 4)
        to_k = lax.rem(k + o // 64, 2)
        return lax.rem(to_z, 2) * 8 + to_x * 2 + to_k, to_y * 2 + to_z // 2

    barrier = pltpu.get_barrier_semaphore()

    @pl.loop(1, 128)
    def _(o):
        pl.semaphore_signal(barrier, inc=1, device_id=peer(o), device_id_type=MESH)

    pl.semaphore_wait(barrier, 127)

    def is_first(to_row):
        return ((run == 0) & (to_row < 8)) | ((run == 1) & (to_row >= 8) & (to_row < 12))

    def send_first(base, count):
        @pl.loop(0, 8 * count)
        def _(t):
            i = lax.rem(t, count)
            to_row, to_col = base + i, lax.rem(col + t // count + i, 8)

            @pl.when((to_row != row) | (to_col != col))
            def _():
                pltpu.make_async_remote_copy(
                    src_ref=packed(lax.rem(to_row, 8), to_col),
                    dst_ref=first.at[h * 8 + col],
                    send_sem=block_send,
                    recv_sem=first_sem,
                    device_id=(to_row, to_col),
                    device_id_type=MESH,
                ).start()

            @pl.when((to_row == row) & (to_col == col))
            def _():
                first[h * 8 + col] = packed(lax.rem(to_row, 8), to_col)[...]

    pl.when(run == 0)(lambda: send_first(0, 8))
    pl.when(run == 1)(lambda: send_first(8, 4))

    def send_blocks(start, stop):
        @pl.loop(start, stop)
        def _(o):
            to_row, to_col = peer(o)

            @pl.when(jnp.logical_not(is_first(to_row)))
            def _():
                pltpu.make_async_remote_copy(
                    src_ref=packed(lax.rem(to_row, 8), to_col),
                    dst_ref=arrived.at[me],
                    send_sem=block_send,
                    recv_sem=block_sem.at[row],
                    device_id=(to_row, to_col),
                    device_id_type=MESH,
                ).start()

    def await_blocks(ref, sem, send=False):
        copy = pltpu.make_async_remote_copy(
            src_ref=ref,
            dst_ref=ref,
            send_sem=sem,
            recv_sem=sem,
            device_id=row_peers[0],
            device_id_type=MESH,
        )
        copy.wait_send() if send else copy.wait_recv()

    mine = jnp.where(row < 8, 0, 1)
    own_first = (row < 12) & (run == mine)

    @pl.when((row < 12) & own_first)
    def _():
        await_blocks(first.at[pl.ds(0, 15)], first_sem)

    @pl.when((row < 12) & jnp.logical_not(own_first))
    def _():
        await_blocks(first, first_sem)

    @pl.when((row >= 8) & (row < 12))
    def _():
        @pl.loop(0, 16)
        def _(i):
            arrived[(i // 8 * 8 + 1) * 8 + lax.rem(i, 8)] = first[i]

    early, mover = Mover(early_sem), Mover(send_sem)

    @pl.when(row < 12)
    def _():
        found = [run_of(maps_ref, member, row)[1] for member in range(2)]

        @pl.loop(0, 12)
        def _(m):
            total = front_ref[0:128, block_at(m)]
            for member in range(2):
                other, also = run_of(maps_ref, member, m * 8 + col)
                total = total + first[member * 8 + other] * (found[member] * also).astype(F32)
            g1[row, :, block_at(m)] = total

    def turned(m):
        return g1.at[row, :, pl.ds(128 * m, 128)]

    def head(e):
        return g2.at[e, :, pl.ds(0, 128)]

    own_head = (row < 12) & (run == col)
    for j in range(2):
        for o in range(8):
            target = (col + 8 * j, lax.rem(col + o, 8))
            early.send(
                lambda t=target: (row < 12) & ((t[0] != row) | (t[1] != col)),
                lambda j=j: turned(j),
                lambda: head_sem.at[row],
                target,
                lambda: head(row),
            )

    @pl.when(own_head)
    def _():
        g2[row, :, 0:128] = g1[row, :, block_at(h)]

    for j in range(2):
        target = (col + 8 * j, run)
        for l in range(1, 6):
            mover.send(
                lambda t=target: (row < 12) & ((t[0] != row) | (t[1] != col)),
                lambda j=j, l=l: turned(2 * l + j),
                lambda: turn_sem.at[row],
                target,
                lambda l=l: g2.at[row, :, pl.ds(128 * l, 128)],
            )

    @pl.when(own_head)
    def _():
        for l in range(1, 6):
            g2[row, :, 128 * l : 128 * l + 128] = g1[row, :, block_at(2 * l + h)]

    row_places = ((h, x, k), row_peers)
    wide = pl.ds(128, 1408)
    rows1 = RowGather(
        mover,
        lambda q: g1.at[q, :, wide],
        lambda q, i: g1.at[q, pl.ds(64 * i, 64), wide],
        g1_sem,
        lambda q: q < 12,
        row_places,
    )
    rest = pl.ds(128, 640)
    cols2 = ColGather(
        mover,
        lambda e: g2.at[e, :, rest],
        lambda e, i: g2.at[e, pl.ds(64 * i, 64), rest],
        g2_sem,
        ((y, s), col_peers),
    )
    pivots = [
        RowGather(
            early,
            lambda q, t=t: pv.at[pl.ds(512 * t, 512), block_at(q)],
            lambda q, i, t=t: pv.at[pl.ds(512 * t + 256 * i, 256), block_at(q)],
            pv_sem.at[t],
            lambda q, t=t: q < 4 * (t + 1),
            row_places,
        )
        for t in range(3)
    ]
    for e in range(12):
        await_copy(
            jnp.logical_not(own_head & (row == e)), head(e), head_sem.at[e], (e, lax.rem(row, 8))
        )

    @pl.when(row < 12)
    def _():
        @pl.loop(0, 12)
        def _(e):
            pv[block_at(e), block_at(row)] = g2[e, :, 0:128]

    for p in pivots:
        p.to_pair()
    for slot in (col, col + 8):
        await_copy(
            (slot < 12) & jnp.logical_not(own_head & (row == slot)),
            g2.at[lax.rem(slot, 12), :, rest],
            turn_sem.at[slot],
            (lax.rem(slot, 12), lax.rem(row, 8)),
        )
    cols2.to_pair()
    for p in pivots:
        p.to_ring()
    for p in pivots:
        p.forward()
    rows1.to_pair()
    cols2.to_ring()
    for p in pivots:
        p.to_mate()
    for p in pivots:
        p.finish()
    rows1.to_ring()
    early.finish()

    def step0():
        send_blocks(1, 16)

    def step1():
        cols2.forward()
        send_blocks(16, 36)

    def step2():
        rows1.forward()
        send_blocks(36, 64)

    def step3():
        send_blocks(64, 96)

    def step4():
        rows1.to_mate()
        send_blocks(96, 128)

    chol_loop(pv, dinv, [step0, step1, step2, step3, step4])
    cols2.finish()
    rows1.finish()
    mover.finish()
    solve_steps(g1, g2, pv, dinv, xh, xl, yh, yl)

    for q in range(16):
        early_row = (row < 12) & (lax.rem(jnp.int32(q), 8) == mine)
        wanted = jnp.logical_not(early_row)

        @pl.when(wanted & (row == q))
        def _():
            await_blocks(arrived.at[pl.ds(0, 7)], block_sem.at[q])

        @pl.when(wanted & (row != q))
        def _():
            await_blocks(arrived.at[pl.ds(0, 8)], block_sem.at[q])

    await_blocks(arrived.at[pl.ds(0, 127)], block_send, True)

    @pl.loop(0, 6)
    def _(l):
        runs = [run_of(maps_ref, member, l * 16 + row) for member in range(2)]

        @pl.loop(0, 12)
        def _(m):
            total = front_ref[block_at(l), block_at(m)] - pv[block_at(l), block_at(m)]
            for member in range(2):
                mine, found = runs[member]
                other, also = run_of(maps_ref, member, m * 8 + col)
                update = arrived[(member * 8 + mine) * 8 + other]
                total = total + update * (found * also).astype(F32)
            out_ref[block_at(l), block_at(m)] = total

    place_steps(row, col, out_ref, yh, yl)


def panel(maps, front, children):
    return pl.pallas_call(
        panel_kernel,
        out_shape=jax.ShapeDtypeStruct(front.shape, F32),
        in_specs=[SMEM, VMEM, pl.BlockSpec(memory_space=pl.ANY)],
        out_specs=VMEM,
        scratch_shapes=[
            pltpu.VMEM((128, 128, 128), F32),
            pltpu.VMEM((12, 128, 1536), F32),
            pltpu.VMEM((12, 128, 768), F32),
            pltpu.VMEM((1536, 1536), F32),
            pltpu.VMEM((24, 128, 128), F32),
            pltpu.VMEM((1536, 1536), BF16),
            pltpu.VMEM((1536, 1536), BF16),
            pltpu.VMEM((768, 1536), BF16),
            pltpu.VMEM((768, 1536), BF16),
            pltpu.SemaphoreType.DMA,
            pltpu.SemaphoreType.DMA,
            pltpu.SemaphoreType.DMA,
            pltpu.SemaphoreType.DMA((16,)),
            pltpu.SemaphoreType.DMA((96,)),
            pltpu.SemaphoreType.DMA((64,)),
            pltpu.SemaphoreType.DMA((16,)),
            pltpu.SemaphoreType.DMA((16,)),
            pltpu.SemaphoreType.DMA((2, 16)),
            pltpu.SemaphoreType.DMA((2, 16)),
            pltpu.SemaphoreType.DMA((3, 2, 16)),
        ],
        compiler_params=pltpu.CompilerParams(
            collective_id=0, has_side_effects=True, vmem_limit_bytes=63 * 2**20
        ),
        name="panel",
    )(maps, front, children)


def shards(front, children, maps):
    return panel(maps, front, children)


def solution(mesh):
    in_specs = (P("row", "col"), P("row", "col"), P())
    out_specs = P("row", "col")
    return jax.shard_map(shards, mesh=mesh, in_specs=in_specs, out_specs=out_specs, check_vma=False)
```

```python
import jax
import jax.numpy as jnp
from jax import lax
from jax.experimental import pallas as pl
from jax.experimental.pallas import tpu as pltpu
from jax.sharding import PartitionSpec as P

HIGHEST = lax.Precision.HIGHEST
MESH = pl.DeviceIdType.MESH
F32 = jnp.float32
BF16 = jnp.bfloat16
NN = (((1,), (0,)), ((), ()))
NT = (((1,), (1,)), ((), ()))
VMEM = pl.BlockSpec(memory_space=pltpu.VMEM)
SMEM = pl.BlockSpec(memory_space=pltpu.SMEM)
VMEM_LIMIT = 60 * 2**20


def run_of(maps_ref, member, block):
    run = jnp.int32(0)
    found = jnp.int32(0)
    for j in range(8):
        start = maps_ref[member, 8 * j]
        hit = ((block >= start) & (block < start + 8)).astype(jnp.int32)
        run = jnp.maximum(run, hit * j)
        found = jnp.maximum(found, hit)
    return run, found


class Mover:
    def __init__(self, send_sem):
        self.send_sem = send_sem
        self.sent = []

    def send(self, guard, ref, recv_sem, target, to=None):
        number = len(self.sent)

        def copy():
            return pltpu.make_async_remote_copy(
                src_ref=ref(),
                dst_ref=(to or ref)(),
                send_sem=self.send_sem.at[number],
                recv_sem=recv_sem(),
                device_id=target,
                device_id_type=MESH,
            )

        self.sent.append((guard, copy))
        pl.when(guard())(lambda: copy().start())

    def finish(self):
        for guard, copy in self.sent:
            pl.when(guard())(lambda copy=copy: copy().wait_send())


def await_copy(guard, dst, recv_sem, peer):
    @pl.when(guard)
    def _():
        pltpu.make_async_remote_copy(
            src_ref=dst,
            dst_ref=dst,
            send_sem=recv_sem,
            recv_sem=recv_sem,
            device_id=peer,
            device_id_type=MESH,
        ).wait_recv()


class Gather:
    def __init__(self, mover, view, half, sem, needed):
        self.mover, self.view, self.half, self.sem, self.needed = mover, view, half, sem, needed

    def whole(self, slot, target):
        self.mover.send(
            lambda: self.needed(slot), lambda: self.view(slot), lambda: self.sem.at[0, slot], target
        )

    def part(self, slot, i, target):
        self.mover.send(
            lambda: self.needed(slot),
            lambda: self.half(slot, i),
            lambda: self.sem.at[i, slot],
            target,
        )

    def got(self, slot, peer):
        await_copy(self.needed(slot), self.view(slot), self.sem.at[0, slot], peer)

    def got_part(self, slot, i, peer):
        await_copy(self.needed(slot), self.half(slot, i), self.sem.at[i, slot], peer)

    def forward(self):
        for slot in self.near[-1]:
            self.got(slot, self.left)
            self.part(slot, 0, self.right)
        for slot in self.near[1]:
            self.got(slot, self.right)
            self.part(slot, 1, self.left)


class RowGather(Gather):
    def __init__(self, mover, view, half, sem, needed, places):
        super().__init__(mover, view, half, sem, needed)
        (h, x, k), (self.z_peer, self.right, self.left, self.mate) = places
        at = lambda h, x, k: h * 8 + lax.rem(x + 4, 4) * 2 + k
        self.own, self.other = at(h, x, k), at(1 - h, x, k)
        self.near = {d: [at(h, x + d, k), at(1 - h, x + d, k)] for d in (-1, 1, 2)}
        self.theirs = [at(g, jnp.int32(p), 1 - k) for g in range(2) for p in range(4)]

    def to_pair(self):
        for target in (self.z_peer, self.right, self.left, self.mate):
            self.whole(self.own, target)

    def to_ring(self):
        self.got(self.other, self.z_peer)
        for target in (self.right, self.left, self.mate):
            self.whole(self.other, target)

    def forward(self):
        super().forward()
        for slot in self.near[-1] + self.near[1]:
            self.whole(slot, self.mate)

    def to_mate(self):
        for slot in self.near[2]:
            self.got_part(slot, 0, self.left)
            self.got_part(slot, 1, self.right)
            self.whole(slot, self.mate)

    def finish(self):
        for slot in self.theirs:
            self.got(slot, self.mate)


class ColGather(Gather):
    def __init__(self, mover, view, half, sem, places):
        super().__init__(mover, view, half, sem, lambda e: e < 12)
        (y, s), (self.z_peer, self.right, self.left) = places
        at = lambda y, s: lax.rem(y + 4, 4) * 2 + s
        self.own = [at(y, s), at(y, s) + 8]
        self.other = [at(y, 1 - s), at(y, 1 - s) + 8]
        self.near = {
            d: [at(y + d, t) + e for t in range(2) for e in (0, 8)] for d in (-1, 1, 2)
        }

    def to_pair(self):
        for slot in self.own:
            for target in (self.z_peer, self.right, self.left):
                self.whole(slot, target)

    def to_ring(self):
        for slot in self.other:
            self.got(slot, self.z_peer)
            for target in (self.right, self.left):
                self.whole(slot, target)

    def finish(self):
        for slot in self.near[2]:
            self.got_part(slot, 0, self.left)
            self.got_part(slot, 1, self.right)


def factor128(a):
    full = (8, 128)
    rows = lax.broadcasted_iota(jnp.int32, full, 0)
    lanes = lax.broadcasted_iota(jnp.int32, full, 1)
    strips = [a[8 * g : 8 * g + 8, :] for g in range(16)]
    units = [jnp.where(lanes == rows + 8 * g, 1.0, 0.0).astype(F32) for g in range(16)]
    uppers, inverses = [], []
    for g in range(16):
        s, t = strips[g], units[g]
        cols = [jnp.broadcast_to(s[:, 8 * g + m : 8 * g + m + 1], full) for m in range(8)]
        e = [[jnp.broadcast_to(cols[m][i : i + 1, :], full) for m in range(i + 1)] for i in range(8)]
        z = [jnp.broadcast_to(s[i : i + 1, :], full) for i in range(8)]
        y = [jnp.broadcast_to(t[i : i + 1, :], full) for i in range(8)]
        l = [[None] * 8 for _ in range(8)]
        r = []
        for k in range(8):
            r.append(pl.reciprocal(e[k][k], approx=True))
            for i in range(k + 1, 8):
                l[i][k] = e[i][k] * r[k]
            for j in range(k + 1, 8):
                for i in range(j, 8):
                    e[i][j] = e[i][j] - l[i][k] * e[j][k]
            for i in range(k + 1, 8):
                z[i] = z[i] - l[i][k] * z[k]
                y[i] = y[i] - l[i][k] * y[k]
        u = jnp.zeros(full, F32)
        w = jnp.zeros(full, F32)
        for i in range(8):
            q = lax.rsqrt(e[i][i])
            u = jnp.where(rows == i, z[i] * q, u)
            w = jnp.where(rows == i, y[i] * q, w)
        uppers.append(jnp.where(lanes >= rows + 8 * g, u, 0.0))
        inverses.append(w)
        top = g // 4 * 4 + 4
        if g + 1 < top:
            v, x = [None] * 8, [None] * 8
            for i in reversed(range(8)):
                v[i], x[i] = z[i] * r[i], y[i] * r[i]
                for m in range(i + 1, 8):
                    v[i] = v[i] - l[m][i] * v[m]
                    x[i] = x[i] - l[m][i] * x[m]
            for h in range(g + 1, top):
                c = [
                    jnp.broadcast_to(strips[h][:, 8 * g + m : 8 * g + m + 1], full)
                    for m in range(8)
                ]
                p = [c[m] * v[m] for m in range(8)]
                o = [c[m] * x[m] for m in range(8)]
                while len(p) > 1:
                    p = [p[2 * i] + p[2 * i + 1] for i in range(len(p) // 2)]
                    o = [o[2 * i] + o[2 * i + 1] for i in range(len(o) // 2)]
                strips[h] = strips[h] - p[0]
                units[h] = units[h] - o[0]
        elif top < 16:
            u = jnp.concatenate(uppers[top - 4 : top], 0)
            w = jnp.concatenate(inverses[top - 4 : top], 0)
            product = lax.dot_general(
                u,
                jnp.concatenate([u, w], 1),
                (((0,), (0,)), ((), ())),
                precision=HIGHEST,
                preferred_element_type=F32,
            )
            for h in range(top, 16):
                strips[h] = strips[h] - product[8 * h : 8 * h + 8, :128]
                units[h] = units[h] - product[8 * h : 8 * h + 8, 128:]
    return jnp.concatenate(uppers, 0), jnp.concatenate(inverses, 0)


def dot(a, b, dims=NN):
    return lax.dot_general(a, b, dims, precision=HIGHEST, preferred_element_type=jnp.float32)


def inverse_at(dinv, J):
    a, b, c, d = (dinv[J * 4 + i] for i in range(4))
    return jnp.concatenate([jnp.concatenate([a, b], 1), jnp.concatenate([c, d], 1)], 0)


def chol_loop(pv, dinv, between, nsteps=6):
    @pl.loop(0, nsteps)
    def _(J):
        ca = pl.multiple_of(J * 256, 256)
        cb = pl.multiple_of(J * 256 + 128, 128)
        for step, action in enumerate(between):
            pl.when(J == step)(action)
        ua, ia = factor128(pv[pl.ds(ca, 128), pl.ds(ca, 128)])
        la = ua.T
        pv[pl.ds(ca, 128), pl.ds(ca, 128)] = la
        wb = dot(pv[pl.ds(cb, 128), pl.ds(ca, 128)], ia, NT)
        pv[pl.ds(cb, 128), pl.ds(ca, 128)] = wb
        ub, ib = factor128(pv[pl.ds(cb, 128), pl.ds(cb, 128)] - dot(wb, wb, NT))
        pv[pl.ds(cb, 128), pl.ds(cb, 128)] = ub.T
        off = -dot(ib, dot(wb, ia))
        dinv[J * 4] = ia
        dinv[J * 4 + 1] = jnp.zeros((128, 128), F32)
        dinv[J * 4 + 2] = off
        dinv[J * 4 + 3] = ib
        inv = inverse_at(dinv, J)
        @pl.loop(J + 1, nsteps)
        def _(R):
            ro = pl.multiple_of(R * 256, 256)
            pv[pl.ds(ro, 256), pl.ds(ca, 256)] = dot(pv[pl.ds(ro, 256), pl.ds(ca, 256)], inv, NT)
        @pl.loop(J + 1, nsteps)
        def _(I):
            io = pl.multiple_of(I * 256, 256)
            wi = pv[pl.ds(io, 256), pl.ds(ca, 256)]
            @pl.loop(I, nsteps)
            def _(R):
                ro = pl.multiple_of(R * 256, 256)
                pv[pl.ds(ro, 256), pl.ds(io, 256)] -= dot(pv[pl.ds(ro, 256), pl.ds(ca, 256)], wi, NT)


def split(v):
    hi = v.astype(BF16)
    return hi, (v - hi.astype(F32)).astype(BF16)


def dot3(ah, al, bh, bl):
    a = jnp.concatenate([ah, ah, al], 1)
    b = jnp.concatenate([bh, bl, bh], 0)
    return lax.dot_general(a, b, NN, preferred_element_type=F32)


def solve_steps(g1, g2, l_ref, d_ref, xh, xl, yh, yl):
    for i in range(6):
        dh, dl = split(inverse_at(d_ref, i))
        lh, ll = split(l_ref[256 * i : 256 * i + 256, : 256 * i]) if i else (None, None)
        span = slice(256 * i, 256 * i + 256)
        blocks = slice(2 * i, 2 * i + 2)

        @pl.loop(0, 2)
        def _(n):
            cols = pl.ds(pl.multiple_of(n * 768, 256), 768)
            rhs = g1[blocks, :, cols].reshape(256, 768)
            if i:
                rhs = rhs - dot3(lh, ll, xh[: 256 * i, cols], xl[: 256 * i, cols])
            hi, lo = split(dot3(dh, dl, *split(rhs)))
            xh[span, cols] = hi
            xl[span, cols] = lo

        rhs = g2[blocks].reshape(256, 768)
        if i:
            rhs = rhs - dot3(lh, ll, *split(g2[: 2 * i].reshape(256 * i, 768)))
        g2[blocks] = dot3(dh, dl, *split(rhs)).reshape(2, 128, 768)
    for l in range(6):
        rows = slice(128 * l, 128 * l + 128)
        hi, lo = split(g2[:, :, rows].reshape(1536, 128).T)
        yh[rows, :] = hi
        yl[rows, :] = lo

    @pl.loop(0, 6)
    def _(t):
        rows = pl.ds(pl.multiple_of(t // 2 * 256, 256), 256)
        cols = pl.ds(pl.multiple_of(lax.rem(t, 2) * 768, 256), 768)
        l_ref[rows, cols] = dot3(yh[rows, :], yl[rows, :], xh[:, cols], xl[:, cols])


def place_steps(row, col, out_ref, yh, yl):
    @pl.when(row < 12)
    def _():
        out_ref[0:128, :] = jnp.zeros((128, 1536), F32)

    def place(block, m):
        lanes = pl.ds(pl.multiple_of(block * 128, 128), 128)
        values = yh[:, lanes].astype(F32) + yl[:, lanes].astype(F32)
        i = lax.broadcasted_iota(jnp.int32, values.shape, 0)
        j = lax.broadcasted_iota(jnp.int32, values.shape, 1)
        matrix_row = (i // 128 * 16 + row) * 128 + lax.rem(i, 128)
        out_ref[:, 128 * m : 128 * m + 128] = jnp.where(
            matrix_row >= block * 128 + j, values, 0.0
        )

    place(col, 0)

    @pl.when(col < 4)
    def _():
        place(col + 8, 1)


def panel_kernel(
    maps_ref,
    front_ref,
    child_ref,
    out_ref,
    arrived,
    g1,
    g2,
    pv,
    dinv,
    xh,
    xl,
    yh,
    yl,
    load_sem,
    block_send,
    first_sem,
    block_sem,
    early_sem,
    send_sem,
    head_sem,
    turn_sem,
    g1_sem,
    g2_sem,
    pv_sem,
):
    first = dinv.at[pl.ds(0, 16)]
    row, col = lax.axis_index("row"), lax.axis_index("col")
    h, x, k = row // 8, lax.rem(row, 8) // 2, lax.rem(row, 2)
    y, s = col // 2, lax.rem(col, 2)
    z = s * 2 + h
    me = row * 8 + col
    at_x = lambda p: h * 8 + lax.rem(p + 4, 4) * 2 + k
    at_y = lambda p: lax.rem(p + 4, 4) * 2 + s
    row_peers = [
        ((1 - h) * 8 + x * 2 + k, col),
        (at_x(x + 1), col),
        (at_x(x - 1), col),
        (h * 8 + x * 2 + 1 - k, col),
    ]
    col_peers = [(row, y * 2 + 1 - s), (row, at_y(y + 1)), (row, at_y(y - 1))]

    def block_at(i):
        return pl.ds(pl.multiple_of(i * 128, 128), 128)

    for i in range(8):
        for j in range(8):
            pltpu.make_async_copy(
                child_ref.at[pl.ds(128 * i, 128), pl.ds(128 * j, 128)],
                arrived.at[i * 8 + j],
                load_sem,
            ).start()
    pltpu.make_async_copy(arrived.at[pl.ds(0, 64)], arrived.at[pl.ds(64, 64)], load_sem).wait()
    run = lax.rem(row, 8)
    row_start = lax.rem(maps_ref[h, 8 * run], 8)
    col_start = lax.rem(maps_ref[h, 8 * col], 8)

    @pl.loop(0, 8)
    def _(r):
        i = lax.rem(r - row_start + 8, 8)

        @pl.loop(0, 8)
        def _(c):
            j = lax.rem(c - col_start + 8, 8)
            p = r * 8 + c
            out_ref[block_at(p // 12), block_at(lax.rem(p, 12))] = arrived[i * 8 + j]

    def packed(r, c):
        p = r * 8 + c
        return out_ref.at[block_at(p // 12), block_at(lax.rem(p, 12))]

    arrived[me] = packed(run, col)[...]

    def peer(o):
        o = lax.rem(o * 37, 128)
        to_x = lax.rem(x + lax.rem(o, 4), 4)
        to_y = lax.rem(y + lax.rem(o // 4, 4), 4)
        to_z = lax.rem(z + lax.rem(o // 16, 4), 4)
        to_k = lax.rem(k + o // 64, 2)
        return lax.rem(to_z, 2) * 8 + to_x * 2 + to_k, to_y * 2 + to_z // 2

    barrier = pltpu.get_barrier_semaphore()

    @pl.loop(1, 128)
    def _(o):
        pl.semaphore_signal(barrier, inc=1, device_id=peer(o), device_id_type=MESH)

    pl.semaphore_wait(barrier, 127)

    def is_first(to_row):
        return ((run == 0) & (to_row < 8)) | ((run == 1) & (to_row >= 8) & (to_row < 12))

    def send_first(base, count):
        @pl.loop(0, 8 * count)
        def _(t):
            i = lax.rem(t, count)
            to_row, to_col = base + i, lax.rem(col + t // count + i, 8)

            @pl.when((to_row != row) | (to_col != col))
            def _():
                pltpu.make_async_remote_copy(
                    src_ref=packed(lax.rem(to_row, 8), to_col),
                    dst_ref=first.at[h * 8 + col],
                    send_sem=block_send,
                    recv_sem=first_sem,
                    device_id=(to_row, to_col),
                    device_id_type=MESH,
                ).start()

            @pl.when((to_row == row) & (to_col == col))
            def _():
                first[h * 8 + col] = packed(lax.rem(to_row, 8), to_col)[...]

    pl.when(run == 0)(lambda: send_first(0, 8))
    pl.when(run == 1)(lambda: send_first(8, 4))

    def send_blocks(start, stop, step):
        @pl.loop(start, stop)
        def _(i):
            to_row, to_col = peer(step(i))

            @pl.when(jnp.logical_not(is_first(to_row)))
            def _():
                pltpu.make_async_remote_copy(
                    src_ref=packed(lax.rem(to_row, 8), to_col),
                    dst_ref=arrived.at[me],
                    send_sem=block_send,
                    recv_sem=block_sem.at[row],
                    device_id=(to_row, to_col),
                    device_id_type=MESH,
                ).start()

    def await_blocks(ref, sem, send=False):
        copy = pltpu.make_async_remote_copy(
            src_ref=ref,
            dst_ref=ref,
            send_sem=sem,
            recv_sem=sem,
            device_id=row_peers[0],
            device_id_type=MESH,
        )
        copy.wait_send() if send else copy.wait_recv()

    mine = jnp.where(row < 8, 0, 1)
    own_first = (row < 12) & (run == mine)

    @pl.when((row < 12) & own_first)
    def _():
        await_blocks(first.at[pl.ds(0, 15)], first_sem)

    @pl.when((row < 12) & jnp.logical_not(own_first))
    def _():
        await_blocks(first, first_sem)

    @pl.when((row >= 8) & (row < 12))
    def _():
        @pl.loop(0, 16)
        def _(i):
            arrived[(i // 8 * 8 + 1) * 8 + lax.rem(i, 8)] = first[i]

    early, mover = Mover(early_sem), Mover(send_sem)

    @pl.when(row < 12)
    def _():
        found = [run_of(maps_ref, member, row)[1] for member in range(2)]

        @pl.loop(0, 12)
        def _(m):
            total = front_ref[0:128, block_at(m)]
            for member in range(2):
                other, also = run_of(maps_ref, member, m * 8 + col)
                total = total + first[member * 8 + other] * (found[member] * also).astype(F32)
            g1[row, :, block_at(m)] = total

    def pivot_block(b):
        return pv.at[block_at(row), block_at(b)]

    for j in range(2):
        block = col + 8 * j

        @pl.when((row < 12) & (block <= row))
        def _():
            pv[block_at(row), block_at(block)] = g1[row, :, 128 * j : 128 * j + 128]

        for o in range(1, 8):
            early.send(
                lambda b=block: (row < 12) & (b <= row),
                lambda b=block: pivot_block(b),
                lambda b=block: head_sem.at[b],
                (row, lax.rem(col + o, 8)),
            )

    own_turn = (row < 12) & (run == col)

    def turn():
        for j in range(2):
            target = (col + 8 * j, run)
            for l in range(6):
                mover.send(
                    lambda t=target: (row < 12) & ((t[0] != row) | (t[1] != col)),
                    lambda j=j, l=l: g1.at[row, :, pl.ds(128 * (2 * l + j), 128)],
                    lambda: turn_sem.at[row],
                    target,
                    lambda l=l: g2.at[row, :, pl.ds(128 * l, 128)],
                )

        @pl.when(own_turn)
        def _():
            for l in range(6):
                g2[row, :, 128 * l : 128 * l + 128] = g1[row, :, block_at(2 * l + h)]

    def turned():
        for slot in (col, col + 8):
            held = lax.rem(slot, 12)
            await_copy(
                (slot < 12) & jnp.logical_not(own_turn & (row == slot)),
                g2.at[held],
                turn_sem.at[slot],
                (held, lax.rem(row, 8)),
            )

    row_places = ((h, x, k), row_peers)
    wide = pl.ds(128, 1408)
    rows1 = RowGather(
        mover,
        lambda q: g1.at[q, :, wide],
        lambda q, i: g1.at[q, pl.ds(64 * i, 64), wide],
        g1_sem,
        lambda q: q < 12,
        row_places,
    )
    cols2 = ColGather(
        mover,
        lambda e: g2.at[e],
        lambda e, i: g2.at[e, pl.ds(64 * i, 64), :],
        g2_sem,
        ((y, s), col_peers),
    )
    pivots = [
        RowGather(
            early,
            lambda q, t=t: pv.at[block_at(q), pl.ds(512 * t, 512)],
            lambda q, i, t=t: pv.at[
                pl.ds(pl.multiple_of(q * 128 + 64 * i, 64), 64), pl.ds(512 * t, 512)
            ],
            pv_sem.at[t],
            lambda q, t=t: (q < 12) & (q >= 4 * t),
            row_places,
        )
        for t in range(3)
    ]
    for b in range(12):
        await_copy(
            (row < 12) & (b <= row) & (col != b % 8), pivot_block(b), head_sem.at[b], (row, b % 8)
        )
    for p in pivots:
        p.to_pair()
    send_blocks(1, 32, lambda i: 4 * i)
    for p in pivots:
        p.to_ring()
    for p in pivots:
        p.forward()
    turn()
    rows1.to_pair()
    for p in pivots:
        p.to_mate()
    for p in pivots:
        p.finish()
    rows1.to_ring()
    early.finish()

    def send_others(start, stop):
        send_blocks(start, stop, lambda i: i // 3 * 4 + 1 + lax.rem(i, 3))

    def step0():
        turned()
        cols2.to_pair()
        send_others(0, 8)

    def step1():
        cols2.to_ring()
        rows1.forward()
        send_others(8, 24)

    def step2():
        cols2.forward()
        rows1.to_mate()
        send_others(24, 48)

    def step3():
        send_others(48, 72)

    def step4():
        send_others(72, 96)

    chol_loop(pv, dinv, [step0, step1, step2, step3, step4])
    cols2.finish()
    rows1.finish()
    mover.finish()
    solve_steps(g1, g2, pv, dinv, xh, xl, yh, yl)

    for q in range(16):
        early_row = (row < 12) & (lax.rem(jnp.int32(q), 8) == mine)
        wanted = jnp.logical_not(early_row)

        @pl.when(wanted & (row == q))
        def _():
            await_blocks(arrived.at[pl.ds(0, 7)], block_sem.at[q])

        @pl.when(wanted & (row != q))
        def _():
            await_blocks(arrived.at[pl.ds(0, 8)], block_sem.at[q])

    await_blocks(arrived.at[pl.ds(0, 127)], block_send, True)

    @pl.loop(0, 6)
    def _(l):
        runs = [run_of(maps_ref, member, l * 16 + row) for member in range(2)]

        @pl.loop(0, 12)
        def _(m):
            total = front_ref[block_at(l), block_at(m)] - pv[block_at(l), block_at(m)]
            for member in range(2):
                mine, found = runs[member]
                other, also = run_of(maps_ref, member, m * 8 + col)
                update = arrived[(member * 8 + mine) * 8 + other]
                total = total + update * (found * also).astype(F32)
            out_ref[block_at(l), block_at(m)] = total

    place_steps(row, col, out_ref, yh, yl)


def panel(maps, front, children):
    return pl.pallas_call(
        panel_kernel,
        out_shape=jax.ShapeDtypeStruct(front.shape, F32),
        in_specs=[SMEM, VMEM, pl.BlockSpec(memory_space=pl.ANY)],
        out_specs=VMEM,
        scratch_shapes=[
            pltpu.VMEM((128, 128, 128), F32),
            pltpu.VMEM((12, 128, 1536), F32),
            pltpu.VMEM((12, 128, 768), F32),
            pltpu.VMEM((1536, 1536), F32),
            pltpu.VMEM((24, 128, 128), F32),
            pltpu.VMEM((1536, 1536), BF16),
            pltpu.VMEM((1536, 1536), BF16),
            pltpu.VMEM((768, 1536), BF16),
            pltpu.VMEM((768, 1536), BF16),
            pltpu.SemaphoreType.DMA,
            pltpu.SemaphoreType.DMA,
            pltpu.SemaphoreType.DMA,
            pltpu.SemaphoreType.DMA((16,)),
            pltpu.SemaphoreType.DMA((96,)),
            pltpu.SemaphoreType.DMA((64,)),
            pltpu.SemaphoreType.DMA((16,)),
            pltpu.SemaphoreType.DMA((16,)),
            pltpu.SemaphoreType.DMA((2, 16)),
            pltpu.SemaphoreType.DMA((2, 16)),
            pltpu.SemaphoreType.DMA((3, 2, 16)),
        ],
        compiler_params=pltpu.CompilerParams(
            collective_id=0, has_side_effects=True, vmem_limit_bytes=63 * 2**20
        ),
        name="panel",
    )(maps, front, children)


def shards(front, children, maps):
    return panel(maps, front, children)


def solution(mesh):
    in_specs = (P("row", "col"), P("row", "col"), P())
    out_specs = P("row", "col")
    return jax.shard_map(shards, mesh=mesh, in_specs=in_specs, out_specs=out_specs, check_vma=False)
```

```python
import jax
import jax.numpy as jnp
from jax import lax
from jax.experimental import pallas as pl
from jax.experimental.pallas import tpu as pltpu
from jax.sharding import PartitionSpec as P

HIGHEST = lax.Precision.HIGHEST
MESH = pl.DeviceIdType.MESH
F32 = jnp.float32
BF16 = jnp.bfloat16
NN = (((1,), (0,)), ((), ()))
NT = (((1,), (1,)), ((), ()))
VMEM = pl.BlockSpec(memory_space=pltpu.VMEM)
SMEM = pl.BlockSpec(memory_space=pltpu.SMEM)
VMEM_LIMIT = 60 * 2**20


def run_of(maps_ref, member, block):
    run = jnp.int32(0)
    found = jnp.int32(0)
    for j in range(8):
        start = maps_ref[member, 8 * j]
        hit = ((block >= start) & (block < start + 8)).astype(jnp.int32)
        run = jnp.maximum(run, hit * j)
        found = jnp.maximum(found, hit)
    return run, found


class Mover:
    def __init__(self, send_sem):
        self.send_sem = send_sem
        self.sent = []

    def send(self, guard, ref, recv_sem, target, to=None):
        number = len(self.sent)

        def copy():
            return pltpu.make_async_remote_copy(
                src_ref=ref(),
                dst_ref=(to or ref)(),
                send_sem=self.send_sem.at[number],
                recv_sem=recv_sem(),
                device_id=target,
                device_id_type=MESH,
            )

        self.sent.append((guard, copy))
        pl.when(guard())(lambda: copy().start())

    def finish(self):
        for guard, copy in self.sent:
            pl.when(guard())(lambda copy=copy: copy().wait_send())


def await_copy(guard, dst, recv_sem, peer):
    @pl.when(guard)
    def _():
        pltpu.make_async_remote_copy(
            src_ref=dst,
            dst_ref=dst,
            send_sem=recv_sem,
            recv_sem=recv_sem,
            device_id=peer,
            device_id_type=MESH,
        ).wait_recv()


class Gather:
    def __init__(self, mover, view, half, sem, needed):
        self.mover, self.view, self.half, self.sem, self.needed = mover, view, half, sem, needed

    def whole(self, slot, target):
        self.mover.send(
            lambda: self.needed(slot), lambda: self.view(slot), lambda: self.sem.at[0, slot], target
        )

    def part(self, slot, i, target):
        self.mover.send(
            lambda: self.needed(slot),
            lambda: self.half(slot, i),
            lambda: self.sem.at[i, slot],
            target,
        )

    def got(self, slot, peer):
        await_copy(self.needed(slot), self.view(slot), self.sem.at[0, slot], peer)

    def got_part(self, slot, i, peer):
        await_copy(self.needed(slot), self.half(slot, i), self.sem.at[i, slot], peer)

    def forward(self):
        for slot in self.near[-1]:
            self.got(slot, self.left)
            self.part(slot, 0, self.right)
        for slot in self.near[1]:
            self.got(slot, self.right)
            self.part(slot, 1, self.left)


class RowGather(Gather):
    def __init__(self, mover, view, half, sem, needed, places):
        super().__init__(mover, view, half, sem, needed)
        (h, x, k), (self.z_peer, self.right, self.left, self.mate) = places
        at = lambda h, x, k: h * 8 + lax.rem(x + 4, 4) * 2 + k
        self.own, self.other = at(h, x, k), at(1 - h, x, k)
        self.near = {d: [at(h, x + d, k), at(1 - h, x + d, k)] for d in (-1, 1, 2)}
        self.theirs = [at(g, jnp.int32(p), 1 - k) for g in range(2) for p in range(4)]

    def to_pair(self):
        for target in (self.z_peer, self.right, self.left, self.mate):
            self.whole(self.own, target)

    def to_ring(self):
        self.got(self.other, self.z_peer)
        for target in (self.right, self.left, self.mate):
            self.whole(self.other, target)

    def forward(self):
        super().forward()
        for slot in self.near[-1] + self.near[1]:
            self.whole(slot, self.mate)

    def to_mate(self):
        for slot in self.near[2]:
            self.got_part(slot, 0, self.left)
            self.got_part(slot, 1, self.right)
            self.whole(slot, self.mate)

    def finish(self):
        for slot in self.theirs:
            self.got(slot, self.mate)


class ColGather(Gather):
    def __init__(self, mover, view, half, sem, places):
        super().__init__(mover, view, half, sem, lambda e: e < 12)
        (y, s), (self.z_peer, self.right, self.left) = places
        at = lambda y, s: lax.rem(y + 4, 4) * 2 + s
        self.own = [at(y, s), at(y, s) + 8]
        self.other = [at(y, 1 - s), at(y, 1 - s) + 8]
        self.near = {
            d: [at(y + d, t) + e for t in range(2) for e in (0, 8)] for d in (-1, 1, 2)
        }

    def to_pair(self):
        for slot in self.own:
            for target in (self.z_peer, self.right, self.left):
                self.whole(slot, target)

    def to_ring(self):
        for slot in self.other:
            self.got(slot, self.z_peer)
            for target in (self.right, self.left):
                self.whole(slot, target)

    def finish(self):
        for slot in self.near[2]:
            self.got_part(slot, 0, self.left)
            self.got_part(slot, 1, self.right)


def factor128(a):
    full = (8, 128)
    rows = lax.broadcasted_iota(jnp.int32, full, 0)
    lanes = lax.broadcasted_iota(jnp.int32, full, 1)
    strips = [a[8 * g : 8 * g + 8, :] for g in range(16)]
    units = [jnp.where(lanes == rows + 8 * g, 1.0, 0.0).astype(F32) for g in range(16)]
    uppers, inverses = [], []
    for g in range(16):
        s, t = strips[g], units[g]
        cols = [jnp.broadcast_to(s[:, 8 * g + m : 8 * g + m + 1], full) for m in range(8)]
        e = [[jnp.broadcast_to(cols[m][i : i + 1, :], full) for m in range(i + 1)] for i in range(8)]
        z = [jnp.broadcast_to(s[i : i + 1, :], full) for i in range(8)]
        y = [jnp.broadcast_to(t[i : i + 1, :], full) for i in range(8)]
        l = [[None] * 8 for _ in range(8)]
        r = []
        for k in range(8):
            r.append(pl.reciprocal(e[k][k], approx=True))
            for i in range(k + 1, 8):
                l[i][k] = e[i][k] * r[k]
            for j in range(k + 1, 8):
                for i in range(j, 8):
                    e[i][j] = e[i][j] - l[i][k] * e[j][k]
            for i in range(k + 1, 8):
                z[i] = z[i] - l[i][k] * z[k]
                y[i] = y[i] - l[i][k] * y[k]
        u = jnp.zeros(full, F32)
        w = jnp.zeros(full, F32)
        for i in range(8):
            q = lax.rsqrt(e[i][i])
            u = jnp.where(rows == i, z[i] * q, u)
            w = jnp.where(rows == i, y[i] * q, w)
        uppers.append(jnp.where(lanes >= rows + 8 * g, u, 0.0))
        inverses.append(w)
        top = g // 4 * 4 + 4
        if g + 1 < top:
            v, x = [None] * 8, [None] * 8
            for i in reversed(range(8)):
                v[i], x[i] = z[i] * r[i], y[i] * r[i]
                for m in range(i + 1, 8):
                    v[i] = v[i] - l[m][i] * v[m]
                    x[i] = x[i] - l[m][i] * x[m]
            for h in range(g + 1, top):
                c = [
                    jnp.broadcast_to(strips[h][:, 8 * g + m : 8 * g + m + 1], full)
                    for m in range(8)
                ]
                p = [c[m] * v[m] for m in range(8)]
                o = [c[m] * x[m] for m in range(8)]
                while len(p) > 1:
                    p = [p[2 * i] + p[2 * i + 1] for i in range(len(p) // 2)]
                    o = [o[2 * i] + o[2 * i + 1] for i in range(len(o) // 2)]
                strips[h] = strips[h] - p[0]
                units[h] = units[h] - o[0]
        elif top < 16:
            u = jnp.concatenate(uppers[top - 4 : top], 0)
            w = jnp.concatenate(inverses[top - 4 : top], 0)
            product = lax.dot_general(
                u,
                jnp.concatenate([u, w], 1),
                (((0,), (0,)), ((), ())),
                precision=HIGHEST,
                preferred_element_type=F32,
            )
            for h in range(top, 16):
                strips[h] = strips[h] - product[8 * h : 8 * h + 8, :128]
                units[h] = units[h] - product[8 * h : 8 * h + 8, 128:]
    return jnp.concatenate(uppers, 0), jnp.concatenate(inverses, 0)


def dot(a, b, dims=NN):
    return lax.dot_general(a, b, dims, precision=HIGHEST, preferred_element_type=jnp.float32)


def inverse_at(dinv, J):
    a, b, c, d = (dinv[J * 4 + i] for i in range(4))
    return jnp.concatenate([jnp.concatenate([a, b], 1), jnp.concatenate([c, d], 1)], 0)


def chol_loop(pv, dinv, beside, nsteps=6):
    @pl.loop(0, nsteps)
    def _(J):
        ca = pl.multiple_of(J * 256, 256)
        cb = pl.multiple_of(J * 256 + 128, 128)
        for step, action in beside.items():
            if step % 2 == 0:
                pl.when(J == step // 2)(action)
        ua, ia = factor128(pv[pl.ds(ca, 128), pl.ds(ca, 128)])
        la = ua.T
        pv[pl.ds(ca, 128), pl.ds(ca, 128)] = la
        wb = dot(pv[pl.ds(cb, 128), pl.ds(ca, 128)], ia, NT)
        pv[pl.ds(cb, 128), pl.ds(ca, 128)] = wb
        for step, action in beside.items():
            if step % 2 == 1:
                pl.when(J == step // 2)(action)
        ub, ib = factor128(pv[pl.ds(cb, 128), pl.ds(cb, 128)] - dot(wb, wb, NT))
        pv[pl.ds(cb, 128), pl.ds(cb, 128)] = ub.T
        off = -dot(ib, dot(wb, ia))
        dinv[J * 4] = ia
        dinv[J * 4 + 1] = jnp.zeros((128, 128), F32)
        dinv[J * 4 + 2] = off
        dinv[J * 4 + 3] = ib
        inv = inverse_at(dinv, J)
        @pl.loop(J + 1, nsteps)
        def _(R):
            ro = pl.multiple_of(R * 256, 256)
            pv[pl.ds(ro, 256), pl.ds(ca, 256)] = dot(pv[pl.ds(ro, 256), pl.ds(ca, 256)], inv, NT)
        @pl.loop(J + 1, nsteps)
        def _(I):
            io = pl.multiple_of(I * 256, 256)
            wi = pv[pl.ds(io, 256), pl.ds(ca, 256)]
            @pl.loop(I, nsteps)
            def _(R):
                ro = pl.multiple_of(R * 256, 256)
                pv[pl.ds(ro, 256), pl.ds(io, 256)] -= dot(pv[pl.ds(ro, 256), pl.ds(ca, 256)], wi, NT)


def split(v):
    hi = v.astype(BF16)
    return hi, (v - hi.astype(F32)).astype(BF16)


def dot3(ah, al, bh, bl):
    a = jnp.concatenate([ah, ah, al], 1)
    b = jnp.concatenate([bh, bl, bh], 0)
    return lax.dot_general(a, b, NN, preferred_element_type=F32)


def solve_x(g1, l_ref, d_ref, xh, xl):
    for i in range(6):
        dh, dl = split(inverse_at(d_ref, i))
        lh, ll = split(l_ref[256 * i : 256 * i + 256, : 256 * i]) if i else (None, None)

        @pl.loop(0, 2)
        def _(n):
            cols = pl.ds(pl.multiple_of(n * 768, 256), 768)
            rhs = g1[2 * i : 2 * i + 2, :, cols].reshape(256, 768)
            if i:
                rhs = rhs - dot3(lh, ll, xh[: 256 * i, cols], xl[: 256 * i, cols])
            hi, lo = split(dot3(dh, dl, *split(rhs)))
            xh[256 * i : 256 * i + 256, cols] = hi
            xl[256 * i : 256 * i + 256, cols] = lo


def solve_y(g2, l_ref, d_ref, yh, yl):
    for i in range(6):
        dh, dl = split(inverse_at(d_ref, i))
        lh, ll = split(l_ref[256 * i : 256 * i + 256, : 256 * i]) if i else (None, None)

        @pl.loop(0, 3)
        def _(n):
            cols = pl.ds(pl.multiple_of(n * 256, 256), 256)
            rhs = g2[2 * i : 2 * i + 2, :, cols].reshape(256, 256)
            if i:
                rhs = rhs - dot3(lh, ll, *split(g2[: 2 * i, :, cols].reshape(256 * i, 256)))
            g2[2 * i : 2 * i + 2, :, cols] = dot3(dh, dl, *split(rhs)).reshape(2, 128, 256)

    for l in range(6):
        rows = slice(128 * l, 128 * l + 128)
        hi, lo = split(g2[:, :, rows].reshape(1536, 128).T)
        yh[rows, :] = hi
        yl[rows, :] = lo


def update_steps(l_ref, xh, xl, yh, yl):
    @pl.loop(0, 6)
    def _(t):
        rows = pl.ds(pl.multiple_of(t // 2 * 256, 256), 256)
        cols = pl.ds(pl.multiple_of(lax.rem(t, 2) * 768, 256), 768)
        l_ref[rows, cols] = dot3(yh[rows, :], yl[rows, :], xh[:, cols], xl[:, cols])


def place_steps(row, col, out_ref, yh, yl):
    @pl.when(row < 12)
    def _():
        out_ref[0:128, :] = jnp.zeros((128, 1536), F32)

    def place(block, m):
        lanes = pl.ds(pl.multiple_of(block * 128, 128), 128)
        values = yh[:, lanes].astype(F32) + yl[:, lanes].astype(F32)
        i = lax.broadcasted_iota(jnp.int32, values.shape, 0)
        j = lax.broadcasted_iota(jnp.int32, values.shape, 1)
        matrix_row = (i // 128 * 16 + row) * 128 + lax.rem(i, 128)
        out_ref[:, 128 * m : 128 * m + 128] = jnp.where(
            matrix_row >= block * 128 + j, values, 0.0
        )

    place(col, 0)

    @pl.when(col < 4)
    def _():
        place(col + 8, 1)


def panel_kernel(
    maps_ref,
    front_ref,
    child_ref,
    out_ref,
    mid,
    arrived,
    g1,
    g2,
    pv,
    dinv,
    xh,
    xl,
    yh,
    yl,
    load_sem,
    mid_send,
    mid_sem,
    block_send,
    first_sem,
    block_sem,
    early_sem,
    send_sem,
    head_sem,
    turn_sem,
    g1_sem,
    g2_sem,
    pv_sem,
):
    first = dinv.at[pl.ds(0, 16)]
    row, col = lax.axis_index("row"), lax.axis_index("col")
    h, x, k = row // 8, lax.rem(row, 8) // 2, lax.rem(row, 2)
    y, s = col // 2, lax.rem(col, 2)
    z = s * 2 + h
    at_x = lambda p: h * 8 + lax.rem(p + 4, 4) * 2 + k
    at_y = lambda p: lax.rem(p + 4, 4) * 2 + s
    row_peers = [
        ((1 - h) * 8 + x * 2 + k, col),
        (at_x(x + 1), col),
        (at_x(x - 1), col),
        (h * 8 + x * 2 + 1 - k, col),
    ]
    col_peers = [(row, y * 2 + 1 - s), (row, at_y(y + 1)), (row, at_y(y - 1))]

    def block_at(i):
        return pl.ds(pl.multiple_of(i * 128, 128), 128)

    for i in range(8):
        for j in range(8):
            pltpu.make_async_copy(
                child_ref.at[pl.ds(128 * i, 128), pl.ds(128 * j, 128)],
                arrived.at[i * 8 + j],
                load_sem,
            ).start()
    pltpu.make_async_copy(arrived.at[pl.ds(0, 64)], mid, load_sem).wait()
    run = lax.rem(row, 8)
    row_start = lax.rem(maps_ref[h, 8 * run], 8)
    col_start = lax.rem(maps_ref[h, 8 * col], 8)

    @pl.loop(0, 8)
    def _(r):
        i = lax.rem(r - row_start + 8, 8)

        @pl.loop(0, 8)
        def _(c):
            j = lax.rem(c - col_start + 8, 8)
            p = r * 8 + c
            out_ref[block_at(p // 12), block_at(lax.rem(p, 12))] = arrived[i * 8 + j]

    def staged(p):
        return out_ref.at[block_at(p // 12), block_at(lax.rem(p, 12))]

    for j in range(2):
        mid[(run * 4 + y) * 2 + j] = staged(run * 8 + y * 2 + j)[...]

    def peer(o):
        to_x = lax.rem(x + lax.rem(o, 4), 4)
        to_y = lax.rem(y + lax.rem(o // 4, 4), 4)
        to_z = lax.rem(z + lax.rem(o // 16, 4), 4)
        to_k = lax.rem(k + o // 64, 2)
        return lax.rem(to_z, 2) * 8 + to_x * 2 + to_k, to_y * 2 + to_z // 2

    barrier = pltpu.get_barrier_semaphore()

    @pl.loop(1, 128)
    def _(o):
        pl.semaphore_signal(barrier, inc=1, device_id=peer(o), device_id_type=MESH)

    pl.semaphore_wait(barrier, 127)

    @pl.loop(1, 32)
    def _(i):
        o = lax.rem(i * 13, 32)
        to_row, to_col = peer(lax.rem(o, 16) + o // 16 * 64)
        for j in range(2):
            pltpu.make_async_remote_copy(
                src_ref=staged(lax.rem(to_row, 8) * 8 + to_col // 2 * 2 + j),
                dst_ref=mid.at[(run * 4 + y) * 2 + j],
                send_sem=mid_send,
                recv_sem=mid_sem,
                device_id=(to_row, to_col),
                device_id_type=MESH,
            ).start()

    def await_blocks(ref, sem, send=False):
        copy = pltpu.make_async_remote_copy(
            src_ref=ref,
            dst_ref=ref,
            send_sem=sem,
            recv_sem=sem,
            device_id=row_peers[0],
            device_id_type=MESH,
        )
        copy.wait_send() if send else copy.wait_recv()

    await_blocks(mid.at[pl.ds(0, 62)], mid_sem)
    await_blocks(mid.at[pl.ds(0, 62)], mid_send, True)

    def along_z(d):
        to_z = lax.rem(z + d, 4)
        return lax.rem(to_z, 2), to_z // 2

    def stage(l, d):
        to_h, to_s = along_z(d)
        held, found = run_of(maps_ref, h, l * 16 + to_h * 8 + run)
        for j in range(4):
            block = mid[(held * 4 + j) * 2 + to_s] * found.astype(F32)
            if d:
                staged(((d - 1) * 6 + l) * 4 + j)[...] = block
            elif isinstance(l, int):
                first[z * 4 + j] = block
            else:
                arrived[(z * 5 + l - 1) * 4 + j] = block

    def send_staged(l, d, dst, sem):
        to_h, to_s = along_z(d)
        for j in range(4):
            pltpu.make_async_remote_copy(
                src_ref=staged(((d - 1) * 6 + l) * 4 + j),
                dst_ref=dst(j),
                send_sem=block_send,
                recv_sem=sem,
                device_id=(to_h * 8 + run, y * 2 + to_s),
                device_id_type=MESH,
            ).start()

    for d in (1, 3, 2):
        stage(0, d)
        send_staged(0, d, lambda j: first.at[z * 4 + j], first_sem)
    stage(0, 0)

    @pl.loop(1, 6)
    def _(l):
        for d in range(4):
            stage(l, d)

    def send_rest():
        @pl.loop(1, 6)
        def _(l):
            for d in (1, 3, 2):
                send_staged(l, d, lambda j: arrived.at[(z * 5 + l - 1) * 4 + j], block_sem)

    await_blocks(first.at[pl.ds(0, 12)], first_sem)

    early, mover = Mover(early_sem), Mover(send_sem)

    own = jnp.minimum(row, 12)

    def placed(blocks, count, m, total):
        for member in range(2):
            other, found = run_of(maps_ref, member, m * 8 + col)
            update = blocks[(lax.rem(other, 2) * 2 + member) * count + other // 2]
            total = total + update * found.astype(F32)
        return total

    @pl.loop(0, 12)
    def _(m):
        g1[own, :, block_at(m)] = placed(first, 4, m, front_ref[0:128, block_at(m)])

    def pivot_block(b):
        return pv.at[block_at(row), block_at(b)]

    for j in range(2):
        block = col + 8 * j

        @pl.when((row < 12) & (block <= row))
        def _():
            pv[block_at(row), block_at(block)] = g1[row, :, 128 * j : 128 * j + 128]

        for o in range(1, 8):
            early.send(
                lambda b=block: (row < 12) & (b <= row),
                lambda b=block: pivot_block(b),
                lambda b=block: head_sem.at[b],
                (row, lax.rem(col + o, 8)),
            )

    own_turn = (row < 12) & (run == col)

    def turn():
        for j in range(2):
            target = (col + 8 * j, run)
            for l in range(6):
                mover.send(
                    lambda t=target: (row < 12) & ((t[0] != row) | (t[1] != col)),
                    lambda j=j, l=l: g1.at[row, :, pl.ds(128 * (2 * l + j), 128)],
                    lambda: turn_sem.at[row],
                    target,
                    lambda l=l: g2.at[row, :, pl.ds(128 * l, 128)],
                )

        @pl.when(own_turn)
        def _():
            for l in range(6):
                g2[row, :, 128 * l : 128 * l + 128] = g1[row, :, block_at(2 * l + h)]

    def turned():
        for slot in (col, col + 8):
            held = lax.rem(slot, 12)
            await_copy(
                (slot < 12) & jnp.logical_not(own_turn & (row == slot)),
                g2.at[held],
                turn_sem.at[slot],
                (held, lax.rem(row, 8)),
            )

    row_places = ((h, x, k), row_peers)
    wide = pl.ds(128, 1408)
    rows1 = RowGather(
        mover,
        lambda q: g1.at[q, :, wide],
        lambda q, i: g1.at[q, pl.ds(64 * i, 64), wide],
        g1_sem,
        lambda q: q < 12,
        row_places,
    )
    cols2 = ColGather(
        mover,
        lambda e: g2.at[e],
        lambda e, i: g2.at[e, pl.ds(64 * i, 64), :],
        g2_sem,
        ((y, s), col_peers),
    )
    pivots = [
        RowGather(
            early,
            lambda q, t=t: pv.at[block_at(q), pl.ds(512 * t, 512)],
            lambda q, i, t=t: pv.at[
                pl.ds(pl.multiple_of(q * 128 + 64 * i, 64), 64), pl.ds(512 * t, 512)
            ],
            pv_sem.at[t],
            lambda q, t=t: (q < 12) & (q >= 4 * t),
            row_places,
        )
        for t in range(3)
    ]
    for b in range(12):
        await_copy(
            (row < 12) & (b <= row) & (col != b % 8), pivot_block(b), head_sem.at[b], (row, b % 8)
        )
    for p in pivots:
        p.to_pair()
    for p in pivots:
        p.to_ring()
    for p in pivots:
        p.forward()
    turn()
    rows1.to_pair()
    for p in pivots:
        p.to_mate()
    for p in pivots:
        p.finish()
    early.finish()

    def step2():
        rows1.to_ring()
        turned()
        cols2.to_pair()

    def step9():
        cols2.forward()
        rows1.to_mate()

    chol_loop(
        pv,
        dinv,
        {2: step2, 3: send_rest, 5: cols2.to_ring, 6: rows1.forward, 9: step9},
    )
    rows1.finish()
    solve_x(g1, pv, dinv, xh, xl)
    cols2.finish()
    mover.finish()
    solve_y(g2, pv, dinv, yh, yl)
    update_steps(pv, xh, xl, yh, yl)

    await_blocks(arrived.at[pl.ds(0, 60)], block_sem)
    await_blocks(arrived.at[pl.ds(0, 72)], block_send, True)

    @pl.loop(0, 12)
    def _(m):
        out_ref[0:128, block_at(m)] = g1[own, :, block_at(m)] - pv[0:128, block_at(m)]

    @pl.loop(1, 6)
    def _(l):
        @pl.loop(0, 12)
        def _(m):
            total = front_ref[block_at(l), block_at(m)] - pv[block_at(l), block_at(m)]
            for member in range(2):
                other, found = run_of(maps_ref, member, m * 8 + col)
                held = (lax.rem(other, 2) * 2 + member) * 5 + l - 1
                total = total + arrived[held * 4 + other // 2] * found.astype(F32)
            out_ref[block_at(l), block_at(m)] = total

    place_steps(row, col, out_ref, yh, yl)


def panel(maps, front, children):
    return pl.pallas_call(
        panel_kernel,
        out_shape=jax.ShapeDtypeStruct(front.shape, F32),
        in_specs=[SMEM, VMEM, pl.BlockSpec(memory_space=pl.ANY)],
        out_specs=VMEM,
        scratch_shapes=[
            pltpu.VMEM((64, 128, 128), F32),
            pltpu.VMEM((80, 128, 128), F32),
            pltpu.VMEM((13, 128, 1536), F32),
            pltpu.VMEM((12, 128, 768), F32),
            pltpu.VMEM((1536, 1536), F32),
            pltpu.VMEM((24, 128, 128), F32),
            pltpu.VMEM((1536, 1536), BF16),
            pltpu.VMEM((1536, 1536), BF16),
            pltpu.VMEM((768, 1536), BF16),
            pltpu.VMEM((768, 1536), BF16),
            pltpu.SemaphoreType.DMA,
            pltpu.SemaphoreType.DMA,
            pltpu.SemaphoreType.DMA,
            pltpu.SemaphoreType.DMA,
            pltpu.SemaphoreType.DMA,
            pltpu.SemaphoreType.DMA,
            pltpu.SemaphoreType.DMA((96,)),
            pltpu.SemaphoreType.DMA((64,)),
            pltpu.SemaphoreType.DMA((16,)),
            pltpu.SemaphoreType.DMA((16,)),
            pltpu.SemaphoreType.DMA((2, 16)),
            pltpu.SemaphoreType.DMA((2, 16)),
            pltpu.SemaphoreType.DMA((3, 2, 16)),
        ],
        compiler_params=pltpu.CompilerParams(
            collective_id=0, has_side_effects=True, vmem_limit_bytes=63 * 2**20
        ),
        name="panel",
    )(maps, front, children)


def shards(front, children, maps):
    return panel(maps, front, children)


def solution(mesh):
    in_specs = (P("row", "col"), P("row", "col"), P())
    out_specs = P("row", "col")
    return jax.shard_map(shards, mesh=mesh, in_specs=in_specs, out_specs=out_specs, check_vma=False)
```

```python
import jax
import jax.numpy as jnp
from jax import lax
from jax.experimental import pallas as pl
from jax.experimental.pallas import tpu as pltpu
from jax.sharding import PartitionSpec as P

HIGHEST = lax.Precision.HIGHEST
MESH = pl.DeviceIdType.MESH
F32 = jnp.float32
BF16 = jnp.bfloat16
NN = (((1,), (0,)), ((), ()))
NT = (((1,), (1,)), ((), ()))
VMEM = pl.BlockSpec(memory_space=pltpu.VMEM)
SMEM = pl.BlockSpec(memory_space=pltpu.SMEM)
VMEM_LIMIT = 60 * 2**20


def run_of(maps_ref, member, block):
    run = jnp.int32(0)
    found = jnp.int32(0)
    for j in range(8):
        start = maps_ref[member, 8 * j]
        hit = ((block >= start) & (block < start + 8)).astype(jnp.int32)
        run = jnp.maximum(run, hit * j)
        found = jnp.maximum(found, hit)
    return run, found


class Mover:
    def __init__(self, send_sem):
        self.send_sem = send_sem
        self.sent = []

    def send(self, guard, ref, recv_sem, target, to=None):
        number = len(self.sent)

        def copy():
            return pltpu.make_async_remote_copy(
                src_ref=ref(),
                dst_ref=(to or ref)(),
                send_sem=self.send_sem.at[number],
                recv_sem=recv_sem(),
                device_id=target,
                device_id_type=MESH,
            )

        self.sent.append((guard, copy))
        pl.when(guard())(lambda: copy().start())

    def finish(self):
        for guard, copy in self.sent:
            pl.when(guard())(lambda copy=copy: copy().wait_send())


def await_copy(guard, dst, recv_sem, peer):
    @pl.when(guard)
    def _():
        pltpu.make_async_remote_copy(
            src_ref=dst,
            dst_ref=dst,
            send_sem=recv_sem,
            recv_sem=recv_sem,
            device_id=peer,
            device_id_type=MESH,
        ).wait_recv()


class Gather:
    def __init__(self, mover, view, half, sem, needed):
        self.mover, self.view, self.half, self.sem, self.needed = mover, view, half, sem, needed

    def whole(self, slot, target):
        self.mover.send(
            lambda: self.needed(slot), lambda: self.view(slot), lambda: self.sem.at[0, slot], target
        )

    def part(self, slot, i, target):
        self.mover.send(
            lambda: self.needed(slot),
            lambda: self.half(slot, i),
            lambda: self.sem.at[i, slot],
            target,
        )

    def got(self, slot, peer):
        await_copy(self.needed(slot), self.view(slot), self.sem.at[0, slot], peer)

    def got_part(self, slot, i, peer):
        await_copy(self.needed(slot), self.half(slot, i), self.sem.at[i, slot], peer)

    def forward(self):
        for slot in self.near[-1]:
            self.got(slot, self.left)
            self.part(slot, 0, self.right)
        for slot in self.near[1]:
            self.got(slot, self.right)
            self.part(slot, 1, self.left)


class RowGather(Gather):
    def __init__(self, mover, view, half, sem, needed, places):
        super().__init__(mover, view, half, sem, needed)
        (h, x, k), (self.z_peer, self.right, self.left, self.mate) = places
        at = lambda h, x, k: h * 8 + lax.rem(x + 4, 4) * 2 + k
        self.own, self.other = at(h, x, k), at(1 - h, x, k)
        self.near = {d: [at(h, x + d, k), at(1 - h, x + d, k)] for d in (-1, 1, 2)}
        self.theirs = [at(g, jnp.int32(p), 1 - k) for g in range(2) for p in range(4)]

    def to_pair(self):
        for target in (self.z_peer, self.right, self.left, self.mate):
            self.whole(self.own, target)

    def to_ring(self):
        self.got(self.other, self.z_peer)
        for target in (self.right, self.left, self.mate):
            self.whole(self.other, target)

    def forward(self):
        super().forward()
        for slot in self.near[-1] + self.near[1]:
            self.whole(slot, self.mate)

    def to_mate(self):
        for slot in self.near[2]:
            self.got_part(slot, 0, self.left)
            self.got_part(slot, 1, self.right)
            self.whole(slot, self.mate)

    def finish(self):
        for slot in self.theirs:
            self.got(slot, self.mate)


class ColGather(Gather):
    def __init__(self, mover, view, half, sem, places):
        super().__init__(mover, view, half, sem, lambda e: e < 12)
        (y, s), (self.z_peer, self.right, self.left) = places
        at = lambda y, s: lax.rem(y + 4, 4) * 2 + s
        self.own = [at(y, s), at(y, s) + 8]
        self.other = [at(y, 1 - s), at(y, 1 - s) + 8]
        self.near = {
            d: [at(y + d, t) + e for t in range(2) for e in (0, 8)] for d in (-1, 1, 2)
        }

    def to_pair(self):
        for slot in self.own:
            for target in (self.z_peer, self.right, self.left):
                self.whole(slot, target)

    def to_ring(self):
        for slot in self.other:
            self.got(slot, self.z_peer)
            for target in (self.right, self.left):
                self.whole(slot, target)

    def finish(self):
        for slot in self.near[2]:
            self.got_part(slot, 0, self.left)
            self.got_part(slot, 1, self.right)


def factor128(a):
    full = (8, 128)
    rows = lax.broadcasted_iota(jnp.int32, full, 0)
    lanes = lax.broadcasted_iota(jnp.int32, full, 1)
    strips = [a[8 * g : 8 * g + 8, :] for g in range(16)]
    units = [jnp.where(lanes == rows + 8 * g, 1.0, 0.0).astype(F32) for g in range(16)]
    uppers, inverses = [], []
    for g in range(16):
        s, t = strips[g], units[g]
        cols = [jnp.broadcast_to(s[:, 8 * g + m : 8 * g + m + 1], full) for m in range(8)]
        e = [[jnp.broadcast_to(cols[m][i : i + 1, :], full) for m in range(i + 1)] for i in range(8)]
        z = [jnp.broadcast_to(s[i : i + 1, :], full) for i in range(8)]
        y = [jnp.broadcast_to(t[i : i + 1, :], full) for i in range(8)]
        l = [[None] * 8 for _ in range(8)]
        r = []
        for k in range(8):
            r.append(pl.reciprocal(e[k][k], approx=True))
            for i in range(k + 1, 8):
                l[i][k] = e[i][k] * r[k]
            for j in range(k + 1, 8):
                for i in range(j, 8):
                    e[i][j] = e[i][j] - l[i][k] * e[j][k]
            for i in range(k + 1, 8):
                z[i] = z[i] - l[i][k] * z[k]
                y[i] = y[i] - l[i][k] * y[k]
        u = jnp.zeros(full, F32)
        w = jnp.zeros(full, F32)
        for i in range(8):
            q = lax.rsqrt(e[i][i])
            u = jnp.where(rows == i, z[i] * q, u)
            w = jnp.where(rows == i, y[i] * q, w)
        uppers.append(jnp.where(lanes >= rows + 8 * g, u, 0.0))
        inverses.append(w)
        top = g // 4 * 4 + 4
        if g + 1 < top:
            v, x = [None] * 8, [None] * 8
            for i in reversed(range(8)):
                v[i], x[i] = z[i] * r[i], y[i] * r[i]
                for m in range(i + 1, 8):
                    v[i] = v[i] - l[m][i] * v[m]
                    x[i] = x[i] - l[m][i] * x[m]
            for h in range(g + 1, top):
                c = [
                    jnp.broadcast_to(strips[h][:, 8 * g + m : 8 * g + m + 1], full)
                    for m in range(8)
                ]
                p = [c[m] * v[m] for m in range(8)]
                o = [c[m] * x[m] for m in range(8)]
                while len(p) > 1:
                    p = [p[2 * i] + p[2 * i + 1] for i in range(len(p) // 2)]
                    o = [o[2 * i] + o[2 * i + 1] for i in range(len(o) // 2)]
                strips[h] = strips[h] - p[0]
                units[h] = units[h] - o[0]
        elif top < 16:
            u = jnp.concatenate(uppers[top - 4 : top], 0)
            w = jnp.concatenate(inverses[top - 4 : top], 0)
            product = lax.dot_general(
                u,
                jnp.concatenate([u, w], 1),
                (((0,), (0,)), ((), ())),
                precision=HIGHEST,
                preferred_element_type=F32,
            )
            for h in range(top, 16):
                strips[h] = strips[h] - product[8 * h : 8 * h + 8, :128]
                units[h] = units[h] - product[8 * h : 8 * h + 8, 128:]
    return jnp.concatenate(uppers, 0), jnp.concatenate(inverses, 0)


def dot(a, b, dims=NN):
    return lax.dot_general(a, b, dims, precision=HIGHEST, preferred_element_type=jnp.float32)


def inverse_at(dinv, J):
    a, b, c, d = (dinv[J * 4 + i] for i in range(4))
    return jnp.concatenate([jnp.concatenate([a, b], 1), jnp.concatenate([c, d], 1)], 0)


def split(v):
    hi = v.astype(BF16)
    return hi, (v - hi.astype(F32)).astype(BF16)


def pair(v, left):
    hi, lo = split(v)
    return jnp.concatenate([hi, hi, lo] if left else [hi, lo, hi], 1)


def dot_pairs(a, b):
    return lax.dot_general(a, b, NT, preferred_element_type=F32)


def chol_loop(pv, dinv, beside, after_first, nsteps=6):
    @pl.loop(0, nsteps)
    def _(J):
        ca = pl.multiple_of(J * 256, 256)
        cb = pl.multiple_of(J * 256 + 128, 128)
        for step, action in beside.items():
            if step % 2 == 0:
                pl.when(J == step // 2)(action)
        ua, ia = factor128(pv[pl.ds(ca, 128), pl.ds(ca, 128)])
        la = ua.T
        pv[pl.ds(ca, 128), pl.ds(ca, 128)] = la
        wb = dot(pv[pl.ds(cb, 128), pl.ds(ca, 128)], ia, NT)
        pv[pl.ds(cb, 128), pl.ds(ca, 128)] = wb
        for step, action in beside.items():
            if step % 2 == 1:
                pl.when(J == step // 2)(action)
        ub, ib = factor128(pv[pl.ds(cb, 128), pl.ds(cb, 128)] - dot(wb, wb, NT))
        pv[pl.ds(cb, 128), pl.ds(cb, 128)] = ub.T
        off = -dot(ib, dot(wb, ia))
        pl.when(J == 0)(after_first)
        dinv[J * 4] = ia
        dinv[J * 4 + 1] = jnp.zeros((128, 128), F32)
        dinv[J * 4 + 2] = off
        dinv[J * 4 + 3] = ib
        inv = pair(inverse_at(dinv, J), False)
        @pl.loop(J + 1, nsteps)
        def _(R):
            ro = pl.multiple_of(R * 256, 256)
            block = pair(pv[pl.ds(ro, 256), pl.ds(ca, 256)], True)
            pv[pl.ds(ro, 256), pl.ds(ca, 256)] = dot_pairs(block, inv)
        @pl.loop(J + 1, nsteps)
        def _(I):
            io = pl.multiple_of(I * 256, 256)
            wi = pair(pv[pl.ds(io, 256), pl.ds(ca, 256)], False)
            @pl.loop(I, nsteps)
            def _(R):
                ro = pl.multiple_of(R * 256, 256)
                block = pair(pv[pl.ds(ro, 256), pl.ds(ca, 256)], True)
                pv[pl.ds(ro, 256), pl.ds(io, 256)] -= dot_pairs(block, wi)


def dot3(ah, al, bh, bl):
    a = jnp.concatenate([ah, ah, al], 1)
    b = jnp.concatenate([bh, bl, bh], 0)
    return lax.dot_general(a, b, NN, preferred_element_type=F32)


def solve_x(g1, l_ref, d_ref, xh, xl):
    for i in range(6):
        dh, dl = split(inverse_at(d_ref, i))
        lh, ll = split(l_ref[256 * i : 256 * i + 256, : 256 * i]) if i else (None, None)

        @pl.loop(0, 2)
        def _(n):
            cols = pl.ds(pl.multiple_of(n * 768, 256), 768)
            rhs = g1[2 * i : 2 * i + 2, :, cols].reshape(256, 768)
            if i:
                rhs = rhs - dot3(lh, ll, xh[: 256 * i, cols], xl[: 256 * i, cols])
            hi, lo = split(dot3(dh, dl, *split(rhs)))
            xh[256 * i : 256 * i + 256, cols] = hi
            xl[256 * i : 256 * i + 256, cols] = lo


def solve_y(g2, l_ref, d_ref, yh, yl):
    for i in range(6):
        dh, dl = split(inverse_at(d_ref, i))
        lh, ll = split(l_ref[256 * i : 256 * i + 256, : 256 * i]) if i else (None, None)

        @pl.loop(0, 3)
        def _(n):
            cols = pl.ds(pl.multiple_of(n * 256, 256), 256)
            rhs = g2[2 * i : 2 * i + 2, :, cols].reshape(256, 256)
            if i:
                rhs = rhs - dot3(lh, ll, *split(g2[: 2 * i, :, cols].reshape(256 * i, 256)))
            g2[2 * i : 2 * i + 2, :, cols] = dot3(dh, dl, *split(rhs)).reshape(2, 128, 256)

    for l in range(6):
        rows = slice(128 * l, 128 * l + 128)
        hi, lo = split(g2[:, :, rows].reshape(1536, 128).T)
        yh[rows, :] = hi
        yl[rows, :] = lo


def update_steps(l_ref, xh, xl, yh, yl):
    @pl.loop(0, 6)
    def _(t):
        rows = pl.ds(pl.multiple_of(t // 2 * 256, 256), 256)
        cols = pl.ds(pl.multiple_of(lax.rem(t, 2) * 768, 256), 768)
        l_ref[rows, cols] = dot3(yh[rows, :], yl[rows, :], xh[:, cols], xl[:, cols])


def place_steps(row, col, out_ref, yh, yl):
    @pl.when(row < 12)
    def _():
        out_ref[0:128, :] = jnp.zeros((128, 1536), F32)

    def place(block, m):
        lanes = pl.ds(pl.multiple_of(block * 128, 128), 128)
        values = yh[:, lanes].astype(F32) + yl[:, lanes].astype(F32)
        i = lax.broadcasted_iota(jnp.int32, values.shape, 0)
        j = lax.broadcasted_iota(jnp.int32, values.shape, 1)
        matrix_row = (i // 128 * 16 + row) * 128 + lax.rem(i, 128)
        out_ref[:, 128 * m : 128 * m + 128] = jnp.where(
            matrix_row >= block * 128 + j, values, 0.0
        )

    place(col, 0)

    @pl.when(col < 4)
    def _():
        place(col + 8, 1)


def panel_kernel(
    maps_ref,
    front_ref,
    child_ref,
    out_ref,
    mid,
    arrived,
    g1,
    g2,
    pv,
    dinv,
    xh,
    xl,
    yh,
    yl,
    load_sem,
    mid_send,
    mid_sem,
    block_send,
    first_sem,
    block_sem,
    early_sem,
    later_sem,
    send_sem,
    head_sem,
    turn_sem,
    g1_sem,
    g2_sem,
    pv_sem,
):
    first = dinv.at[pl.ds(0, 16)]
    row, col = lax.axis_index("row"), lax.axis_index("col")
    h, x, k = row // 8, lax.rem(row, 8) // 2, lax.rem(row, 2)
    y, s = col // 2, lax.rem(col, 2)
    z = s * 2 + h
    at_x = lambda p: h * 8 + lax.rem(p + 4, 4) * 2 + k
    at_y = lambda p: lax.rem(p + 4, 4) * 2 + s
    row_peers = [
        ((1 - h) * 8 + x * 2 + k, col),
        (at_x(x + 1), col),
        (at_x(x - 1), col),
        (h * 8 + x * 2 + 1 - k, col),
    ]
    col_peers = [(row, y * 2 + 1 - s), (row, at_y(y + 1)), (row, at_y(y - 1))]

    def block_at(i):
        return pl.ds(pl.multiple_of(i * 128, 128), 128)

    def peer(o):
        to_x = lax.rem(x + lax.rem(o, 4), 4)
        to_y = lax.rem(y + lax.rem(o // 4, 4), 4)
        to_z = lax.rem(z + lax.rem(o // 16, 4), 4)
        to_k = lax.rem(k + o // 64, 2)
        return lax.rem(to_z, 2) * 8 + to_x * 2 + to_k, to_y * 2 + to_z // 2

    barrier = pltpu.get_barrier_semaphore()

    @pl.loop(1, 128)
    def _(o):
        pl.semaphore_signal(barrier, inc=1, device_id=peer(o), device_id_type=MESH)

    for i in range(8):
        for j in range(8):
            pltpu.make_async_copy(
                child_ref.at[pl.ds(128 * i, 128), pl.ds(128 * j, 128)],
                arrived.at[i * 8 + j],
                load_sem,
            ).start()
    loaded = arrived.at[pl.ds(0, 64)]
    pltpu.make_async_copy(loaded, loaded, load_sem).wait()
    run = lax.rem(row, 8)
    row_start = lax.rem(maps_ref[h, 8 * run], 8)
    col_start = lax.rem(maps_ref[h, 8 * col], 8)

    @pl.loop(0, 8)
    def _(r):
        i = lax.rem(r - row_start + 8, 8)

        @pl.loop(0, 8)
        def _(c):
            j = lax.rem(c - col_start + 8, 8)
            p = r * 8 + c
            out_ref[block_at(p // 12), block_at(lax.rem(p, 12))] = arrived[i * 8 + j]

    def staged(p):
        return out_ref.at[block_at(p // 12), block_at(lax.rem(p, 12))]

    for j in range(2):
        mid[(run * 4 + y) * 2 + j] = staged(run * 8 + y * 2 + j)[...]

    pl.semaphore_wait(barrier, 127)

    @pl.loop(1, 32)
    def _(i):
        o = lax.rem(i * 13, 32)
        to_row, to_col = peer(lax.rem(o, 16) + o // 16 * 64)
        for j in range(2):
            pltpu.make_async_remote_copy(
                src_ref=staged(lax.rem(to_row, 8) * 8 + to_col // 2 * 2 + j),
                dst_ref=mid.at[(run * 4 + y) * 2 + j],
                send_sem=mid_send,
                recv_sem=mid_sem,
                device_id=(to_row, to_col),
                device_id_type=MESH,
            ).start()

    def await_blocks(ref, sem, send=False):
        copy = pltpu.make_async_remote_copy(
            src_ref=ref,
            dst_ref=ref,
            send_sem=sem,
            recv_sem=sem,
            device_id=row_peers[0],
            device_id_type=MESH,
        )
        copy.wait_send() if send else copy.wait_recv()

    await_blocks(mid.at[pl.ds(0, 62)], mid_sem)
    await_blocks(mid.at[pl.ds(0, 62)], mid_send, True)

    def along_z(d):
        to_z = lax.rem(z + d, 4)
        return lax.rem(to_z, 2), to_z // 2

    def stage(l, d):
        to_h, to_s = along_z(d)
        held, found = run_of(maps_ref, h, l * 16 + to_h * 8 + run)
        for j in range(4):
            block = mid[(held * 4 + j) * 2 + to_s] * found.astype(F32)
            if d:
                staged(((d - 1) * 6 + l) * 4 + j)[...] = block
            elif isinstance(l, int):
                first[z * 4 + j] = block
            else:
                arrived[(z * 5 + l - 1) * 4 + j] = block

    def send_staged(l, d, dst, sem):
        to_h, to_s = along_z(d)
        for j in range(4):
            pltpu.make_async_remote_copy(
                src_ref=staged(((d - 1) * 6 + l) * 4 + j),
                dst_ref=dst(j),
                send_sem=block_send,
                recv_sem=sem,
                device_id=(to_h * 8 + run, y * 2 + to_s),
                device_id_type=MESH,
            ).start()

    for d in (1, 3, 2):
        stage(0, d)
        send_staged(0, d, lambda j: first.at[z * 4 + j], first_sem)
    stage(0, 0)

    @pl.loop(1, 6)
    def _(l):
        for d in range(4):
            stage(l, d)

    def send_rest():
        @pl.loop(1, 6)
        def _(l):
            for d in (1, 3, 2):
                send_staged(l, d, lambda j: arrived.at[(z * 5 + l - 1) * 4 + j], block_sem)

    await_blocks(first.at[pl.ds(0, 12)], first_sem)

    early, later, mover = Mover(early_sem), Mover(later_sem), Mover(send_sem)

    own = jnp.minimum(row, 12)

    def placed(blocks, count, m, total):
        for member in range(2):
            other, found = run_of(maps_ref, member, m * 8 + col)
            update = blocks[(lax.rem(other, 2) * 2 + member) * count + other // 2]
            total = total + update * found.astype(F32)
        return total

    @pl.loop(0, 12)
    def _(m):
        g1[own, :, block_at(m)] = placed(first, 4, m, front_ref[0:128, block_at(m)])

    def pivot_block(b):
        return pv.at[block_at(row), block_at(b)]

    for j in range(2):
        block = col + 8 * j

        @pl.when((row < 12) & (block <= row))
        def _():
            pv[block_at(row), block_at(block)] = g1[row, :, 128 * j : 128 * j + 128]

        for o in range(1, 8):
            early.send(
                lambda b=block: (row < 12) & (b <= row),
                lambda b=block: pivot_block(b),
                lambda b=block: head_sem.at[b],
                (row, lax.rem(col + o, 8)),
            )

    own_turn = (row < 12) & (run == col)

    def turn():
        for j in range(2):
            target = (col + 8 * j, run)
            for l in range(6):
                mover.send(
                    lambda t=target: (row < 12) & ((t[0] != row) | (t[1] != col)),
                    lambda j=j, l=l: g1.at[row, :, pl.ds(128 * (2 * l + j), 128)],
                    lambda: turn_sem.at[row],
                    target,
                    lambda l=l: g2.at[row, :, pl.ds(128 * l, 128)],
                )

        @pl.when(own_turn)
        def _():
            for l in range(6):
                g2[row, :, 128 * l : 128 * l + 128] = g1[row, :, block_at(2 * l + h)]

    def turned():
        for slot in (col, col + 8):
            held = lax.rem(slot, 12)
            await_copy(
                (slot < 12) & jnp.logical_not(own_turn & (row == slot)),
                g2.at[held],
                turn_sem.at[slot],
                (held, lax.rem(row, 8)),
            )

    row_places = ((h, x, k), row_peers)
    wide = pl.ds(128, 1408)
    rows1 = RowGather(
        mover,
        lambda q: g1.at[q, :, wide],
        lambda q, i: g1.at[q, pl.ds(64 * i, 64), wide],
        g1_sem,
        lambda q: q < 12,
        row_places,
    )
    cols2 = ColGather(
        mover,
        lambda e: g2.at[e],
        lambda e, i: g2.at[e, pl.ds(64 * i, 64), :],
        g2_sem,
        ((y, s), col_peers),
    )
    pivots = [
        RowGather(
            later if t else early,
            lambda q, t=t: pv.at[block_at(q), pl.ds(512 * t, 512)],
            lambda q, i, t=t: pv.at[
                pl.ds(pl.multiple_of(q * 128 + 64 * i, 64), 64), pl.ds(512 * t, 512)
            ],
            pv_sem.at[t],
            lambda q, t=t: (q < 12) & (q >= 4 * t),
            row_places,
        )
        for t in range(3)
    ]
    for b in range(12):
        await_copy(
            (row < 12) & (b <= row) & (col != b % 8), pivot_block(b), head_sem.at[b], (row, b % 8)
        )
    for p in pivots:
        p.to_pair()
    for p in pivots:
        p.to_ring()
    pivots[0].forward()
    pivots[0].to_mate()
    for p in pivots[1:]:
        p.forward()
    turn()
    rows1.to_pair()
    pivots[0].finish()
    early.finish()

    def step1():
        for p in pivots[1:]:
            p.to_mate()

    def after_first():
        for p in pivots[1:]:
            p.finish()
        later.finish()

    def step2():
        rows1.to_ring()
        turned()
        cols2.to_pair()

    def step9():
        cols2.forward()
        rows1.to_mate()

    chol_loop(
        pv,
        dinv,
        {1: step1, 2: step2, 3: send_rest, 5: cols2.to_ring, 6: rows1.forward, 9: step9},
        after_first,
    )
    rows1.finish()
    solve_x(g1, pv, dinv, xh, xl)
    cols2.finish()
    mover.finish()
    solve_y(g2, pv, dinv, yh, yl)
    update_steps(pv, xh, xl, yh, yl)

    await_blocks(arrived.at[pl.ds(0, 60)], block_sem)
    await_blocks(arrived.at[pl.ds(0, 72)], block_send, True)

    @pl.loop(0, 12)
    def _(m):
        out_ref[0:128, block_at(m)] = g1[own, :, block_at(m)] - pv[0:128, block_at(m)]

    @pl.loop(1, 6)
    def _(l):
        @pl.loop(0, 12)
        def _(m):
            total = front_ref[block_at(l), block_at(m)] - pv[block_at(l), block_at(m)]
            for member in range(2):
                other, found = run_of(maps_ref, member, m * 8 + col)
                held = (lax.rem(other, 2) * 2 + member) * 5 + l - 1
                total = total + arrived[held * 4 + other // 2] * found.astype(F32)
            out_ref[block_at(l), block_at(m)] = total

    place_steps(row, col, out_ref, yh, yl)


def panel(maps, front, children):
    return pl.pallas_call(
        panel_kernel,
        out_shape=jax.ShapeDtypeStruct(front.shape, F32),
        in_specs=[SMEM, VMEM, pl.BlockSpec(memory_space=pl.ANY)],
        out_specs=VMEM,
        scratch_shapes=[
            pltpu.VMEM((64, 128, 128), F32),
            pltpu.VMEM((80, 128, 128), F32),
            pltpu.VMEM((13, 128, 1536), F32),
            pltpu.VMEM((12, 128, 768), F32),
            pltpu.VMEM((1536, 1536), F32),
            pltpu.VMEM((24, 128, 128), F32),
            pltpu.VMEM((1536, 1536), BF16),
            pltpu.VMEM((1536, 1536), BF16),
            pltpu.VMEM((768, 1536), BF16),
            pltpu.VMEM((768, 1536), BF16),
            pltpu.SemaphoreType.DMA,
            pltpu.SemaphoreType.DMA,
            pltpu.SemaphoreType.DMA,
            pltpu.SemaphoreType.DMA,
            pltpu.SemaphoreType.DMA,
            pltpu.SemaphoreType.DMA,
            pltpu.SemaphoreType.DMA((48,)),
            pltpu.SemaphoreType.DMA((48,)),
            pltpu.SemaphoreType.DMA((64,)),
            pltpu.SemaphoreType.DMA((16,)),
            pltpu.SemaphoreType.DMA((16,)),
            pltpu.SemaphoreType.DMA((2, 16)),
            pltpu.SemaphoreType.DMA((2, 16)),
            pltpu.SemaphoreType.DMA((3, 2, 16)),
        ],
        compiler_params=pltpu.CompilerParams(
            collective_id=0, has_side_effects=True, vmem_limit_bytes=63 * 2**20
        ),
        name="panel",
    )(maps, front, children)


def shards(front, children, maps):
    return panel(maps, front, children)


def solution(mesh):
    in_specs = (P("row", "col"), P("row", "col"), P())
    out_specs = P("row", "col")
    return jax.shard_map(shards, mesh=mesh, in_specs=in_specs, out_specs=out_specs, check_vma=False)
```

```python
import jax
import jax.numpy as jnp
from jax import lax
from jax.experimental import pallas as pl
from jax.experimental.pallas import tpu as pltpu
from jax.sharding import PartitionSpec as P

HIGHEST = lax.Precision.HIGHEST
MESH = pl.DeviceIdType.MESH
F32 = jnp.float32
BF16 = jnp.bfloat16
NN = (((1,), (0,)), ((), ()))
NT = (((1,), (1,)), ((), ()))
VMEM = pl.BlockSpec(memory_space=pltpu.VMEM)
SMEM = pl.BlockSpec(memory_space=pltpu.SMEM)
VMEM_LIMIT = 60 * 2**20


def run_of(maps_ref, member, block):
    run = jnp.int32(0)
    found = jnp.int32(0)
    for j in range(8):
        start = maps_ref[member, 8 * j]
        hit = ((block >= start) & (block < start + 8)).astype(jnp.int32)
        run = jnp.maximum(run, hit * j)
        found = jnp.maximum(found, hit)
    return run, found


class Mover:
    def __init__(self, send_sem):
        self.send_sem = send_sem
        self.sent = []

    def send(self, guard, ref, recv_sem, target, to=None):
        number = len(self.sent)

        def copy():
            return pltpu.make_async_remote_copy(
                src_ref=ref(),
                dst_ref=(to or ref)(),
                send_sem=self.send_sem.at[number],
                recv_sem=recv_sem(),
                device_id=target,
                device_id_type=MESH,
            )

        self.sent.append((guard, copy))
        pl.when(guard())(lambda: copy().start())

    def finish(self):
        for guard, copy in self.sent:
            pl.when(guard())(lambda copy=copy: copy().wait_send())


def await_copy(guard, dst, recv_sem, peer):
    @pl.when(guard)
    def _():
        pltpu.make_async_remote_copy(
            src_ref=dst,
            dst_ref=dst,
            send_sem=recv_sem,
            recv_sem=recv_sem,
            device_id=peer,
            device_id_type=MESH,
        ).wait_recv()


class Gather:
    def __init__(self, mover, view, half, sem, needed):
        self.mover, self.view, self.half, self.sem, self.needed = mover, view, half, sem, needed

    def whole(self, slot, target):
        self.mover.send(
            lambda: self.needed(slot), lambda: self.view(slot), lambda: self.sem.at[0, slot], target
        )

    def part(self, slot, i, target):
        self.mover.send(
            lambda: self.needed(slot),
            lambda: self.half(slot, i),
            lambda: self.sem.at[i, slot],
            target,
        )

    def got(self, slot, peer):
        await_copy(self.needed(slot), self.view(slot), self.sem.at[0, slot], peer)

    def got_part(self, slot, i, peer):
        await_copy(self.needed(slot), self.half(slot, i), self.sem.at[i, slot], peer)

    def forward(self):
        for slot in self.near[-1]:
            self.got(slot, self.left)
            self.part(slot, 0, self.right)
        for slot in self.near[1]:
            self.got(slot, self.right)
            self.part(slot, 1, self.left)


class RowGather(Gather):
    def __init__(self, mover, view, half, sem, needed, places):
        super().__init__(mover, view, half, sem, needed)
        (h, x, k), (self.z_peer, self.right, self.left, self.mate) = places
        at = lambda h, x, k: h * 8 + lax.rem(x + 4, 4) * 2 + k
        self.own, self.other = at(h, x, k), at(1 - h, x, k)
        self.near = {d: [at(h, x + d, k), at(1 - h, x + d, k)] for d in (-1, 1, 2)}
        self.theirs = [at(g, jnp.int32(p), 1 - k) for g in range(2) for p in range(4)]

    def to_pair(self):
        for target in (self.z_peer, self.right, self.left, self.mate):
            self.whole(self.own, target)

    def to_ring(self):
        self.got(self.other, self.z_peer)
        for target in (self.right, self.left, self.mate):
            self.whole(self.other, target)

    def forward(self):
        super().forward()
        for slot in self.near[-1] + self.near[1]:
            self.whole(slot, self.mate)

    def to_mate(self):
        for slot in self.near[2]:
            self.got_part(slot, 0, self.left)
            self.got_part(slot, 1, self.right)
            self.whole(slot, self.mate)

    def finish(self):
        for slot in self.theirs:
            self.got(slot, self.mate)


class ColGather(Gather):
    def __init__(self, mover, view, half, sem, places):
        super().__init__(mover, view, half, sem, lambda e: e < 12)
        (y, s), (self.z_peer, self.right, self.left) = places
        at = lambda y, s: lax.rem(y + 4, 4) * 2 + s
        self.own = [at(y, s), at(y, s) + 8]
        self.other = [at(y, 1 - s), at(y, 1 - s) + 8]
        self.near = {
            d: [at(y + d, t) + e for t in range(2) for e in (0, 8)] for d in (-1, 1, 2)
        }

    def to_pair(self):
        for slot in self.own:
            for target in (self.z_peer, self.right, self.left):
                self.whole(slot, target)

    def to_ring(self):
        for slot in self.other:
            self.got(slot, self.z_peer)
            for target in (self.right, self.left):
                self.whole(slot, target)

    def finish(self):
        for slot in self.near[2]:
            self.got_part(slot, 0, self.left)
            self.got_part(slot, 1, self.right)


def factor128(a):
    full = (8, 128)
    rows = lax.broadcasted_iota(jnp.int32, full, 0)
    lanes = lax.broadcasted_iota(jnp.int32, full, 1)
    strips = [a[8 * g : 8 * g + 8, :] for g in range(16)]
    units = [jnp.where(lanes == rows + 8 * g, 1.0, 0.0).astype(F32) for g in range(16)]
    uppers, inverses = [], []
    for g in range(16):
        s, t = strips[g], units[g]
        cols = [jnp.broadcast_to(s[:, 8 * g + m : 8 * g + m + 1], full) for m in range(8)]
        e = [[jnp.broadcast_to(cols[m][i : i + 1, :], full) for m in range(i + 1)] for i in range(8)]
        z = [jnp.broadcast_to(s[i : i + 1, :], full) for i in range(8)]
        y = [jnp.broadcast_to(t[i : i + 1, :], full) for i in range(8)]
        l = [[None] * 8 for _ in range(8)]
        r = []
        for k in range(8):
            r.append(pl.reciprocal(e[k][k], approx=True))
            for i in range(k + 1, 8):
                l[i][k] = e[i][k] * r[k]
            for j in range(k + 1, 8):
                for i in range(j, 8):
                    e[i][j] = e[i][j] - l[i][k] * e[j][k]
            for i in range(k + 1, 8):
                z[i] = z[i] - l[i][k] * z[k]
                y[i] = y[i] - l[i][k] * y[k]
        u = jnp.zeros(full, F32)
        w = jnp.zeros(full, F32)
        for i in range(8):
            q = lax.rsqrt(e[i][i])
            u = jnp.where(rows == i, z[i] * q, u)
            w = jnp.where(rows == i, y[i] * q, w)
        uppers.append(jnp.where(lanes >= rows + 8 * g, u, 0.0))
        inverses.append(w)
        top = g // 4 * 4 + 4
        if g + 1 < top:
            v, x = [None] * 8, [None] * 8
            for i in reversed(range(8)):
                v[i], x[i] = z[i] * r[i], y[i] * r[i]
                for m in range(i + 1, 8):
                    v[i] = v[i] - l[m][i] * v[m]
                    x[i] = x[i] - l[m][i] * x[m]
            for h in range(g + 1, top):
                c = [
                    jnp.broadcast_to(strips[h][:, 8 * g + m : 8 * g + m + 1], full)
                    for m in range(8)
                ]
                p = [c[m] * v[m] for m in range(8)]
                o = [c[m] * x[m] for m in range(8)]
                while len(p) > 1:
                    p = [p[2 * i] + p[2 * i + 1] for i in range(len(p) // 2)]
                    o = [o[2 * i] + o[2 * i + 1] for i in range(len(o) // 2)]
                strips[h] = strips[h] - p[0]
                units[h] = units[h] - o[0]
        elif top < 16:
            u = jnp.concatenate(uppers[top - 4 : top], 0)
            w = jnp.concatenate(inverses[top - 4 : top], 0)
            product = lax.dot_general(
                u,
                jnp.concatenate([u, w], 1),
                (((0,), (0,)), ((), ())),
                precision=HIGHEST,
                preferred_element_type=F32,
            )
            for h in range(top, 16):
                strips[h] = strips[h] - product[8 * h : 8 * h + 8, :128]
                units[h] = units[h] - product[8 * h : 8 * h + 8, 128:]
    return jnp.concatenate(uppers, 0), jnp.concatenate(inverses, 0)


def dot(a, b, dims=NN):
    return lax.dot_general(a, b, dims, precision=HIGHEST, preferred_element_type=jnp.float32)


def inverse_at(dinv, J):
    a, b, c, d = (dinv[J * 4 + i] for i in range(4))
    return jnp.concatenate([jnp.concatenate([a, b], 1), jnp.concatenate([c, d], 1)], 0)


def split(v):
    hi = v.astype(BF16)
    return hi, (v - hi.astype(F32)).astype(BF16)


def pair(v, left):
    hi, lo = split(v)
    return jnp.concatenate([hi, hi, lo] if left else [hi, lo, hi], 1)


def dot_pairs(a, b):
    return lax.dot_general(a, b, NT, preferred_element_type=F32)


def chol_loop(pv, dinv, beside, after_first, nsteps=6):
    @pl.loop(0, nsteps)
    def _(J):
        ca = pl.multiple_of(J * 256, 256)
        cb = pl.multiple_of(J * 256 + 128, 128)
        for step, action in beside.items():
            if step % 2 == 0:
                pl.when(J == step // 2)(action)
        ua, ia = factor128(pv[pl.ds(ca, 128), pl.ds(ca, 128)])
        la = ua.T
        pv[pl.ds(ca, 128), pl.ds(ca, 128)] = la
        wb = dot(pv[pl.ds(cb, 128), pl.ds(ca, 128)], ia, NT)
        pv[pl.ds(cb, 128), pl.ds(ca, 128)] = wb
        for step, action in beside.items():
            if step % 2 == 1:
                pl.when(J == step // 2)(action)
        ub, ib = factor128(pv[pl.ds(cb, 128), pl.ds(cb, 128)] - dot(wb, wb, NT))
        pv[pl.ds(cb, 128), pl.ds(cb, 128)] = ub.T
        off = -dot(ib, dot(wb, ia))
        pl.when(J == 0)(after_first)
        dinv[J * 4] = ia
        dinv[J * 4 + 1] = jnp.zeros((128, 128), F32)
        dinv[J * 4 + 2] = off
        dinv[J * 4 + 3] = ib
        inv = pair(inverse_at(dinv, J), False)
        @pl.loop(J + 1, nsteps)
        def _(R):
            ro = pl.multiple_of(R * 256, 256)
            block = pair(pv[pl.ds(ro, 256), pl.ds(ca, 256)], True)
            pv[pl.ds(ro, 256), pl.ds(ca, 256)] = dot_pairs(block, inv)
        @pl.loop(J + 1, nsteps)
        def _(I):
            io = pl.multiple_of(I * 256, 256)
            wi = pair(pv[pl.ds(io, 256), pl.ds(ca, 256)], False)
            @pl.loop(I, nsteps)
            def _(R):
                ro = pl.multiple_of(R * 256, 256)
                block = pair(pv[pl.ds(ro, 256), pl.ds(ca, 256)], True)
                pv[pl.ds(ro, 256), pl.ds(io, 256)] -= dot_pairs(block, wi)


def dot3(ah, al, bh, bl):
    a = jnp.concatenate([ah, ah, al], 1)
    b = jnp.concatenate([bh, bl, bh], 0)
    return lax.dot_general(a, b, NN, preferred_element_type=F32)


def solve_x(g1, l_ref, d_ref, xh, xl):
    for i in range(6):
        dh, dl = split(inverse_at(d_ref, i))
        lh, ll = split(l_ref[256 * i : 256 * i + 256, : 256 * i]) if i else (None, None)

        @pl.loop(0, 2)
        def _(n):
            cols = pl.ds(pl.multiple_of(n * 768, 256), 768)
            rhs = g1[2 * i : 2 * i + 2, :, cols].reshape(256, 768)
            if i:
                rhs = rhs - dot3(lh, ll, xh[: 256 * i, cols], xl[: 256 * i, cols])
            hi, lo = split(dot3(dh, dl, *split(rhs)))
            xh[256 * i : 256 * i + 256, cols] = hi
            xl[256 * i : 256 * i + 256, cols] = lo


def solve_y(g2, l_ref, d_ref, yh, yl):
    for i in range(6):
        dh, dl = split(inverse_at(d_ref, i))
        lh, ll = split(l_ref[256 * i : 256 * i + 256, : 256 * i]) if i else (None, None)

        @pl.loop(0, 3)
        def _(n):
            cols = pl.ds(pl.multiple_of(n * 256, 256), 256)
            rhs = g2[2 * i : 2 * i + 2, :, cols].reshape(256, 256)
            if i:
                rhs = rhs - dot3(lh, ll, *split(g2[: 2 * i, :, cols].reshape(256 * i, 256)))
            g2[2 * i : 2 * i + 2, :, cols] = dot3(dh, dl, *split(rhs)).reshape(2, 128, 256)

    for l in range(6):
        rows = slice(128 * l, 128 * l + 128)
        hi, lo = split(g2[:, :, rows].reshape(1536, 128).T)
        yh[rows, :] = hi
        yl[rows, :] = lo


def update_steps(l_ref, xh, xl, yh, yl):
    @pl.loop(0, 6)
    def _(t):
        rows = pl.ds(pl.multiple_of(t // 2 * 256, 256), 256)
        cols = pl.ds(pl.multiple_of(lax.rem(t, 2) * 768, 256), 768)
        l_ref[rows, cols] = dot3(yh[rows, :], yl[rows, :], xh[:, cols], xl[:, cols])


def place_steps(row, col, out_ref, yh, yl):
    @pl.when(row < 12)
    def _():
        out_ref[0:128, :] = jnp.zeros((128, 1536), F32)

    def place(block, m):
        lanes = pl.ds(pl.multiple_of(block * 128, 128), 128)
        values = yh[:, lanes].astype(F32) + yl[:, lanes].astype(F32)
        i = lax.broadcasted_iota(jnp.int32, values.shape, 0)
        j = lax.broadcasted_iota(jnp.int32, values.shape, 1)
        matrix_row = (i // 128 * 16 + row) * 128 + lax.rem(i, 128)
        out_ref[:, 128 * m : 128 * m + 128] = jnp.where(
            matrix_row >= block * 128 + j, values, 0.0
        )

    place(col, 0)

    @pl.when(col < 4)
    def _():
        place(col + 8, 1)


def panel_kernel(
    maps_ref,
    front_ref,
    child_ref,
    out_ref,
    mid,
    arrived,
    g1,
    g2,
    pv,
    dinv,
    xh,
    xl,
    yh,
    yl,
    load_sem,
    mid_send,
    mid_sem,
    block_send,
    first_sem,
    block_sem,
    early_sem,
    later_sem,
    send_sem,
    head_sem,
    turn_sem,
    g1_sem,
    g2_sem,
    pv_sem,
):
    first = dinv.at[pl.ds(0, 16)]
    row, col = lax.axis_index("row"), lax.axis_index("col")
    h, x, k = row // 8, lax.rem(row, 8) // 2, lax.rem(row, 2)
    y, s = col // 2, lax.rem(col, 2)
    z = s * 2 + h
    at_x = lambda p: h * 8 + lax.rem(p + 4, 4) * 2 + k
    at_y = lambda p: lax.rem(p + 4, 4) * 2 + s
    row_peers = [
        ((1 - h) * 8 + x * 2 + k, col),
        (at_x(x + 1), col),
        (at_x(x - 1), col),
        (h * 8 + x * 2 + 1 - k, col),
    ]
    col_peers = [(row, y * 2 + 1 - s), (row, at_y(y + 1)), (row, at_y(y - 1))]

    def block_at(i):
        return pl.ds(pl.multiple_of(i * 128, 128), 128)

    def peer(o):
        to_x = lax.rem(x + lax.rem(o, 4), 4)
        to_y = lax.rem(y + lax.rem(o // 4, 4), 4)
        to_z = lax.rem(z + lax.rem(o // 16, 4), 4)
        to_k = lax.rem(k + o // 64, 2)
        return lax.rem(to_z, 2) * 8 + to_x * 2 + to_k, to_y * 2 + to_z // 2

    barrier = pltpu.get_barrier_semaphore()

    @pl.loop(1, 128)
    def _(o):
        pl.semaphore_signal(barrier, inc=1, device_id=peer(o), device_id_type=MESH)

    for i in range(8):
        for j in range(8):
            pltpu.make_async_copy(
                child_ref.at[pl.ds(128 * i, 128), pl.ds(128 * j, 128)],
                arrived.at[i * 8 + j],
                load_sem,
            ).start()
    loaded = arrived.at[pl.ds(0, 64)]
    pltpu.make_async_copy(loaded, loaded, load_sem).wait()
    run = lax.rem(row, 8)
    row_start = lax.rem(maps_ref[h, 8 * run], 8)
    col_start = lax.rem(maps_ref[h, 8 * col], 8)

    @pl.loop(0, 8)
    def _(r):
        i = lax.rem(r - row_start + 8, 8)

        @pl.loop(0, 8)
        def _(c):
            j = lax.rem(c - col_start + 8, 8)
            p = r * 8 + c
            out_ref[block_at(p // 12), block_at(lax.rem(p, 12))] = arrived[i * 8 + j]

    def staged(p):
        return out_ref.at[block_at(p // 12), block_at(lax.rem(p, 12))]

    for j in range(2):
        mid[(run * 4 + y) * 2 + j] = staged(run * 8 + y * 2 + j)[...]

    pl.semaphore_wait(barrier, 127)

    @pl.loop(1, 32)
    def _(i):
        o = lax.rem(i * 13, 32)
        to_row, to_col = peer(lax.rem(o, 16) + o // 16 * 64)
        for j in range(2):
            pltpu.make_async_remote_copy(
                src_ref=staged(lax.rem(to_row, 8) * 8 + to_col // 2 * 2 + j),
                dst_ref=mid.at[(run * 4 + y) * 2 + j],
                send_sem=mid_send,
                recv_sem=mid_sem,
                device_id=(to_row, to_col),
                device_id_type=MESH,
            ).start()

    def await_blocks(ref, sem, send=False):
        copy = pltpu.make_async_remote_copy(
            src_ref=ref,
            dst_ref=ref,
            send_sem=sem,
            recv_sem=sem,
            device_id=row_peers[0],
            device_id_type=MESH,
        )
        copy.wait_send() if send else copy.wait_recv()

    await_blocks(mid.at[pl.ds(0, 62)], mid_sem)
    await_blocks(mid.at[pl.ds(0, 62)], mid_send, True)

    def along_z(d):
        to_z = lax.rem(z + d, 4)
        return lax.rem(to_z, 2), to_z // 2

    def stage(l, d):
        to_h, to_s = along_z(d)
        held, found = run_of(maps_ref, h, l * 16 + to_h * 8 + run)
        for j in range(4):
            block = mid[(held * 4 + j) * 2 + to_s] * found.astype(F32)
            if d:
                staged(((d - 1) * 6 + l) * 4 + j)[...] = block
            elif isinstance(l, int):
                first[z * 4 + j] = block
            else:
                arrived[(z * 5 + l - 1) * 4 + j] = block

    def send_staged(l, d, dst, sem):
        to_h, to_s = along_z(d)
        for j in range(4):
            pltpu.make_async_remote_copy(
                src_ref=staged(((d - 1) * 6 + l) * 4 + j),
                dst_ref=dst(j),
                send_sem=block_send,
                recv_sem=sem,
                device_id=(to_h * 8 + run, y * 2 + to_s),
                device_id_type=MESH,
            ).start()

    for d in (1, 3, 2):
        stage(0, d)
        send_staged(0, d, lambda j: first.at[z * 4 + j], first_sem)
    stage(0, 0)

    @pl.loop(1, 6)
    def _(l):
        for d in range(4):
            stage(l, d)

    def send_rest():
        @pl.loop(1, 6)
        def _(l):
            for d in (1, 3, 2):
                send_staged(l, d, lambda j: arrived.at[(z * 5 + l - 1) * 4 + j], block_sem)

    await_blocks(first.at[pl.ds(0, 12)], first_sem)

    early, later, mover = Mover(early_sem), Mover(later_sem), Mover(send_sem)

    own = jnp.minimum(row, 12)

    def placed(blocks, count, m, total):
        for member in range(2):
            other, found = run_of(maps_ref, member, m * 8 + col)
            update = blocks[(lax.rem(other, 2) * 2 + member) * count + other // 2]
            total = total + update * found.astype(F32)
        return total

    @pl.loop(0, 12)
    def _(m):
        g1[own, :, block_at(m)] = placed(first, 4, m, front_ref[0:128, block_at(m)])

    def pivot_block(b):
        return pv.at[block_at(row), block_at(b)]

    for j in range(2):
        block = col + 8 * j

        @pl.when((row < 12) & (block <= row))
        def _():
            pv[block_at(row), block_at(block)] = g1[row, :, 128 * j : 128 * j + 128]

        for o in range(1, 8):
            early.send(
                lambda b=block: (row < 12) & (b <= row),
                lambda b=block: pivot_block(b),
                lambda b=block: head_sem.at[b],
                (row, lax.rem(col + o, 8)),
            )

    own_turn = (row < 12) & (run == col)

    def turn():
        for j in range(2):
            target = (col + 8 * j, run)
            for l in range(6):
                mover.send(
                    lambda t=target: (row < 12) & ((t[0] != row) | (t[1] != col)),
                    lambda j=j, l=l: g1.at[row, :, pl.ds(128 * (2 * l + j), 128)],
                    lambda: turn_sem.at[row],
                    target,
                    lambda l=l: g2.at[row, :, pl.ds(128 * l, 128)],
                )

        @pl.when(own_turn)
        def _():
            for l in range(6):
                g2[row, :, 128 * l : 128 * l + 128] = g1[row, :, block_at(2 * l + h)]

    def turned():
        for slot in (col, col + 8):
            held = lax.rem(slot, 12)
            await_copy(
                (slot < 12) & jnp.logical_not(own_turn & (row == slot)),
                g2.at[held],
                turn_sem.at[slot],
                (held, lax.rem(row, 8)),
            )

    row_places = ((h, x, k), row_peers)
    wide = pl.ds(128, 1408)
    rows1 = RowGather(
        mover,
        lambda q: g1.at[q, :, wide],
        lambda q, i: g1.at[q, pl.ds(64 * i, 64), wide],
        g1_sem,
        lambda q: q < 12,
        row_places,
    )
    cols2 = ColGather(
        mover,
        lambda e: g2.at[e],
        lambda e, i: g2.at[e, pl.ds(64 * i, 64), :],
        g2_sem,
        ((y, s), col_peers),
    )
    pivots = [
        RowGather(
            later if t else early,
            lambda q, t=t: pv.at[block_at(q), pl.ds(512 * t, 512)],
            lambda q, i, t=t: pv.at[
                pl.ds(pl.multiple_of(q * 128 + 64 * i, 64), 64), pl.ds(512 * t, 512)
            ],
            pv_sem.at[t],
            lambda q, t=t: (q < 12) & (q >= 4 * t),
            row_places,
        )
        for t in range(3)
    ]
    for b in range(12):
        await_copy(
            (row < 12) & (b <= row) & (col != b % 8), pivot_block(b), head_sem.at[b], (row, b % 8)
        )
    for p in pivots:
        p.to_pair()
    for p in pivots:
        p.to_ring()
    pivots[0].forward()
    pivots[0].to_mate()
    for p in pivots[1:]:
        p.forward()
    rows1.to_pair()
    turn()
    pivots[0].finish()
    early.finish()

    def step1():
        for p in pivots[1:]:
            p.to_mate()

    def after_first():
        for p in pivots[1:]:
            p.finish()
        later.finish()

    def step4():
        turned()
        cols2.to_pair()
        send_rest()

    chol_loop(
        pv,
        dinv,
        {
            1: step1,
            2: rows1.to_ring,
            4: step4,
            6: rows1.forward,
            7: cols2.to_ring,
            9: rows1.to_mate,
            11: cols2.forward,
        },
        after_first,
    )
    rows1.finish()
    solve_x(g1, pv, dinv, xh, xl)
    cols2.finish()
    mover.finish()
    solve_y(g2, pv, dinv, yh, yl)
    update_steps(pv, xh, xl, yh, yl)

    await_blocks(arrived.at[pl.ds(0, 60)], block_sem)
    await_blocks(arrived.at[pl.ds(0, 72)], block_send, True)

    @pl.loop(0, 12)
    def _(m):
        out_ref[0:128, block_at(m)] = g1[own, :, block_at(m)] - pv[0:128, block_at(m)]

    @pl.loop(1, 6)
    def _(l):
        @pl.loop(0, 12)
        def _(m):
            total = front_ref[block_at(l), block_at(m)] - pv[block_at(l), block_at(m)]
            for member in range(2):
                other, found = run_of(maps_ref, member, m * 8 + col)
                held = (lax.rem(other, 2) * 2 + member) * 5 + l - 1
                total = total + arrived[held * 4 + other // 2] * found.astype(F32)
            out_ref[block_at(l), block_at(m)] = total

    place_steps(row, col, out_ref, yh, yl)


def panel(maps, front, children):
    return pl.pallas_call(
        panel_kernel,
        out_shape=jax.ShapeDtypeStruct(front.shape, F32),
        in_specs=[SMEM, VMEM, pl.BlockSpec(memory_space=pl.ANY)],
        out_specs=VMEM,
        scratch_shapes=[
            pltpu.VMEM((64, 128, 128), F32),
            pltpu.VMEM((80, 128, 128), F32),
            pltpu.VMEM((13, 128, 1536), F32),
            pltpu.VMEM((12, 128, 768), F32),
            pltpu.VMEM((1536, 1536), F32),
            pltpu.VMEM((24, 128, 128), F32),
            pltpu.VMEM((1536, 1536), BF16),
            pltpu.VMEM((1536, 1536), BF16),
            pltpu.VMEM((768, 1536), BF16),
            pltpu.VMEM((768, 1536), BF16),
            pltpu.SemaphoreType.DMA,
            pltpu.SemaphoreType.DMA,
            pltpu.SemaphoreType.DMA,
            pltpu.SemaphoreType.DMA,
            pltpu.SemaphoreType.DMA,
            pltpu.SemaphoreType.DMA,
            pltpu.SemaphoreType.DMA((48,)),
            pltpu.SemaphoreType.DMA((48,)),
            pltpu.SemaphoreType.DMA((64,)),
            pltpu.SemaphoreType.DMA((16,)),
            pltpu.SemaphoreType.DMA((16,)),
            pltpu.SemaphoreType.DMA((2, 16)),
            pltpu.SemaphoreType.DMA((2, 16)),
            pltpu.SemaphoreType.DMA((3, 2, 16)),
        ],
        compiler_params=pltpu.CompilerParams(
            collective_id=0, has_side_effects=True, vmem_limit_bytes=63 * 2**20
        ),
        name="panel",
    )(maps, front, children)


def shards(front, children, maps):
    return panel(maps, front, children)


def solution(mesh):
    in_specs = (P("row", "col"), P("row", "col"), P())
    out_specs = P("row", "col")
    return jax.shard_map(shards, mesh=mesh, in_specs=in_specs, out_specs=out_specs, check_vma=False)
```

```python
import jax
import jax.numpy as jnp
from jax import lax
from jax.experimental import pallas as pl
from jax.experimental.pallas import tpu as pltpu
from jax.sharding import PartitionSpec as P

MESH = pl.DeviceIdType.MESH
F32 = jnp.float32
BF16 = jnp.bfloat16
NN = (((1,), (0,)), ((), ()))
NT = (((1,), (1,)), ((), ()))
VMEM = pl.BlockSpec(memory_space=pltpu.VMEM)
SMEM = pl.BlockSpec(memory_space=pltpu.SMEM)
VMEM_LIMIT = 60 * 2**20


def run_of(maps_ref, member, block):
    run = jnp.int32(0)
    found = jnp.int32(0)
    for j in range(8):
        start = maps_ref[member, 8 * j]
        hit = ((block >= start) & (block < start + 8)).astype(jnp.int32)
        run = jnp.maximum(run, hit * j)
        found = jnp.maximum(found, hit)
    return run, found


class Mover:
    def __init__(self, send_sem):
        self.send_sem = send_sem
        self.sent = []

    def send(self, guard, ref, recv_sem, target, to=None):
        number = len(self.sent)

        def copy():
            return pltpu.make_async_remote_copy(
                src_ref=ref(),
                dst_ref=(to or ref)(),
                send_sem=self.send_sem.at[number],
                recv_sem=recv_sem(),
                device_id=target,
                device_id_type=MESH,
            )

        self.sent.append((guard, copy))
        pl.when(guard())(lambda: copy().start())

    def finish(self):
        for guard, copy in self.sent:
            pl.when(guard())(lambda copy=copy: copy().wait_send())


def await_copy(guard, dst, recv_sem, peer):
    @pl.when(guard)
    def _():
        pltpu.make_async_remote_copy(
            src_ref=dst,
            dst_ref=dst,
            send_sem=recv_sem,
            recv_sem=recv_sem,
            device_id=peer,
            device_id_type=MESH,
        ).wait_recv()


class Gather:
    def __init__(self, mover, view, half, sem, needed):
        self.mover, self.view, self.half, self.sem, self.needed = mover, view, half, sem, needed

    def whole(self, slot, target):
        self.mover.send(
            lambda: self.needed(slot), lambda: self.view(slot), lambda: self.sem.at[0, slot], target
        )

    def part(self, slot, i, target):
        self.mover.send(
            lambda: self.needed(slot),
            lambda: self.half(slot, i),
            lambda: self.sem.at[i, slot],
            target,
        )

    def got(self, slot, peer):
        await_copy(self.needed(slot), self.view(slot), self.sem.at[0, slot], peer)

    def got_part(self, slot, i, peer):
        await_copy(self.needed(slot), self.half(slot, i), self.sem.at[i, slot], peer)

    def forward(self):
        for slot in self.near[-1]:
            self.got(slot, self.left)
            self.part(slot, 0, self.right)
        for slot in self.near[1]:
            self.got(slot, self.right)
            self.part(slot, 1, self.left)


class RowGather(Gather):
    def __init__(self, mover, view, half, sem, needed, places):
        super().__init__(mover, view, half, sem, needed)
        (h, x, k), (self.z_peer, self.right, self.left, self.mate) = places
        at = lambda h, x, k: h * 8 + lax.rem(x + 4, 4) * 2 + k
        self.own, self.other = at(h, x, k), at(1 - h, x, k)
        self.near = {d: [at(h, x + d, k), at(1 - h, x + d, k)] for d in (-1, 1, 2)}
        self.theirs = [at(g, jnp.int32(p), 1 - k) for g in range(2) for p in range(4)]

    def to_pair(self):
        for target in (self.z_peer, self.right, self.left, self.mate):
            self.whole(self.own, target)

    def to_ring(self):
        self.got(self.other, self.z_peer)
        for target in (self.right, self.left, self.mate):
            self.whole(self.other, target)

    def forward(self):
        super().forward()
        for slot in self.near[-1] + self.near[1]:
            self.whole(slot, self.mate)

    def to_mate(self):
        for slot in self.near[2]:
            self.got_part(slot, 0, self.left)
            self.got_part(slot, 1, self.right)
            self.whole(slot, self.mate)

    def finish(self):
        for slot in self.theirs:
            self.got(slot, self.mate)


class ColGather(Gather):
    def __init__(self, mover, view, half, sem, places):
        super().__init__(mover, view, half, sem, lambda e: e < 12)
        (y, s), (self.z_peer, self.right, self.left) = places
        at = lambda y, s: lax.rem(y + 4, 4) * 2 + s
        self.own = [at(y, s), at(y, s) + 8]
        self.other = [at(y, 1 - s), at(y, 1 - s) + 8]
        self.near = {
            d: [at(y + d, t) + e for t in range(2) for e in (0, 8)] for d in (-1, 1, 2)
        }

    def to_pair(self):
        for slot in self.own:
            for target in (self.z_peer, self.right, self.left):
                self.whole(slot, target)

    def to_ring(self):
        for slot in self.other:
            self.got(slot, self.z_peer)
            for target in (self.right, self.left):
                self.whole(slot, target)

    def finish(self):
        for slot in self.near[2]:
            self.got_part(slot, 0, self.left)
            self.got_part(slot, 1, self.right)


def factor128(a):
    full = (8, 128)
    rows = lax.broadcasted_iota(jnp.int32, full, 0)
    lanes = lax.broadcasted_iota(jnp.int32, full, 1)
    strips = [a[8 * g : 8 * g + 8, :] for g in range(16)]
    units = [jnp.where(lanes == rows + 8 * g, 1.0, 0.0).astype(F32) for g in range(16)]
    uppers, inverses = [], []
    for g in range(16):
        s, t = strips[g], units[g]
        cols = [jnp.broadcast_to(s[:, 8 * g + m : 8 * g + m + 1], full) for m in range(8)]
        e = [[jnp.broadcast_to(cols[m][i : i + 1, :], full) for m in range(i + 1)] for i in range(8)]
        z = [jnp.broadcast_to(s[i : i + 1, :], full) for i in range(8)]
        y = [jnp.broadcast_to(t[i : i + 1, :], full) for i in range(8)]
        l = [[None] * 8 for _ in range(8)]
        r = []
        for k in range(8):
            r.append(pl.reciprocal(e[k][k], approx=True))
            for i in range(k + 1, 8):
                l[i][k] = e[i][k] * r[k]
            for j in range(k + 1, 8):
                for i in range(j, 8):
                    e[i][j] = e[i][j] - l[i][k] * e[j][k]
            for i in range(k + 1, 8):
                z[i] = z[i] - l[i][k] * z[k]
                y[i] = y[i] - l[i][k] * y[k]
        u = jnp.zeros(full, F32)
        w = jnp.zeros(full, F32)
        for i in range(8):
            q = lax.rsqrt(e[i][i])
            u = jnp.where(rows == i, z[i] * q, u)
            w = jnp.where(rows == i, y[i] * q, w)
        uppers.append(jnp.where(lanes >= rows + 8 * g, u, 0.0))
        inverses.append(w)
        top = g // 4 * 4 + 4
        if g + 1 < top:
            v, x = [None] * 8, [None] * 8
            for i in reversed(range(8)):
                v[i], x[i] = z[i] * r[i], y[i] * r[i]
                for m in range(i + 1, 8):
                    v[i] = v[i] - l[m][i] * v[m]
                    x[i] = x[i] - l[m][i] * x[m]
            for h in range(g + 1, top):
                c = [
                    jnp.broadcast_to(strips[h][:, 8 * g + m : 8 * g + m + 1], full)
                    for m in range(8)
                ]
                p = [c[m] * v[m] for m in range(8)]
                o = [c[m] * x[m] for m in range(8)]
                while len(p) > 1:
                    p = [p[2 * i] + p[2 * i + 1] for i in range(len(p) // 2)]
                    o = [o[2 * i] + o[2 * i + 1] for i in range(len(o) // 2)]
                strips[h] = strips[h] - p[0]
                units[h] = units[h] - o[0]
        elif top < 16:
            u = jnp.concatenate(uppers[top - 4 : top], 0)
            w = jnp.concatenate(inverses[top - 4 : top], 0)
            uh, ul = split(u)
            bh, bl = split(jnp.concatenate([u, w], 1))
            product = lax.dot_general(
                jnp.concatenate([uh, uh, ul], 0),
                jnp.concatenate([bh, bl, bh], 0),
                (((0,), (0,)), ((), ())),
                preferred_element_type=F32,
            )
            for h in range(top, 16):
                strips[h] = strips[h] - product[8 * h : 8 * h + 8, :128]
                units[h] = units[h] - product[8 * h : 8 * h + 8, 128:]
    return jnp.concatenate(uppers, 0), jnp.concatenate(inverses, 0)


def inverse_at(dinv, J):
    a, b, c, d = (dinv[J * 4 + i] for i in range(4))
    return jnp.concatenate([jnp.concatenate([a, b], 1), jnp.concatenate([c, d], 1)], 0)


def split(v):
    hi = v.astype(BF16)
    return hi, (v - hi.astype(F32)).astype(BF16)


def pair(v, left):
    hi, lo = split(v)
    return jnp.concatenate([hi, hi, lo] if left else [hi, lo, hi], 1)


def dot_pairs(a, b):
    return lax.dot_general(a, b, NT, preferred_element_type=F32)


def chol_loop(pv, dinv, beside, after_first, nsteps=6):
    @pl.loop(0, nsteps)
    def _(J):
        ca = pl.multiple_of(J * 256, 256)
        cb = pl.multiple_of(J * 256 + 128, 128)
        for step, action in beside.items():
            if step % 2 == 0:
                pl.when(J == step // 2)(action)
        ua, ia = factor128(pv[pl.ds(ca, 128), pl.ds(ca, 128)])
        la = ua.T
        pv[pl.ds(ca, 128), pl.ds(ca, 128)] = la
        wb = dot_pairs(pair(pv[pl.ds(cb, 128), pl.ds(ca, 128)], True), pair(ia, False))
        pv[pl.ds(cb, 128), pl.ds(ca, 128)] = wb
        for step, action in beside.items():
            if step % 2 == 1:
                pl.when(J == step // 2)(action)
        ub, ib = factor128(pv[pl.ds(cb, 128), pl.ds(cb, 128)] - dot_pairs(pair(wb, True), pair(wb, False)))
        pv[pl.ds(cb, 128), pl.ds(cb, 128)] = ub.T
        off = -dot3(*split(ib), *split(dot3(*split(wb), *split(ia))))
        pl.when(J == 0)(after_first)
        dinv[J * 4] = ia
        dinv[J * 4 + 1] = jnp.zeros((128, 128), F32)
        dinv[J * 4 + 2] = off
        dinv[J * 4 + 3] = ib
        inv = pair(inverse_at(dinv, J), False)
        @pl.loop(J + 1, nsteps)
        def _(R):
            ro = pl.multiple_of(R * 256, 256)
            block = pair(pv[pl.ds(ro, 256), pl.ds(ca, 256)], True)
            pv[pl.ds(ro, 256), pl.ds(ca, 256)] = dot_pairs(block, inv)
        @pl.loop(J + 1, nsteps)
        def _(I):
            io = pl.multiple_of(I * 256, 256)
            wi = pair(pv[pl.ds(io, 256), pl.ds(ca, 256)], False)
            @pl.loop(I, nsteps)
            def _(R):
                ro = pl.multiple_of(R * 256, 256)
                block = pair(pv[pl.ds(ro, 256), pl.ds(ca, 256)], True)
                pv[pl.ds(ro, 256), pl.ds(io, 256)] -= dot_pairs(block, wi)


def dot3(ah, al, bh, bl):
    a = jnp.concatenate([ah, ah, al], 1)
    b = jnp.concatenate([bh, bl, bh], 0)
    return lax.dot_general(a, b, NN, preferred_element_type=F32)


def solve_x(g1, l_ref, d_ref, xh, xl):
    for i in range(6):
        dh, dl = split(inverse_at(d_ref, i))
        lh, ll = split(l_ref[256 * i : 256 * i + 256, : 256 * i]) if i else (None, None)

        @pl.loop(0, 2)
        def _(n):
            cols = pl.ds(pl.multiple_of(n * 768, 256), 768)
            rhs = g1[2 * i : 2 * i + 2, :, cols].reshape(256, 768)
            if i:
                rhs = rhs - dot3(lh, ll, xh[: 256 * i, cols], xl[: 256 * i, cols])
            hi, lo = split(dot3(dh, dl, *split(rhs)))
            xh[256 * i : 256 * i + 256, cols] = hi
            xl[256 * i : 256 * i + 256, cols] = lo


def solve_y(g2, l_ref, d_ref, yh, yl):
    for i in range(6):
        dh, dl = split(inverse_at(d_ref, i))
        lh, ll = split(l_ref[256 * i : 256 * i + 256, : 256 * i]) if i else (None, None)

        @pl.loop(0, 3)
        def _(n):
            cols = pl.ds(pl.multiple_of(n * 256, 256), 256)
            rhs = g2[2 * i : 2 * i + 2, :, cols].reshape(256, 256)
            if i:
                rhs = rhs - dot3(lh, ll, *split(g2[: 2 * i, :, cols].reshape(256 * i, 256)))
            g2[2 * i : 2 * i + 2, :, cols] = dot3(dh, dl, *split(rhs)).reshape(2, 128, 256)

    for l in range(6):
        rows = slice(128 * l, 128 * l + 128)
        hi, lo = split(g2[:, :, rows].reshape(1536, 128).T)
        yh[rows, :] = hi
        yl[rows, :] = lo


def update_steps(l_ref, xh, xl, yh, yl):
    @pl.loop(0, 6)
    def _(t):
        rows = pl.ds(pl.multiple_of(t // 2 * 256, 256), 256)
        cols = pl.ds(pl.multiple_of(lax.rem(t, 2) * 768, 256), 768)
        l_ref[rows, cols] = dot3(yh[rows, :], yl[rows, :], xh[:, cols], xl[:, cols])


def place_steps(row, col, out_ref, yh, yl):
    @pl.when(row < 12)
    def _():
        out_ref[0:128, :] = jnp.zeros((128, 1536), F32)

    def place(block, m):
        lanes = pl.ds(pl.multiple_of(block * 128, 128), 128)
        values = yh[:, lanes].astype(F32) + yl[:, lanes].astype(F32)
        i = lax.broadcasted_iota(jnp.int32, values.shape, 0)
        j = lax.broadcasted_iota(jnp.int32, values.shape, 1)
        matrix_row = (i // 128 * 16 + row) * 128 + lax.rem(i, 128)
        out_ref[:, 128 * m : 128 * m + 128] = jnp.where(
            matrix_row >= block * 128 + j, values, 0.0
        )

    place(col, 0)

    @pl.when(col < 4)
    def _():
        place(col + 8, 1)


def panel_kernel(
    maps_ref,
    front_ref,
    child_ref,
    out_ref,
    mid,
    arrived,
    g1,
    g2,
    pv,
    dinv,
    xh,
    xl,
    yh,
    yl,
    load_sem,
    mid_send,
    mid_sem,
    block_send,
    first_sem,
    block_sem,
    early_sem,
    later_sem,
    send_sem,
    head_sem,
    turn_sem,
    g1_sem,
    g2_sem,
    pv_sem,
):
    first = dinv.at[pl.ds(0, 16)]
    row, col = lax.axis_index("row"), lax.axis_index("col")
    h, x, k = row // 8, lax.rem(row, 8) // 2, lax.rem(row, 2)
    y, s = col // 2, lax.rem(col, 2)
    z = s * 2 + h
    at_x = lambda p: h * 8 + lax.rem(p + 4, 4) * 2 + k
    at_y = lambda p: lax.rem(p + 4, 4) * 2 + s
    row_peers = [
        ((1 - h) * 8 + x * 2 + k, col),
        (at_x(x + 1), col),
        (at_x(x - 1), col),
        (h * 8 + x * 2 + 1 - k, col),
    ]
    col_peers = [(row, y * 2 + 1 - s), (row, at_y(y + 1)), (row, at_y(y - 1))]

    def block_at(i):
        return pl.ds(pl.multiple_of(i * 128, 128), 128)

    def peer(o):
        to_x = lax.rem(x + lax.rem(o, 4), 4)
        to_y = lax.rem(y + lax.rem(o // 4, 4), 4)
        to_z = lax.rem(z + lax.rem(o // 16, 4), 4)
        to_k = lax.rem(k + o // 64, 2)
        return lax.rem(to_z, 2) * 8 + to_x * 2 + to_k, to_y * 2 + to_z // 2

    barrier = pltpu.get_barrier_semaphore()

    @pl.loop(1, 128)
    def _(o):
        pl.semaphore_signal(barrier, inc=1, device_id=peer(o), device_id_type=MESH)

    for i in range(8):
        for j in range(8):
            pltpu.make_async_copy(
                child_ref.at[pl.ds(128 * i, 128), pl.ds(128 * j, 128)],
                arrived.at[i * 8 + j],
                load_sem,
            ).start()
    loaded = arrived.at[pl.ds(0, 64)]
    pltpu.make_async_copy(loaded, loaded, load_sem).wait()
    run = lax.rem(row, 8)
    row_start = lax.rem(maps_ref[h, 8 * run], 8)
    col_start = lax.rem(maps_ref[h, 8 * col], 8)

    @pl.loop(0, 8)
    def _(r):
        i = lax.rem(r - row_start + 8, 8)

        @pl.loop(0, 8)
        def _(c):
            j = lax.rem(c - col_start + 8, 8)
            p = r * 8 + c
            out_ref[block_at(p // 12), block_at(lax.rem(p, 12))] = arrived[i * 8 + j]

    def staged(p):
        return out_ref.at[block_at(p // 12), block_at(lax.rem(p, 12))]

    for j in range(2):
        mid[(run * 4 + y) * 2 + j] = staged(run * 8 + y * 2 + j)[...]

    pl.semaphore_wait(barrier, 127)

    @pl.loop(1, 32)
    def _(i):
        o = lax.rem(i * 13, 32)
        to_row, to_col = peer(lax.rem(o, 16) + o // 16 * 64)
        for j in range(2):
            pltpu.make_async_remote_copy(
                src_ref=staged(lax.rem(to_row, 8) * 8 + to_col // 2 * 2 + j),
                dst_ref=mid.at[(run * 4 + y) * 2 + j],
                send_sem=mid_send,
                recv_sem=mid_sem,
                device_id=(to_row, to_col),
                device_id_type=MESH,
            ).start()

    def await_blocks(ref, sem, send=False):
        copy = pltpu.make_async_remote_copy(
            src_ref=ref,
            dst_ref=ref,
            send_sem=sem,
            recv_sem=sem,
            device_id=row_peers[0],
            device_id_type=MESH,
        )
        copy.wait_send() if send else copy.wait_recv()

    await_blocks(mid.at[pl.ds(0, 62)], mid_sem)
    await_blocks(mid.at[pl.ds(0, 62)], mid_send, True)

    def along_z(d):
        to_z = lax.rem(z + d, 4)
        return lax.rem(to_z, 2), to_z // 2

    def stage(l, d):
        to_h, to_s = along_z(d)
        held, found = run_of(maps_ref, h, l * 16 + to_h * 8 + run)
        for j in range(4):
            block = mid[(held * 4 + j) * 2 + to_s] * found.astype(F32)
            if d:
                staged(((d - 1) * 6 + l) * 4 + j)[...] = block
            elif isinstance(l, int):
                first[z * 4 + j] = block
            else:
                arrived[(z * 5 + l - 1) * 4 + j] = block

    def send_staged(l, d, dst, sem):
        to_h, to_s = along_z(d)
        for j in range(4):
            pltpu.make_async_remote_copy(
                src_ref=staged(((d - 1) * 6 + l) * 4 + j),
                dst_ref=dst(j),
                send_sem=block_send,
                recv_sem=sem,
                device_id=(to_h * 8 + run, y * 2 + to_s),
                device_id_type=MESH,
            ).start()

    for d in (1, 3, 2):
        stage(0, d)
        send_staged(0, d, lambda j: first.at[z * 4 + j], first_sem)
    stage(0, 0)

    @pl.loop(1, 6)
    def _(l):
        for d in range(4):
            stage(l, d)

    def send_rest():
        @pl.loop(1, 6)
        def _(l):
            for d in (1, 3, 2):
                send_staged(l, d, lambda j: arrived.at[(z * 5 + l - 1) * 4 + j], block_sem)

    await_blocks(first.at[pl.ds(0, 12)], first_sem)

    early, later, mover = Mover(early_sem), Mover(later_sem), Mover(send_sem)

    own = jnp.minimum(row, 12)

    def placed(blocks, count, m, total):
        for member in range(2):
            other, found = run_of(maps_ref, member, m * 8 + col)
            update = blocks[(lax.rem(other, 2) * 2 + member) * count + other // 2]
            total = total + update * found.astype(F32)
        return total

    @pl.loop(0, 12)
    def _(m):
        g1[own, :, block_at(m)] = placed(first, 4, m, front_ref[0:128, block_at(m)])

    def pivot_block(b):
        return pv.at[block_at(row), block_at(b)]

    for j in range(2):
        block = col + 8 * j

        @pl.when((row < 12) & (block <= row))
        def _():
            pv[block_at(row), block_at(block)] = g1[row, :, 128 * j : 128 * j + 128]

        for o in range(1, 8):
            early.send(
                lambda b=block: (row < 12) & (b <= row),
                lambda b=block: pivot_block(b),
                lambda b=block: head_sem.at[b],
                (row, lax.rem(col + o, 8)),
            )

    own_turn = (row < 12) & (run == col)

    def turn():
        for j in range(2):
            target = (col + 8 * j, run)
            for l in range(6):
                mover.send(
                    lambda t=target: (row < 12) & ((t[0] != row) | (t[1] != col)),
                    lambda j=j, l=l: g1.at[row, :, pl.ds(128 * (2 * l + j), 128)],
                    lambda: turn_sem.at[row],
                    target,
                    lambda l=l: g2.at[row, :, pl.ds(128 * l, 128)],
                )

        @pl.when(own_turn)
        def _():
            for l in range(6):
                g2[row, :, 128 * l : 128 * l + 128] = g1[row, :, block_at(2 * l + h)]

    def turned():
        for slot in (col, col + 8):
            held = lax.rem(slot, 12)
            await_copy(
                (slot < 12) & jnp.logical_not(own_turn & (row == slot)),
                g2.at[held],
                turn_sem.at[slot],
                (held, lax.rem(row, 8)),
            )

    row_places = ((h, x, k), row_peers)
    wide = pl.ds(128, 1408)
    rows1 = RowGather(
        mover,
        lambda q: g1.at[q, :, wide],
        lambda q, i: g1.at[q, pl.ds(64 * i, 64), wide],
        g1_sem,
        lambda q: q < 12,
        row_places,
    )
    cols2 = ColGather(
        mover,
        lambda e: g2.at[e],
        lambda e, i: g2.at[e, pl.ds(64 * i, 64), :],
        g2_sem,
        ((y, s), col_peers),
    )
    pivots = [
        RowGather(
            later if t else early,
            lambda q, t=t: pv.at[block_at(q), pl.ds(512 * t, 512)],
            lambda q, i, t=t: pv.at[
                pl.ds(pl.multiple_of(q * 128 + 64 * i, 64), 64), pl.ds(512 * t, 512)
            ],
            pv_sem.at[t],
            lambda q, t=t: (q < 12) & (q >= 4 * t),
            row_places,
        )
        for t in range(3)
    ]
    for b in range(12):
        await_copy(
            (row < 12) & (b <= row) & (col != b % 8), pivot_block(b), head_sem.at[b], (row, b % 8)
        )
    for p in pivots:
        p.to_pair()
    for p in pivots:
        p.to_ring()
    pivots[0].forward()
    pivots[0].to_mate()
    for p in pivots[1:]:
        p.forward()
    turn()
    rows1.to_pair()
    pivots[0].finish()
    early.finish()

    def step1():
        for p in pivots[1:]:
            p.to_mate()

    def after_first():
        for p in pivots[1:]:
            p.finish()
        later.finish()

    def step2():
        rows1.to_ring()
        turned()
        cols2.to_pair()

    def step9():
        cols2.forward()
        rows1.to_mate()

    chol_loop(
        pv,
        dinv,
        {1: step1, 2: step2, 3: send_rest, 5: cols2.to_ring, 6: rows1.forward, 9: step9},
        after_first,
    )
    rows1.finish()
    solve_x(g1, pv, dinv, xh, xl)
    cols2.finish()
    mover.finish()
    solve_y(g2, pv, dinv, yh, yl)
    update_steps(pv, xh, xl, yh, yl)

    await_blocks(arrived.at[pl.ds(0, 60)], block_sem)
    await_blocks(arrived.at[pl.ds(0, 72)], block_send, True)

    @pl.loop(0, 12)
    def _(m):
        out_ref[0:128, block_at(m)] = g1[own, :, block_at(m)] - pv[0:128, block_at(m)]

    @pl.loop(1, 6)
    def _(l):
        @pl.loop(0, 12)
        def _(m):
            total = front_ref[block_at(l), block_at(m)] - pv[block_at(l), block_at(m)]
            for member in range(2):
                other, found = run_of(maps_ref, member, m * 8 + col)
                held = (lax.rem(other, 2) * 2 + member) * 5 + l - 1
                total = total + arrived[held * 4 + other // 2] * found.astype(F32)
            out_ref[block_at(l), block_at(m)] = total

    place_steps(row, col, out_ref, yh, yl)


def panel(maps, front, children):
    return pl.pallas_call(
        panel_kernel,
        out_shape=jax.ShapeDtypeStruct(front.shape, F32),
        in_specs=[SMEM, VMEM, pl.BlockSpec(memory_space=pl.ANY)],
        out_specs=VMEM,
        scratch_shapes=[
            pltpu.VMEM((64, 128, 128), F32),
            pltpu.VMEM((80, 128, 128), F32),
            pltpu.VMEM((13, 128, 1536), F32),
            pltpu.VMEM((12, 128, 768), F32),
            pltpu.VMEM((1536, 1536), F32),
            pltpu.VMEM((24, 128, 128), F32),
            pltpu.VMEM((1536, 1536), BF16),
            pltpu.VMEM((1536, 1536), BF16),
            pltpu.VMEM((768, 1536), BF16),
            pltpu.VMEM((768, 1536), BF16),
            pltpu.SemaphoreType.DMA,
            pltpu.SemaphoreType.DMA,
            pltpu.SemaphoreType.DMA,
            pltpu.SemaphoreType.DMA,
            pltpu.SemaphoreType.DMA,
            pltpu.SemaphoreType.DMA,
            pltpu.SemaphoreType.DMA((48,)),
            pltpu.SemaphoreType.DMA((48,)),
            pltpu.SemaphoreType.DMA((64,)),
            pltpu.SemaphoreType.DMA((16,)),
            pltpu.SemaphoreType.DMA((16,)),
            pltpu.SemaphoreType.DMA((2, 16)),
            pltpu.SemaphoreType.DMA((2, 16)),
            pltpu.SemaphoreType.DMA((3, 2, 16)),
        ],
        compiler_params=pltpu.CompilerParams(
            collective_id=0, has_side_effects=True, vmem_limit_bytes=63 * 2**20
        ),
        name="panel",
    )(maps, front, children)


def shards(front, children, maps):
    return panel(maps, front, children)


def solution(mesh):
    in_specs = (P("row", "col"), P("row", "col"), P())
    out_specs = P("row", "col")
    return jax.shard_map(shards, mesh=mesh, in_specs=in_specs, out_specs=out_specs, check_vma=False)
```
